32 devices in a mesh: seq: 2 (over core), vocab: 4 (over y, x), section: 4 (over z).
Axes of the slice: x: 2, y: 2, z: 4, core: 2. Of those that a mesh axis runs over, the one named last changes fastest.
Arguments:
- hidden: bfloat16 [4096, 5120], P(('seq', 'vocab', 'section')), parts along dimension 0, may hold values from -8 to 8
- head_weight: bfloat16 [1024, 5120], P(('seq', 'vocab')), parts along dimension 0, may hold values from -1 to 1
- tokens: int32 [4096], P(('seq', 'vocab', 'section')), parts along dimension 0, may hold values from 0 to 511
- rewards: float32 [4096], P(('seq', 'vocab', 'section')), parts along dimension 0, may hold values from -48 to 48
- group_ids: int32 [4096], P(('seq', 'vocab', 'section')), parts along dimension 0, may hold values from 0 to 255, never falling along the last dimension, each value on 1 to 16 neighbouring positions
Outputs:
- logits: bfloat16 [4096, 512], P(('seq', 'vocab', 'section')), parts along dimension 0
- logprob: float32 [4096], P(('seq', 'vocab', 'section')), parts along dimension 0
- entropy: float32 [4096], P(('seq', 'vocab', 'section')), parts along dimension 0
- previous_grad: bfloat16 [4096, 5120], P(('seq', 'vocab', 'section')), parts along dimension 0
The draws below stay inside these ranges and needn't reach their ends.
There are 2 independent parts, one for each index of `seq`. The reference program is written for one: setup_inputs(seed, part) draws one part's arguments, and reference() takes and returns one part's arrays. A program takes and returns all parts, laid end to end along the dimension named above; each array names one. Nothing has to cross between parts.
Inputs may be any that keep to these rules, and one draw needn't show every extreme that they name: `group_ids`: ids never fall along the rows, every id is used, a group holds 1 to 16 rows and some group exactly 16; row counts of groups, and any partial count of one device, are whole numbers of at most 16 that a program may pack several to a word before they are summed.
All inputs are finite; a program needn't handle non-finite values.
Results may differ from the reference program's by a relative error of at most 0.0049.
Values may be sent and summed in bfloat16 or wider, within the bound.
No kernel may reach another device: no remote copies, remote signals or barrier semaphores. Data moves between devices by JAX's collectives and lax.ppermute only.
A program may use at most 64 MiB of HBM per device.

```python
import math
import jax
import jax.numpy as jnp
import numpy as np
from jax import lax

D = 5120
ROWS_DEV = 128
MOST = 16
VOCAB = 512
ROWS_ALL = 2048
GROUPS = 256


def shared_head(key):
    subkeys = jax.random.split(key, 2)
    gaussian = jax.random.normal(subkeys[0], (VOCAB, D), jnp.float32)
    row_scale = jnp.exp(jax.random.uniform(subkeys[1], (VOCAB, 1), jnp.float32, math.log(0.35), math.log(3.5)))
    return jnp.clip(gaussian * row_scale * (2.0 / math.sqrt(D)), -1.0, 1.0)


def draw_head_weight(key, part):
    return shared_head(key).astype(jnp.bfloat16)


def draw_hidden(key, part):
    key = jax.random.fold_in(key, 11)
    subkeys = jax.random.split(key, 2)
    row_scale = jnp.exp(jax.random.uniform(subkeys[0], (ROWS_ALL, 1), jnp.float32, math.log(0.5), math.log(2.0)))
    states = jnp.clip(jax.random.normal(subkeys[1], (ROWS_ALL, D), jnp.float32), -4.0, 4.0) * row_scale
    return jnp.clip(states, -8.0, 8.0).astype(jnp.bfloat16)


def set_ends(entries, stream_key, smallest, high):
    index_at = [jax.random.randint(jax.random.fold_in(stream_key, axis), (), 0, length) for axis, length in enumerate(entries.shape)]
    widest = entries.shape.index(max(entries.shape))
    beside = index_at[:widest] + [(index_at[widest] + 1) % entries.shape[widest]] + index_at[widest + 1:]
    return entries.at[tuple(index_at)].set(smallest).at[tuple(beside)].set(high)


def shard_levels(own_key, shape, pieces, least, top_value):
    gain = 1.0
    for position, parts in pieces:
        steps = jax.random.uniform(jax.random.fold_in(jax.random.fold_in(own_key, 6), position), (parts,), jnp.float32, least / len(pieces), top_value / len(pieces))
        gain = gain * jnp.repeat(jnp.exp(steps), shape[position] // parts).reshape((-1,) + (1,) * (len(shape) - 1 - position))
    return gain


def profile(amount, total, limit, slope):
    weights = [(1 << 20) // math.isqrt(grade ** slope) + 1 for grade in range(2, amount + 1)]
    rest, holding = total - limit - (amount - 1), [1] * (amount - 1)
    while rest > 0:
        movable = [i for i in range(amount - 1) if holding[i] < limit]
        mass, remaining = sum([weights[i] for i in movable]), rest
        for i in movable:
            addition = min(limit - holding[i], max(1, remaining * weights[i] // mass), rest)
            holding[i] = holding[i] + addition
            rest = rest - addition
    return np.array([limit] + holding)


def uneven(key, count, total, bound, slope):
    if count == 2:
        one = jax.random.randint(key, (), max(1, total - bound), min(bound, total - 1) + 1)
        return jnp.stack([one, total - one])
    sizes = jnp.asarray(profile(count, total, bound, slope), jnp.int32)
    couples = (count - 1) // 2
    source_of, taker = sizes[1:1 + 2 * couples:2], sizes[2:2 + 2 * couples:2]
    room = jnp.minimum(source_of - 1, bound - taker)
    passed = jax.random.randint(jax.random.fold_in(key, 1), (couples,), 0, 1 << 20) % (room + 1)
    sizes = sizes.at[1:1 + 2 * couples:2].set(source_of - passed).at[2:2 + 2 * couples:2].set(taker + passed)
    return sizes[jax.random.permutation(jax.random.fold_in(key, 2), count)]


def bell_draw(stream_key, shape, width, bound, cuts=(), held_as=jnp.bfloat16):
    values = width * jax.random.normal(stream_key, shape, jnp.float32)
    if cuts:
        values = values * shard_levels(stream_key, shape, cuts, -0.22, 0.18)
    return jnp.clip(values, -bound, bound).astype(held_as)


def setup_inputs(seed: int = 0, part: int = 0) -> dict:
    arg_keys = jax.random.split(jax.random.key(seed), 6)
    own_keys = jax.random.split(jax.random.fold_in(arg_keys[5], part), 6)
    return {
        "hidden": draw_hidden(jax.random.fold_in(jax.random.fold_in(arg_keys[5], part), 71), part),
        "head_weight": draw_head_weight(jax.random.fold_in(jax.random.fold_in(arg_keys[5], part), 71), part),
        "tokens": set_ends(jax.random.randint(own_keys[2], (ROWS_ALL,), 0, VOCAB), jax.random.fold_in(own_keys[2], 1), 0, VOCAB - 1).astype(jnp.int32),
        "rewards": bell_draw(own_keys[3], (ROWS_ALL,), 8.0, 48.0, ((0, 16),), jnp.float32),
        "group_ids": jnp.searchsorted(jnp.cumsum(uneven(own_keys[4], GROUPS, ROWS_ALL, MOST, 1)), jnp.arange(ROWS_ALL), side="right").astype(jnp.int32),
    }


def reference(hidden, head_weight, tokens, rewards, group_ids):
    scores = jnp.dot(hidden, head_weight.T, preferred_element_type=jnp.float32)
    logits = scores.astype(jnp.bfloat16)
    row_max = jnp.max(scores, axis=1, keepdims=True)
    unnormed = jnp.exp(scores - row_max)
    denominator = jnp.sum(unnormed, axis=1, keepdims=True)
    probabilities = unnormed / denominator
    log_total = (row_max + jnp.log(denominator))[:, 0]
    chosen = jnp.arange(VOCAB, dtype=jnp.int32)[None, :] == tokens[:, None]
    picked = jnp.sum(jnp.where(chosen, scores, jnp.zeros_like(scores)), axis=1)
    logprob = picked - log_total
    entropy = log_total - jnp.sum(probabilities * scores, axis=1)
    member = (group_ids[:, None] == jnp.arange(GROUPS, dtype=jnp.int32)[None, :]).astype(jnp.float32)
    group_sums = jnp.dot(rewards, member, precision=lax.Precision.HIGHEST)
    group_counts = jnp.sum(member, axis=0)
    row_means = jnp.dot(member, group_sums / group_counts, precision=lax.Precision.HIGHEST)
    advantage = rewards - row_means
    dlogits = (advantage[:, None] * (probabilities - chosen.astype(jnp.float32))).astype(jnp.bfloat16)
    gradient = jnp.dot(dlogits, head_weight, preferred_element_type=jnp.float32).astype(jnp.bfloat16)
    paired = gradient.reshape(ROWS_ALL // (2 * ROWS_DEV), 2, ROWS_DEV, D)
    previous_grad = paired[:, ::-1].reshape(ROWS_ALL, D)
    return logits, logprob, entropy, previous_grad
```

```python
import jax
import jax.numpy as jnp
from jax import lax
from jax.sharding import PartitionSpec as P

EDGE = 16


def swapped(value, axis, mask):
    pairs = [(source, source ^ mask) for source in range(lax.axis_size(axis))]
    return lax.ppermute(value, axis, pairs)


def gathered(own, axis):
    count = lax.axis_size(axis)
    cut = own.shape[0] // 2
    pieces = {0: own}
    masks = [1 << bit for bit in range((count - 1).bit_length())]
    for mask in masks:
        pieces[mask] = swapped(own, axis, mask)
    for offset in sorted(range(1, count), key=lambda o: (bin(o).count("1"), o)):
        if offset in pieces:
            continue
        bits = [mask for mask in masks if offset & mask]
        first = swapped(pieces[offset ^ bits[-1]][:cut], axis, bits[-1])
        second = swapped(pieces[offset ^ bits[0]][cut:], axis, bits[0])
        pieces[offset] = jnp.concatenate([first, second], axis=0)
    return [pieces[offset] for offset in range(count)]


def in_order(blocks, axis):
    index = lax.axis_index(axis)
    count = len(blocks)
    bit = 1
    while bit < count:
        odd = (index & bit) != 0
        blocks = [jnp.where(odd, blocks[i ^ bit], blocks[i]) for i in range(count)]
        bit *= 2
    return jnp.concatenate(blocks, axis=1)


def neighbours(rows, axes):
    count = lax.axis_size(axes)
    before = lax.ppermute(rows[:, -EDGE:], axes, [(i, i + 1) for i in range(count - 1)])
    after = lax.ppermute(rows[:, :EDGE], axes, [(i + 1, i) for i in range(count - 1)])
    return jnp.concatenate([before, rows, after], axis=1)


def body(hidden, head_weight, tokens, rewards, group_ids):
    row_count, model_width = hidden.shape
    shard_rows = head_weight.shape[0]
    half = model_width // 2
    odd = lax.axis_index("section") % 2
    shard = lax.axis_index("vocab")

    head_half = lax.dynamic_slice_in_dim(head_weight, odd * half, half, 1)
    own_half = lax.dynamic_slice_in_dim(hidden, odd * half, half, 1)
    other_half = lax.dynamic_slice_in_dim(hidden, (1 - odd) * half, half, 1)

    heads = gathered(head_half, "vocab")
    partner_half = swapped(other_half, "section", 1)

    labelled = jnp.stack([rewards, (group_ids + 1).astype(jnp.float32)])
    wide = neighbours(labelled, ("vocab", "section"))
    member = (labelled[1][:, None] == wide[1][None, :]).astype(jnp.float32)
    sums = jnp.sum(member * wide[0][None, :], axis=1)
    advantage = rewards - sums / jnp.sum(member, axis=1)
    own_facts = jnp.stack([advantage, tokens.astype(jnp.float32)])
    partner_facts = swapped(own_facts, "section", 1)
    facts = jnp.concatenate([own_facts, partner_facts], axis=1)
    all_advantage = facts[0]
    all_tokens = facts[1].astype(jnp.int32)

    both = jnp.concatenate([own_half, partner_half], axis=0)
    scores, chosen = [], []
    for offset, head in enumerate(heads):
        mine = lax.dot_general(
            both, head, (((1,), (1,)), ((), ())), preferred_element_type=jnp.float32
        )
        theirs = swapped(mine, "section", 1)
        theirs = jnp.concatenate([theirs[row_count:], theirs[:row_count]], axis=0)
        scores.append(mine + theirs)
        ids = (shard ^ offset) * shard_rows + jnp.arange(shard_rows, dtype=jnp.int32)
        chosen.append(ids[None, :] == all_tokens[:, None])
    logits = in_order([s[:row_count].astype(jnp.bfloat16) for s in scores], "vocab")
    scores = jnp.concatenate(scores, axis=1)
    chosen = jnp.concatenate(chosen, axis=1)
    heads = jnp.concatenate(heads, axis=0)

    row_max = jnp.max(scores, axis=1, keepdims=True)
    unnormed = jnp.exp(scores - row_max)
    denominator = jnp.sum(unnormed, axis=1, keepdims=True)
    probabilities = unnormed / denominator
    own = slice(0, row_count)
    log_total = (row_max[own] + jnp.log(denominator[own]))[:, 0]
    picked = jnp.sum(jnp.where(chosen[own], scores[own], 0.0), axis=1)
    logprob = picked - log_total
    entropy = log_total - jnp.sum(probabilities[own] * scores[own], axis=1)

    dlogits = (all_advantage[:, None] * (probabilities - chosen.astype(jnp.float32))).astype(
        jnp.bfloat16
    )
    outgoing = jnp.dot(dlogits[:row_count], heads, preferred_element_type=jnp.float32)
    incoming = swapped(outgoing.astype(jnp.bfloat16), "section", 1)
    staying = jnp.dot(dlogits[row_count:], heads, preferred_element_type=jnp.float32)
    staying = staying.astype(jnp.bfloat16)
    previous_grad = jnp.where(
        odd == 1,
        jnp.concatenate([incoming, staying], axis=1),
        jnp.concatenate([staying, incoming], axis=1),
    )
    return (logits, logprob, entropy, previous_grad)


def solution(mesh):
    placed = (
        P(("seq", "vocab", "section"), None),
        P(("seq", "vocab"), None),
        P(("seq", "vocab", "section")),
        P(("seq", "vocab", "section")),
        P(("seq", "vocab", "section")),
    )
    return jax.shard_map(
        body,
        mesh=mesh,
        in_specs=placed,
        out_specs=(
            P(("seq", "vocab", "section"), None),
            P(("seq", "vocab", "section")),
            P(("seq", "vocab", "section")),
            P(("seq", "vocab", "section"), None),
        ),
        check_vma=False,
    )
```

```python
import functools

import jax
import jax.numpy as jnp
from jax import lax
from jax.experimental import pallas as pl
from jax.experimental.pallas import tpu as pltpu
from jax.sharding import PartitionSpec as P

F32, BF16 = jnp.float32, jnp.bfloat16
ANY = pl.BlockSpec(memory_space=pl.ANY)
SMEM = pl.BlockSpec(memory_space=pltpu.SMEM)
VMEM = pl.BlockSpec(memory_space=pltpu.VMEM)
PARAMS = pltpu.CompilerParams(vmem_limit_bytes=48 * 1024 * 1024)


def swapped(value, axis, mask):
    pairs = [(source, source ^ mask) for source in range(lax.axis_size(axis))]
    return lax.ppermute(value, axis, pairs)


def gathered(upper, lower, axis):
    count = lax.axis_size(axis)
    masks = [1 << bit for bit in range((count - 1).bit_length())]
    uppers, lowers = {0: upper}, {0: lower}
    for mask in masks:
        uppers[mask] = swapped(upper, axis, mask)
    for mask in reversed(masks):
        lowers[mask] = swapped(lower, axis, mask)
    for offset in sorted(range(1, count), key=lambda o: (bin(o).count("1"), o)):
        if offset in uppers:
            continue
        bits = [mask for mask in masks if offset & mask]
        uppers[offset] = swapped(uppers[offset ^ bits[-1]], axis, bits[-1])
        lowers[offset] = swapped(lowers[offset ^ bits[0]], axis, bits[0])
    return [(uppers[offset], lowers[offset]) for offset in range(count)]


def take_kernel(which_ref, value_ref, *refs):
    outs, sem = refs[:-1], refs[-1]
    rows, width = outs[0].shape
    start = pl.multiple_of(which_ref[0] * width, 128)
    copies = [
        pltpu.make_async_copy(
            value_ref.at[pl.ds(i * rows, rows), pl.ds(start, width)], out, sem.at[i]
        )
        for i, out in enumerate(outs)
    ]
    for copy in copies:
        copy.start()
    for copy in copies:
        copy.wait()


def take(which, value, pieces):
    rows, width = value.shape[0] // pieces, value.shape[1] // 2
    return pl.pallas_call(
        take_kernel,
        out_shape=[jax.ShapeDtypeStruct((rows, width), value.dtype)] * pieces,
        in_specs=[SMEM, ANY],
        out_specs=[ANY] * pieces,
        scratch_shapes=[pltpu.SemaphoreType.DMA((pieces,))],
        compiler_params=PARAMS,
        cost_estimate=pl.CostEstimate(
            flops=0, bytes_accessed=value.size * value.dtype.itemsize, transcendentals=0
        ),
        name="take_half",
    )(which, value)


def partial_kernel(which_ref, hidden_ref, partner_ref, *refs):
    heads, (mine_ref, theirs_ref) = refs[:-2], refs[-2:]
    width = partner_ref.shape[1]
    start = pl.multiple_of(which_ref[0] * width, 128)
    head = jnp.concatenate([ref[...] for ref in heads], axis=0)
    dims = (((1,), (1,)), ((), ()))
    theirs_ref[...] = lax.dot_general(partner_ref[...], head, dims, preferred_element_type=F32)
    mine_ref[...] = lax.dot_general(
        hidden_ref[:, pl.ds(start, width)], head, dims, preferred_element_type=F32
    )


def partial_scores(which, hidden, partner_half, heads):
    rows, width = partner_half.shape
    columns = sum(head.shape[0] for head in heads)
    out = jax.ShapeDtypeStruct((rows, columns), F32)
    return pl.pallas_call(
        partial_kernel,
        out_shape=[out, out],
        in_specs=[SMEM] + [VMEM] * (2 + len(heads)),
        out_specs=[VMEM, VMEM],
        compiler_params=PARAMS,
        cost_estimate=pl.CostEstimate(
            flops=4 * rows * columns * width,
            bytes_accessed=2 * width * (2 * rows + columns),
            transcendentals=0,
        ),
        name="partial_scores",
    )(which, hidden, partner_half, *heads)


def loss_kernel(parts, shards, place_ref, tokens_ref, own_ref, before_ref, after_ref, *refs):
    mine, theirs = refs[:parts], refs[parts : 2 * parts]
    heads = refs[2 * parts : -5]
    logits_ref, logprob_ref, entropy_ref, dlogits_ref, outgoing_ref = refs[-5:]
    shard = place_ref[1]
    rows, columns = dlogits_ref.shape
    shard_rows = columns // shards

    eye = lax.broadcasted_iota(jnp.int32, (rows, rows), 0) == lax.broadcasted_iota(
        jnp.int32, (rows, rows), 1
    )

    def upright(row):
        return jnp.sum(jnp.where(eye, row, jnp.zeros_like(row)), axis=1, keepdims=True)

    def flat(column):
        return jnp.sum(jnp.where(eye, column, jnp.zeros_like(column)), axis=0, keepdims=True)

    rewards = upright(own_ref[0:1, :])
    groups = upright(own_ref[1:2, :])
    sums, counts = jnp.zeros((rows, 1), F32), jnp.zeros((rows, 1), F32)
    for ref in (before_ref, own_ref, after_ref):
        member = ref[1:2, :] == groups
        sums += jnp.sum(jnp.where(member, ref[0:1, :], 0.0), axis=1, keepdims=True)
        counts += jnp.sum(jnp.where(member, 1.0, 0.0), axis=1, keepdims=True)
    advantage = rewards - sums / counts
    tokens = upright(tokens_ref[...].astype(F32)).astype(jnp.int32)

    scores = jnp.concatenate([a[...] + b[...] for a, b in zip(mine, theirs)], axis=1)
    for offset in range(shards):
        place = pl.multiple_of((shard ^ offset) * shard_rows, 128)
        block = scores[:, offset * shard_rows : (offset + 1) * shard_rows]
        logits_ref[:, pl.ds(place, shard_rows)] = block.astype(logits_ref.dtype)

    lanes = lax.broadcasted_iota(jnp.int32, (rows, columns), 1)
    relative = ((tokens // shard_rows) ^ shard) * shard_rows + tokens % shard_rows
    chosen = lanes == relative
    row_max = jnp.max(scores, axis=1, keepdims=True)
    unnormed = jnp.exp(scores - row_max)
    denominator = jnp.sum(unnormed, axis=1, keepdims=True)
    probabilities = unnormed / denominator
    log_total = row_max + jnp.log(denominator)
    picked = jnp.sum(jnp.where(chosen, scores, 0.0), axis=1, keepdims=True)
    logprob_ref[...] = flat(picked - log_total)
    entropy_ref[...] = flat(log_total - jnp.sum(probabilities * scores, axis=1, keepdims=True))
    dlogits = (advantage * (probabilities - jnp.where(chosen, 1.0, 0.0))).astype(BF16)
    dlogits_ref[...] = dlogits
    head = jnp.concatenate([ref[...] for ref in heads], axis=0)
    outgoing_ref[...] = jnp.dot(dlogits, head, preferred_element_type=F32).astype(BF16)


def loss(place, tokens, own, before, after, mine, theirs, heads, shards):
    rows = own.shape[1]
    columns = sum(head.shape[0] for head in heads)
    width = heads[0].shape[1]
    flat = jax.ShapeDtypeStruct((1, rows), F32)
    wide = jax.ShapeDtypeStruct((rows, columns), BF16)
    return pl.pallas_call(
        functools.partial(loss_kernel, len(mine), shards),
        out_shape=[wide, flat, flat, wide, jax.ShapeDtypeStruct((rows, width), BF16)],
        in_specs=[SMEM] + [VMEM] * (4 + 2 * len(mine) + len(heads)),
        out_specs=[VMEM] * 5,
        compiler_params=PARAMS,
        cost_estimate=pl.CostEstimate(
            flops=2 * rows * columns * width,
            bytes_accessed=2 * width * (rows + columns),
            transcendentals=rows * columns,
        ),
        name="loss_and_outgoing",
    )(place, tokens, own, before, after, *mine, *theirs, *heads)


def staying_kernel(which_ref, dlogits_ref, *refs):
    heads, (out_ref, held_ref, sem) = refs[:-3], refs[-3:]
    width = held_ref.shape[1]
    start = pl.multiple_of(which_ref[0] * width, 128)
    head = jnp.concatenate([ref[...] for ref in heads], axis=0)
    held_ref[...] = jnp.dot(dlogits_ref[...], head, preferred_element_type=F32).astype(BF16)
    copy = pltpu.make_async_copy(held_ref, out_ref.at[:, pl.ds(start, width)], sem)
    copy.start()
    copy.wait()


def staying_gradient(which, dlogits, heads):
    rows, columns = dlogits.shape
    width = heads[0].shape[1]
    return pl.pallas_call(
        staying_kernel,
        out_shape=jax.ShapeDtypeStruct((rows, 2 * width), BF16),
        in_specs=[SMEM] + [VMEM] * (1 + len(heads)),
        out_specs=ANY,
        scratch_shapes=[pltpu.VMEM((rows, width), BF16), pltpu.SemaphoreType.DMA],
        compiler_params=PARAMS,
        cost_estimate=pl.CostEstimate(
            flops=2 * rows * columns * width,
            bytes_accessed=2 * width * (rows + columns),
            transcendentals=0,
        ),
        name="staying_gradient",
    )(which, dlogits, *heads)


def placed_kernel(which_ref, incoming_ref, _, out_ref, sem):
    width = incoming_ref.shape[1]
    start = pl.multiple_of((1 - which_ref[0]) * width, 128)
    copy = pltpu.make_async_copy(incoming_ref, out_ref.at[:, pl.ds(start, width)], sem)
    copy.start()
    copy.wait()


def placed_beside(which, incoming, gradient):
    return pl.pallas_call(
        placed_kernel,
        out_shape=jax.ShapeDtypeStruct(gradient.shape, gradient.dtype),
        in_specs=[SMEM, ANY, ANY],
        out_specs=ANY,
        scratch_shapes=[pltpu.SemaphoreType.DMA],
        input_output_aliases={2: 0},
        compiler_params=PARAMS,
        name="place_incoming",
    )(which, incoming, gradient)


def body(hidden, head_weight, tokens, rewards, group_ids):
    shards = lax.axis_size("vocab")
    odd = lax.axis_index("section") % 2
    which = odd.reshape(1)
    place = jnp.stack([odd, lax.axis_index("vocab")])

    upper, lower = take(which, head_weight, 2)
    heads = gathered(upper, lower, "vocab")
    (other_half,) = take(1 - which, hidden, 1)
    partner_half = swapped(other_half, "section", 1)

    own = jnp.stack([rewards, (group_ids + 1).astype(F32)])
    count = lax.axis_size(("vocab", "section"))
    after = lax.ppermute(own, ("vocab", "section"), [(i + 1, i) for i in range(count - 1)])
    before = lax.ppermute(own, ("vocab", "section"), [(i, i + 1) for i in range(count - 1)])

    near = [o for o in range(shards) if bin(o).count("1") <= 1]
    far = [o for o in range(shards) if bin(o).count("1") > 1]
    mine, theirs, order = [], [], []
    for offsets in (near, far):
        pieces = [piece for offset in offsets for piece in heads[offset]]
        kept, sent = partial_scores(which, hidden, partner_half, pieces)
        mine.append(kept)
        theirs.append(swapped(sent, "section", 1))
        order += offsets
    pieces = [piece for offset in range(shards) for piece in heads[offset]]
    if order != list(range(shards)):
        mine = reordered(mine, order)
        theirs = reordered(theirs, order)
    logits, logprob, entropy, dlogits, outgoing = loss(
        place, tokens[None, :], own, before, after, mine, theirs, pieces, shards
    )
    partner_dlogits = swapped(dlogits, "section", 1)
    incoming = swapped(outgoing, "section", 1)
    staying = staying_gradient(which, partner_dlogits, pieces)
    previous_grad = placed_beside(which, incoming, staying)
    return (logits, logprob[0], entropy[0], previous_grad)


def reordered(blocks, order):
    whole = jnp.concatenate(blocks, axis=1)
    width = whole.shape[1] // len(order)
    parts = {offset: whole[:, i * width : (i + 1) * width] for i, offset in enumerate(order)}
    return [jnp.concatenate([parts[offset] for offset in sorted(order)], axis=1)]


def solution(mesh):
    placed = (
        P(("seq", "vocab", "section"), None),
        P(("seq", "vocab"), None),
        P(("seq", "vocab", "section")),
        P(("seq", "vocab", "section")),
        P(("seq", "vocab", "section")),
    )
    return jax.shard_map(
        body,
        mesh=mesh,
        in_specs=placed,
        out_specs=(
            P(("seq", "vocab", "section"), None),
            P(("seq", "vocab", "section")),
            P(("seq", "vocab", "section")),
            P(("seq", "vocab", "section"), None),
        ),
        check_vma=False,
    )
```

```python
import functools

import jax
import jax.numpy as jnp
from jax import lax
from jax.experimental import pallas as pl
from jax.experimental.pallas import tpu as pltpu
from jax.sharding import PartitionSpec as P

F32, BF16 = jnp.float32, jnp.bfloat16
HBM = pl.BlockSpec(memory_space=pltpu.HBM)
ANY = pl.BlockSpec(memory_space=pl.ANY)
SMEM = pl.BlockSpec(memory_space=pltpu.SMEM)
VMEM = pl.BlockSpec(memory_space=pltpu.VMEM)
PARAMS = pltpu.CompilerParams(vmem_limit_bytes=48 * 1024 * 1024)


def swapped(value, axis, mask):
    pairs = [(source, source ^ mask) for source in range(lax.axis_size(axis))]
    return lax.ppermute(value, axis, pairs)


def gathered(upper, lower, axis):
    count = lax.axis_size(axis)
    masks = [1 << bit for bit in range((count - 1).bit_length())]
    uppers, lowers = {0: upper}, {0: lower}
    for mask in masks:
        uppers[mask] = swapped(upper, axis, mask)
    for mask in reversed(masks):
        lowers[mask] = swapped(lower, axis, mask)
    for offset in sorted(range(1, count), key=lambda o: (bin(o).count("1"), o)):
        if offset in uppers:
            continue
        bits = [mask for mask in masks if offset & mask]
        uppers[offset] = swapped(uppers[offset ^ bits[-1]], axis, bits[-1])
        lowers[offset] = swapped(lowers[offset ^ bits[0]], axis, bits[0])
    return [(uppers[offset], lowers[offset]) for offset in range(count)]


def halves_kernel(which_ref, hidden_ref, head_ref, other_ref, upper_ref, lower_ref, sem):
    rows, width = other_ref.shape
    other = pl.multiple_of((1 - which_ref[0]) * width, 128)
    mine = pl.multiple_of(which_ref[0] * width, 128)
    copies = []
    for i in range(2):
        part = pl.ds(i * (rows // 2), rows // 2)
        source = hidden_ref.at[part, pl.ds(other, width)]
        copies.append(pltpu.make_async_copy(source, other_ref.at[part, :], sem.at[i]))
    for i, out in enumerate((upper_ref, lower_ref)):
        source = head_ref.at[:, pl.ds(pl.multiple_of(mine + i * (width // 2), 128), width // 2)]
        copies.append(pltpu.make_async_copy(source, out, sem.at[2 + i]))
    for copy in copies:
        copy.start()
    for copy in copies:
        copy.wait()


def halves(which, hidden, head):
    rows, width = hidden.shape[0], hidden.shape[1] // 2
    piece = jax.ShapeDtypeStruct((head.shape[0], width // 2), BF16)
    return pl.pallas_call(
        halves_kernel,
        out_shape=[jax.ShapeDtypeStruct((rows, width), BF16), piece, piece],
        in_specs=[SMEM, HBM, HBM],
        out_specs=[VMEM] * 3,
        scratch_shapes=[pltpu.SemaphoreType.DMA((4,))],
        compiler_params=pltpu.CompilerParams(vmem_limit_bytes=58 * 1024 * 1024),
        name="halves",
    )(which, hidden, head)


def turned_kernel(which_ref, hidden_ref, first_ref, second_ref, *refs):
    out_ref = refs[-1]
    rows, width = first_ref.shape
    block = 256
    for i in range(width // block):
        start = which_ref[0] * width + i * block
        own = hidden_ref[:, pl.ds(pl.multiple_of(start, 128), block)]
        out_ref[i * block : (i + 1) * block, :rows] = own.T
        part = slice(i * block, (i + 1) * block)
        other = first_ref[:, part] + second_ref[:, part]
        out_ref[part, rows:] = other.T


def turned(which, hidden, partner_halves, after):
    rows, width = partner_halves[0].shape
    return pl.pallas_call(
        turned_kernel,
        out_shape=jax.ShapeDtypeStruct((width, 2 * rows), BF16),
        in_specs=[SMEM] + [VMEM] * 3 + [ANY] * len(after),
        out_specs=VMEM,
        compiler_params=PARAMS,
        cost_estimate=pl.CostEstimate(
            flops=0, bytes_accessed=8 * rows * width, transcendentals=0
        ),
        name="turned_rows",
    )(which, hidden, *partner_halves, *after)


def partial_kernel(turned_ref, *refs):
    heads, (mine_ref, theirs_ref) = refs[:-2], refs[-2:]
    shard_rows, depth = heads[0].shape
    rows = mine_ref.shape[1]
    for i in range(len(heads) // 2):
        total = jnp.dot(heads[2 * i][...], turned_ref[:depth, :], preferred_element_type=F32)
        total += jnp.dot(heads[2 * i + 1][...], turned_ref[depth:, :], preferred_element_type=F32)
        mine_ref[i * shard_rows : (i + 1) * shard_rows, :] = total[:, :rows]
        theirs_ref[i * shard_rows : (i + 1) * shard_rows, :] = total[:, rows:]


def partial_scores(turned_rows, heads):
    width, rows = turned_rows.shape
    columns = sum(head.shape[0] for head in heads) // 2
    out = jax.ShapeDtypeStruct((columns, rows // 2), F32)
    return pl.pallas_call(
        partial_kernel,
        out_shape=[out, out],
        in_specs=[VMEM] * (1 + len(heads)),
        out_specs=[VMEM, VMEM],
        compiler_params=PARAMS,
        cost_estimate=pl.CostEstimate(
            flops=2 * rows * columns * width,
            bytes_accessed=2 * width * (rows + columns),
            transcendentals=0,
        ),
        name="partial_scores",
    )(turned_rows, *heads)


def advantage_kernel(own_ref, *refs):
    near, out_ref = refs[:-1], refs[-1]
    rows = own_ref.shape[1]
    eye = lax.broadcasted_iota(jnp.int32, (rows, rows), 0) == lax.broadcasted_iota(
        jnp.int32, (rows, rows), 1
    )
    groups = jnp.sum(jnp.where(eye, own_ref[1:2, :], 0.0), axis=1, keepdims=True)
    sums, counts = jnp.zeros((rows, 1), F32), jnp.zeros((rows, 1), F32)
    for ref in (own_ref, *near):
        member = ref[1:2, :] == groups
        sums += jnp.sum(jnp.where(member, ref[0:1, :], 0.0), axis=1, keepdims=True)
        counts += jnp.sum(jnp.where(member, 1.0, 0.0), axis=1, keepdims=True)
    means = jnp.sum(jnp.where(eye, sums / counts, 0.0), axis=0, keepdims=True)
    out_ref[...] = own_ref[0:1, :] - means


def advantages(own, *near):
    return pl.pallas_call(
        advantage_kernel,
        out_shape=jax.ShapeDtypeStruct((1, own.shape[1]), F32),
        in_specs=[VMEM] * (1 + len(near)),
        out_specs=VMEM,
        compiler_params=PARAMS,
        name="advantage",
    )(own, *near)


def loss_kernel(parts, shards, shard_ref, tokens_ref, advantage_ref, *refs):
    mine, theirs = refs[:parts], refs[parts : 2 * parts]
    logits_ref, logprob_ref, entropy_ref, dlogits_ref = refs[2 * parts :]
    shard = shard_ref[0]
    rows, columns = dlogits_ref.shape
    shard_rows = columns // shards

    scores = jnp.concatenate([a[...] + b[...] for a, b in zip(mine, theirs)], axis=0)
    tokens = tokens_ref[...]
    relative = ((tokens // shard_rows) ^ shard) * shard_rows + tokens % shard_rows
    chosen = lax.broadcasted_iota(jnp.int32, (columns, rows), 0) == relative
    row_max = jnp.max(scores, axis=0, keepdims=True)
    unnormed = jnp.exp(scores - row_max)
    denominator = jnp.sum(unnormed, axis=0, keepdims=True)
    probabilities = unnormed / denominator
    dlogits = advantage_ref[...] * (probabilities - jnp.where(chosen, 1.0, 0.0))
    for i in range(shards):
        block = slice(i * shard_rows, (i + 1) * shard_rows)
        dlogits_ref[:, block] = dlogits[block, :].T.astype(BF16)
        place = pl.multiple_of((shard ^ i) * shard_rows, 128)
        logits_ref[:, pl.ds(place, shard_rows)] = scores[block, :].T.astype(BF16)
    log_total = row_max + jnp.log(denominator)
    picked = jnp.sum(jnp.where(chosen, scores, 0.0), axis=0, keepdims=True)
    logprob_ref[...] = picked - log_total
    entropy_ref[...] = log_total - jnp.sum(probabilities * scores, axis=0, keepdims=True)


def loss(shard, tokens, advantage, mine, theirs, shards):
    rows = tokens.shape[1]
    columns = sum(part.shape[0] for part in mine)
    flat = jax.ShapeDtypeStruct((1, rows), F32)
    wide = jax.ShapeDtypeStruct((rows, columns), BF16)
    return pl.pallas_call(
        functools.partial(loss_kernel, len(mine), shards),
        out_shape=[wide, flat, flat, wide],
        in_specs=[SMEM] + [VMEM] * (2 + 2 * len(mine)),
        out_specs=[VMEM] * 4,
        compiler_params=PARAMS,
        cost_estimate=pl.CostEstimate(
            flops=10 * rows * columns,
            bytes_accessed=12 * rows * columns,
            transcendentals=rows * columns,
        ),
        name="loss",
    )(shard, tokens, advantage, *mine, *theirs)


def multiplied(dlogits, heads, out_ref, start):
    block = 256
    for j in range(heads[0].shape[1] // block):
        part = slice(j * block, (j + 1) * block)
        head = jnp.concatenate([ref[:, part] for ref in heads], axis=0)
        product = jnp.dot(dlogits, head, preferred_element_type=F32)
        out_ref[:, start + j * block : start + (j + 1) * block] = product.astype(BF16)


def gradient_cost(rows, columns, width):
    return pl.CostEstimate(
        flops=2 * rows * columns * width,
        bytes_accessed=2 * width * (rows + columns),
        transcendentals=0,
    )


def first_kernel(dlogits_ref, *refs):
    heads, out_ref = refs[:-1], refs[-1]
    columns = dlogits_ref.shape[1]
    out_ref[:, :columns] = dlogits_ref[...]
    multiplied(dlogits_ref[...], heads, out_ref, columns)


def first_message(dlogits, heads):
    rows, columns = dlogits.shape
    width = heads[0].shape[1]
    return pl.pallas_call(
        first_kernel,
        out_shape=jax.ShapeDtypeStruct((rows, columns + width), BF16),
        in_specs=[VMEM] * (1 + len(heads)),
        out_specs=VMEM,
        compiler_params=PARAMS,
        cost_estimate=gradient_cost(rows, columns, width),
        name="first_message",
    )(dlogits, *heads)


def second_kernel(dlogits_ref, _, *refs):
    multiplied(dlogits_ref[...], refs[:-1], refs[-1], 0)


def second_message(dlogits, first, heads):
    rows, columns = dlogits.shape
    width = heads[0].shape[1]
    return pl.pallas_call(
        second_kernel,
        out_shape=jax.ShapeDtypeStruct((rows, width), BF16),
        in_specs=[VMEM, ANY] + [VMEM] * len(heads),
        out_specs=VMEM,
        compiler_params=PARAMS,
        cost_estimate=gradient_cost(rows, columns, width),
        name="second_message",
    )(dlogits, first, *heads)


def staying_kernel(which_ref, first_ref, *refs):
    heads, (out_ref, held_ref, sem) = refs[:-3], refs[-3:]
    width = held_ref.shape[1]
    depth = width // 2
    columns = first_ref.shape[1] - depth
    mine = pl.multiple_of(which_ref[0] * width, 128)
    other = pl.multiple_of((1 - which_ref[0]) * width, 128)
    copies = [
        pltpu.make_async_copy(
            first_ref.at[:, pl.ds(columns, depth)], out_ref.at[:, pl.ds(other, depth)], sem.at[0]
        )
    ]
    copies[0].start()
    dlogits = first_ref[:, :columns]
    for i in range(2):
        multiplied(dlogits, heads[i::2], held_ref, i * depth)
        copies.append(
            pltpu.make_async_copy(
                held_ref.at[:, pl.ds(i * depth, depth)],
                out_ref.at[:, pl.ds(pl.multiple_of(mine + i * depth, 128), depth)],
                sem.at[i + 1],
            )
        )
        copies[-1].start()
    for copy in copies:
        copy.wait()


def staying_gradient(which, first, heads):
    rows = first.shape[0]
    depth = heads[0].shape[1]
    columns = first.shape[1] - depth
    return pl.pallas_call(
        staying_kernel,
        out_shape=jax.ShapeDtypeStruct((rows, 4 * depth), BF16),
        in_specs=[SMEM] + [VMEM] * (1 + len(heads)),
        out_specs=HBM,
        scratch_shapes=[pltpu.VMEM((rows, 2 * depth), BF16), pltpu.SemaphoreType.DMA((3,))],
        compiler_params=PARAMS,
        cost_estimate=gradient_cost(rows, columns, 2 * depth),
        name="staying_gradient",
    )(which, first, *heads)


def placed_kernel(which_ref, second_ref, _, out_ref, sem):
    rows, depth = second_ref.shape
    start = pl.multiple_of((1 - which_ref[0]) * (2 * depth) + depth, 128)
    copies = []
    for i in range(4):
        part = pl.ds(i * (rows // 4), rows // 4)
        target = out_ref.at[part, pl.ds(start, depth)]
        copies.append(pltpu.make_async_copy(second_ref.at[part, :], target, sem.at[i]))
    for copy in copies:
        copy.start()
    for copy in copies:
        copy.wait()


def placed_beside(which, second, gradient):
    return pl.pallas_call(
        placed_kernel,
        out_shape=jax.ShapeDtypeStruct(gradient.shape, gradient.dtype),
        in_specs=[SMEM, VMEM, HBM],
        out_specs=HBM,
        scratch_shapes=[pltpu.SemaphoreType.DMA((4,))],
        input_output_aliases={2: 0},
        compiler_params=PARAMS,
        name="place_second",
    )(which, second, gradient)


def of_parts(value, axes, parts, pairs):
    count = lax.axis_size(axes)
    moves = [(p * count + a, p * count + b) for p in parts for a, b in pairs]
    return lax.ppermute(value, ("seq",) + axes, moves)


def body(hidden, head_weight, tokens, rewards, group_ids):
    shards = lax.axis_size("vocab")
    which = (lax.axis_index("section") % 2).reshape(1)
    shard = lax.axis_index("vocab").reshape(1)
    parts = lax.axis_size("seq")
    leading, following = range(1, parts), range(1)
    rows_axes = ("vocab", "section")
    count = lax.axis_size(rows_axes)
    sections = lax.axis_size("section")
    pairs = [(i, i ^ 1) for i in range(sections)]
    up = [(i, i + 1) for i in range(count - 1)]
    down = [(i + 1, i) for i in range(count - 1)]
    own = jnp.stack([rewards, (group_ids + 1).astype(F32)])

    other_half, upper, lower = halves(which, hidden, head_weight)
    first_half = of_parts(other_half, ("section",), following, pairs)
    edges = [of_parts(own, rows_axes, following, moves) for moves in (up, down)]

    upper, lower, first_half, edges = lax.optimization_barrier((upper, lower, first_half, edges))
    heads = gathered(upper, lower, "vocab")

    near = [o for o in range(shards) if bin(o).count("1") <= 1]
    far = [o for o in range(shards) if bin(o).count("1") > 1]
    arrived = [piece for o in near[1:] for piece in heads[o]]
    other_half, late, _ = lax.optimization_barrier((other_half, own, arrived))
    second_half = of_parts(other_half, ("section",), leading, pairs)
    edges += [of_parts(late, rows_axes, leading, moves) for moves in (up, down)]
    advantage = advantages(own, *edges)

    rows = turned(which, hidden, (first_half, second_half), (advantage,))
    mine, theirs = [], []
    for offsets in (near, far):
        kept, sent = partial_scores(rows, [piece for o in offsets for piece in heads[o]])
        mine.append(kept)
        theirs.append(swapped(sent, "section", 1))
    mine, theirs = in_order(mine, near + far), in_order(theirs, near + far)
    logits, logprob, entropy, dlogits = loss(
        shard, tokens[None, :], advantage, mine, theirs, shards
    )
    pieces = [piece for pair in heads for piece in pair]
    first = first_message(dlogits, pieces[0::2])
    first_in = swapped(first, "section", 1)
    second_in = swapped(second_message(dlogits, first, pieces[1::2]), "section", 1)
    staying = staying_gradient(which, first_in, pieces)
    previous_grad = placed_beside(which, second_in, staying)
    return (logits, logprob[0], entropy[0], previous_grad)


def in_order(blocks, order):
    if order == sorted(order):
        return blocks
    whole = jnp.concatenate(blocks, axis=0)
    width = whole.shape[0] // len(order)
    parts = {offset: whole[i * width : (i + 1) * width] for i, offset in enumerate(order)}
    return [jnp.concatenate([parts[offset] for offset in sorted(order)], axis=0)]


def solution(mesh):
    placed = (
        P(("seq", "vocab", "section"), None),
        P(("seq", "vocab"), None),
        P(("seq", "vocab", "section")),
        P(("seq", "vocab", "section")),
        P(("seq", "vocab", "section")),
    )
    return jax.shard_map(
        body,
        mesh=mesh,
        in_specs=placed,
        out_specs=(
            P(("seq", "vocab", "section"), None),
            P(("seq", "vocab", "section")),
            P(("seq", "vocab", "section")),
            P(("seq", "vocab", "section"), None),
        ),
        check_vma=False,
    )
```

```python
import functools

import jax
import jax.numpy as jnp
from jax import lax
from jax.experimental import pallas as pl
from jax.experimental.pallas import tpu as pltpu
from jax.sharding import PartitionSpec as P

F32, BF16 = jnp.float32, jnp.bfloat16
HBM = pl.BlockSpec(memory_space=pltpu.HBM)
ANY = pl.BlockSpec(memory_space=pl.ANY)
SMEM = pl.BlockSpec(memory_space=pltpu.SMEM)
VMEM = pl.BlockSpec(memory_space=pltpu.VMEM)
PARAMS = pltpu.CompilerParams(vmem_limit_bytes=48 * 1024 * 1024)


def swapped(value, axis, mask):
    pairs = [(source, source ^ mask) for source in range(lax.axis_size(axis))]
    return lax.ppermute(value, axis, pairs)


def gathered(first_wave, second_wave, before_passing_on, axis):
    count = lax.axis_size(axis)
    masks = [1 << bit for bit in range((count - 1).bit_length())]
    uppers, lowers = {0: first_wave[0]}, {0: first_wave[1]}
    for mask in masks:
        early = mask == masks[0]
        uppers[mask] = swapped((first_wave if early else second_wave)[0], axis, mask)
    for mask in reversed(masks):
        early = mask == masks[-1]
        lowers[mask] = swapped((first_wave if early else second_wave)[1], axis, mask)
    for offset in sorted(range(1, count), key=lambda o: (bin(o).count("1"), o)):
        if offset in uppers:
            continue
        bits = [mask for mask in masks if offset & mask]
        upper, lower, _ = lax.optimization_barrier(
            (uppers[offset ^ bits[-1]], lowers[offset ^ bits[0]], before_passing_on)
        )
        uppers[offset] = swapped(upper, axis, bits[-1])
        lowers[offset] = swapped(lower, axis, bits[0])
    return [(uppers[offset], lowers[offset]) for offset in range(count)]


def take_kernel(which_ref, value_ref, *refs):
    outs, sem = refs[:-1], refs[-1]
    width = outs[0].shape[1]
    start = which_ref[0] * width * len(outs)
    copies = []
    for i, out in enumerate(outs):
        source = value_ref.at[:, pl.ds(pl.multiple_of(start + i * width, 128), width)]
        copies.append(pltpu.make_async_copy(source, out, sem.at[i]))
    for copy in copies:
        copy.start()
    for copy in copies:
        copy.wait()


def take(which, value, pieces):
    rows, width = value.shape[0], value.shape[1] // 2 // pieces
    return pl.pallas_call(
        take_kernel,
        out_shape=[jax.ShapeDtypeStruct((rows, width), value.dtype)] * pieces,
        in_specs=[SMEM, ANY],
        out_specs=[ANY] * pieces,
        scratch_shapes=[pltpu.SemaphoreType.DMA((pieces,))],
        compiler_params=PARAMS,
        cost_estimate=pl.CostEstimate(
            flops=0, bytes_accessed=value.size * value.dtype.itemsize, transcendentals=0
        ),
        name="take_half",
    )(which, value)


def turned_kernel(which_ref, hidden_ref, partner_ref, *refs):
    out_ref = refs[-1]
    rows, width = partner_ref.shape
    block = 256
    for i in range(width // block):
        start = which_ref[0] * width + i * block
        own = hidden_ref[:, pl.ds(pl.multiple_of(start, 128), block)]
        out_ref[i * block : (i + 1) * block, :rows] = own.T
        part = slice(i * block, (i + 1) * block)
        out_ref[part, rows:] = partner_ref[:, part].T


def turned(which, hidden, partner_half, after):
    rows, width = partner_half.shape
    return pl.pallas_call(
        turned_kernel,
        out_shape=jax.ShapeDtypeStruct((width, 2 * rows), BF16),
        in_specs=[SMEM] + [VMEM] * 2 + [ANY] * len(after),
        out_specs=VMEM,
        compiler_params=PARAMS,
        cost_estimate=pl.CostEstimate(
            flops=0, bytes_accessed=8 * rows * width, transcendentals=0
        ),
        name="turned_rows",
    )(which, hidden, partner_half, *after)


def partial_kernel(turned_ref, *refs):
    heads, (mine_ref, theirs_ref) = refs[:-2], refs[-2:]
    shard_rows, depth = heads[0].shape
    rows = mine_ref.shape[1]
    for i in range(len(heads) // 2):
        total = jnp.dot(heads[2 * i][...], turned_ref[:depth, :], preferred_element_type=F32)
        total += jnp.dot(heads[2 * i + 1][...], turned_ref[depth:, :], preferred_element_type=F32)
        mine_ref[i * shard_rows : (i + 1) * shard_rows, :] = total[:, :rows]
        theirs_ref[i * shard_rows : (i + 1) * shard_rows, :] = total[:, rows:]


def partial_scores(turned_rows, heads):
    width, rows = turned_rows.shape
    columns = sum(head.shape[0] for head in heads) // 2
    out = jax.ShapeDtypeStruct((columns, rows // 2), F32)
    return pl.pallas_call(
        partial_kernel,
        out_shape=[out, out],
        in_specs=[VMEM] * (1 + len(heads)),
        out_specs=[VMEM, VMEM],
        compiler_params=PARAMS,
        cost_estimate=pl.CostEstimate(
            flops=2 * rows * columns * width,
            bytes_accessed=2 * width * (rows + columns),
            transcendentals=0,
        ),
        name="partial_scores",
    )(turned_rows, *heads)


def advantage_kernel(own_ref, *refs):
    near, out_ref = refs[:-1], refs[-1]
    rows = own_ref.shape[1]
    eye = lax.broadcasted_iota(jnp.int32, (rows, rows), 0) == lax.broadcasted_iota(
        jnp.int32, (rows, rows), 1
    )
    groups = jnp.sum(jnp.where(eye, own_ref[1:2, :], 0.0), axis=1, keepdims=True)
    sums, counts = jnp.zeros((rows, 1), F32), jnp.zeros((rows, 1), F32)
    for ref in (own_ref, *near):
        member = ref[1:2, :] == groups
        sums += jnp.sum(jnp.where(member, ref[0:1, :], 0.0), axis=1, keepdims=True)
        counts += jnp.sum(jnp.where(member, 1.0, 0.0), axis=1, keepdims=True)
    means = jnp.sum(jnp.where(eye, sums / counts, 0.0), axis=0, keepdims=True)
    out_ref[...] = own_ref[0:1, :] - means


def advantages(own, *near):
    return pl.pallas_call(
        advantage_kernel,
        out_shape=jax.ShapeDtypeStruct((1, own.shape[1]), F32),
        in_specs=[VMEM] * (1 + len(near)),
        out_specs=VMEM,
        compiler_params=PARAMS,
        name="advantage",
    )(own, *near)


def loss_kernel(parts, shards, shard_ref, tokens_ref, advantage_ref, *refs):
    mine, theirs = refs[:parts], refs[parts : 2 * parts]
    logits_ref, logprob_ref, entropy_ref, dlogits_ref = refs[2 * parts :]
    shard = shard_ref[0]
    rows, columns = dlogits_ref.shape
    shard_rows = columns // shards

    scores = jnp.concatenate([a[...] + b[...] for a, b in zip(mine, theirs)], axis=0)
    tokens = tokens_ref[...]
    relative = ((tokens // shard_rows) ^ shard) * shard_rows + tokens % shard_rows
    chosen = lax.broadcasted_iota(jnp.int32, (columns, rows), 0) == relative
    row_max = jnp.max(scores, axis=0, keepdims=True)
    unnormed = jnp.exp(scores - row_max)
    denominator = jnp.sum(unnormed, axis=0, keepdims=True)
    probabilities = unnormed / denominator
    dlogits = advantage_ref[...] * (probabilities - jnp.where(chosen, 1.0, 0.0))
    for i in range(shards):
        block = slice(i * shard_rows, (i + 1) * shard_rows)
        dlogits_ref[:, block] = dlogits[block, :].T.astype(BF16)
        place = pl.multiple_of((shard ^ i) * shard_rows, 128)
        logits_ref[:, pl.ds(place, shard_rows)] = scores[block, :].T.astype(BF16)
    log_total = row_max + jnp.log(denominator)
    picked = jnp.sum(jnp.where(chosen, scores, 0.0), axis=0, keepdims=True)
    logprob_ref[...] = picked - log_total
    entropy_ref[...] = log_total - jnp.sum(probabilities * scores, axis=0, keepdims=True)


def loss(shard, tokens, advantage, mine, theirs, shards):
    rows = tokens.shape[1]
    columns = sum(part.shape[0] for part in mine)
    flat = jax.ShapeDtypeStruct((1, rows), F32)
    wide = jax.ShapeDtypeStruct((rows, columns), BF16)
    return pl.pallas_call(
        functools.partial(loss_kernel, len(mine), shards),
        out_shape=[wide, flat, flat, wide],
        in_specs=[SMEM] + [VMEM] * (2 + 2 * len(mine)),
        out_specs=[VMEM] * 4,
        compiler_params=PARAMS,
        cost_estimate=pl.CostEstimate(
            flops=10 * rows * columns,
            bytes_accessed=12 * rows * columns,
            transcendentals=rows * columns,
        ),
        name="loss",
    )(shard, tokens, advantage, *mine, *theirs)


def multiplied(dlogits, heads, out_ref, start):
    block = 256
    for j in range(heads[0].shape[1] // block):
        part = slice(j * block, (j + 1) * block)
        head = jnp.concatenate([ref[:, part] for ref in heads], axis=0)
        product = jnp.dot(dlogits, head, preferred_element_type=F32)
        out_ref[:, start + j * block : start + (j + 1) * block] = product.astype(BF16)


def gradient_cost(rows, columns, width):
    return pl.CostEstimate(
        flops=2 * rows * columns * width,
        bytes_accessed=2 * width * (rows + columns),
        transcendentals=0,
    )


def first_kernel(dlogits_ref, *refs):
    heads, out_ref = refs[:-1], refs[-1]
    columns = dlogits_ref.shape[1]
    out_ref[:, :columns] = dlogits_ref[...]
    multiplied(dlogits_ref[...], heads, out_ref, columns)


def first_message(dlogits, heads):
    rows, columns = dlogits.shape
    width = heads[0].shape[1]
    return pl.pallas_call(
        first_kernel,
        out_shape=jax.ShapeDtypeStruct((rows, columns + width), BF16),
        in_specs=[VMEM] * (1 + len(heads)),
        out_specs=VMEM,
        compiler_params=PARAMS,
        cost_estimate=gradient_cost(rows, columns, width),
        name="first_message",
    )(dlogits, *heads)


def second_kernel(dlogits_ref, _, *refs):
    multiplied(dlogits_ref[...], refs[:-1], refs[-1], 0)


def second_message(dlogits, first, heads):
    rows, columns = dlogits.shape
    width = heads[0].shape[1]
    return pl.pallas_call(
        second_kernel,
        out_shape=jax.ShapeDtypeStruct((rows, width), BF16),
        in_specs=[VMEM, ANY] + [VMEM] * len(heads),
        out_specs=VMEM,
        compiler_params=PARAMS,
        cost_estimate=gradient_cost(rows, columns, width),
        name="second_message",
    )(dlogits, first, *heads)


def staying_kernel(which_ref, first_ref, *refs):
    heads, (out_ref, held_ref, sem) = refs[:-3], refs[-3:]
    width = held_ref.shape[1]
    depth = width // 2
    columns = first_ref.shape[1] - depth
    mine = pl.multiple_of(which_ref[0] * width, 128)
    other = pl.multiple_of((1 - which_ref[0]) * width, 128)
    copies = [
        pltpu.make_async_copy(
            first_ref.at[:, pl.ds(columns, depth)], out_ref.at[:, pl.ds(other, depth)], sem.at[0]
        )
    ]
    copies[0].start()
    dlogits = first_ref[:, :columns]
    for i in range(2):
        multiplied(dlogits, heads[i::2], held_ref, i * depth)
        copies.append(
            pltpu.make_async_copy(
                held_ref.at[:, pl.ds(i * depth, depth)],
                out_ref.at[:, pl.ds(pl.multiple_of(mine + i * depth, 128), depth)],
                sem.at[i + 1],
            )
        )
        copies[-1].start()
    for copy in copies:
        copy.wait()


def staying_gradient(which, first, heads):
    rows = first.shape[0]
    depth = heads[0].shape[1]
    columns = first.shape[1] - depth
    return pl.pallas_call(
        staying_kernel,
        out_shape=jax.ShapeDtypeStruct((rows, 4 * depth), BF16),
        in_specs=[SMEM] + [VMEM] * (1 + len(heads)),
        out_specs=HBM,
        scratch_shapes=[pltpu.VMEM((rows, 2 * depth), BF16), pltpu.SemaphoreType.DMA((3,))],
        compiler_params=PARAMS,
        cost_estimate=gradient_cost(rows, columns, 2 * depth),
        name="staying_gradient",
    )(which, first, *heads)


def placed_kernel(which_ref, second_ref, _, out_ref, sem):
    rows, depth = second_ref.shape
    start = pl.multiple_of((1 - which_ref[0]) * (2 * depth) + depth, 128)
    copies = []
    for i in range(4):
        part = pl.ds(i * (rows // 4), rows // 4)
        target = out_ref.at[part, pl.ds(start, depth)]
        copies.append(pltpu.make_async_copy(second_ref.at[part, :], target, sem.at[i]))
    for copy in copies:
        copy.start()
    for copy in copies:
        copy.wait()


def placed_beside(which, second, gradient):
    return pl.pallas_call(
        placed_kernel,
        out_shape=jax.ShapeDtypeStruct(gradient.shape, gradient.dtype),
        in_specs=[SMEM, VMEM, HBM],
        out_specs=HBM,
        scratch_shapes=[pltpu.SemaphoreType.DMA((4,))],
        input_output_aliases={2: 0},
        compiler_params=PARAMS,
        name="place_second",
    )(which, second, gradient)


def body(hidden, head_weight, tokens, rewards, group_ids):
    shards = lax.axis_size("vocab")
    which = (lax.axis_index("section") % 2).reshape(1)
    shard = lax.axis_index("vocab").reshape(1)
    near = [o for o in range(shards) if bin(o).count("1") <= 1]
    far = [o for o in range(shards) if bin(o).count("1") > 1]

    pieces = tuple(take(which, head_weight, 2))
    late_hidden, pieces = lax.optimization_barrier((hidden, pieces))
    (other_half,) = take(1 - which, late_hidden, 1)
    other_half, late_pieces = lax.optimization_barrier((other_half, pieces))
    partner_half = swapped(other_half, "section", 1)

    own = jnp.stack([rewards, (group_ids + 1).astype(F32)])
    axes = ("vocab", "section")
    count = lax.axis_size(axes)
    before = lax.ppermute(own, axes, [(i, i + 1) for i in range(count - 1)])
    after = lax.ppermute(own, axes, [(i + 1, i) for i in range(count - 1)])
    advantage = advantages(own, before, after)
    heads = gathered(pieces, late_pieces, advantage, "vocab")

    rows = turned(which, hidden, partner_half, (advantage,))
    mine, theirs = [], []
    for offsets in (near, far):
        kept, sent = partial_scores(rows, [piece for o in offsets for piece in heads[o]])
        mine.append(kept)
        theirs.append(swapped(sent, "section", 1))
    mine, theirs = in_order(mine, near + far), in_order(theirs, near + far)
    logits, logprob, entropy, dlogits = loss(
        shard, tokens[None, :], advantage, mine, theirs, shards
    )
    pieces = [piece for pair in heads for piece in pair]
    first = first_message(dlogits, pieces[0::2])
    first_in = swapped(first, "section", 1)
    second_in = swapped(second_message(dlogits, first, pieces[1::2]), "section", 1)
    staying = staying_gradient(which, first_in, pieces)
    previous_grad = placed_beside(which, second_in, staying)
    return (logits, logprob[0], entropy[0], previous_grad)


def in_order(blocks, order):
    if order == sorted(order):
        return blocks
    whole = jnp.concatenate(blocks, axis=0)
    width = whole.shape[0] // len(order)
    parts = {offset: whole[i * width : (i + 1) * width] for i, offset in enumerate(order)}
    return [jnp.concatenate([parts[offset] for offset in sorted(order)], axis=0)]


def solution(mesh):
    placed = (
        P(("seq", "vocab", "section"), None),
        P(("seq", "vocab"), None),
        P(("seq", "vocab", "section")),
        P(("seq", "vocab", "section")),
        P(("seq", "vocab", "section")),
    )
    return jax.shard_map(
        body,
        mesh=mesh,
        in_specs=placed,
        out_specs=(
            P(("seq", "vocab", "section"), None),
            P(("seq", "vocab", "section")),
            P(("seq", "vocab", "section")),
            P(("seq", "vocab", "section"), None),
        ),
        check_vma=False,
    )
```

```python
import functools

import jax
import jax.numpy as jnp
from jax import lax
from jax.experimental import pallas as pl
from jax.experimental.pallas import tpu as pltpu
from jax.sharding import PartitionSpec as P

F32, BF16 = jnp.float32, jnp.bfloat16
HBM = pl.BlockSpec(memory_space=pltpu.HBM)
ANY = pl.BlockSpec(memory_space=pl.ANY)
SMEM = pl.BlockSpec(memory_space=pltpu.SMEM)
VMEM = pl.BlockSpec(memory_space=pltpu.VMEM)
PARAMS = pltpu.CompilerParams(vmem_limit_bytes=16 * 1024 * 1024)


def swapped(value, axis, mask):
    pairs = [(source, source ^ mask) for source in range(lax.axis_size(axis))]
    return lax.ppermute(value, axis, pairs)


def gathered(first_wave, second_wave, axis):
    count = lax.axis_size(axis)
    masks = [1 << bit for bit in range((count - 1).bit_length())]
    uppers, lowers = {0: first_wave[0]}, {0: first_wave[1]}
    for mask in masks:
        early = mask == masks[0]
        uppers[mask] = swapped((first_wave if early else second_wave)[0], axis, mask)
    for mask in reversed(masks):
        early = mask == masks[-1]
        lowers[mask] = swapped((first_wave if early else second_wave)[1], axis, mask)
    for offset in sorted(range(1, count), key=lambda o: (bin(o).count("1"), o)):
        if offset in uppers:
            continue
        bits = [mask for mask in masks if offset & mask]
        uppers[offset] = swapped(uppers[offset ^ bits[-1]], axis, bits[-1])
        lowers[offset] = swapped(lowers[offset ^ bits[0]], axis, bits[0])
    return [(uppers[offset], lowers[offset]) for offset in range(count)]


def take_kernel(which_ref, value_ref, *refs):
    outs, sem = refs[:-1], refs[-1]
    width = outs[0].shape[1]
    start = which_ref[0] * width * len(outs)
    copies = []
    for i, out in enumerate(outs):
        source = value_ref.at[:, pl.ds(pl.multiple_of(start + i * width, 128), width)]
        copies.append(pltpu.make_async_copy(source, out, sem.at[i]))
    for copy in copies:
        copy.start()
    for copy in copies:
        copy.wait()


def take(which, value, pieces):
    rows, width = value.shape[0], value.shape[1] // 2 // pieces
    return pl.pallas_call(
        take_kernel,
        out_shape=[jax.ShapeDtypeStruct((rows, width), value.dtype)] * pieces,
        in_specs=[SMEM, ANY],
        out_specs=[ANY] * pieces,
        scratch_shapes=[pltpu.SemaphoreType.DMA((pieces,))],
        compiler_params=PARAMS,
        cost_estimate=pl.CostEstimate(
            flops=0, bytes_accessed=value.size * value.dtype.itemsize, transcendentals=0
        ),
        name="take_half",
    )(which, value)


def turned_kernel(which_ref, hidden_ref, partner_ref, out_ref):
    rows, width = partner_ref.shape
    block = 256
    for i in range(width // block):
        start = which_ref[0] * width + i * block
        own = hidden_ref[:, pl.ds(pl.multiple_of(start, 128), block)]
        out_ref[i * block : (i + 1) * block, :rows] = own.T
        part = slice(i * block, (i + 1) * block)
        out_ref[part, rows:] = partner_ref[:, part].T


def turned(which, hidden, partner_half):
    rows, width = partner_half.shape
    return pl.pallas_call(
        turned_kernel,
        out_shape=jax.ShapeDtypeStruct((width, 2 * rows), BF16),
        in_specs=[SMEM] + [VMEM] * 2,
        out_specs=VMEM,
        compiler_params=PARAMS,
        cost_estimate=pl.CostEstimate(
            flops=0, bytes_accessed=8 * rows * width, transcendentals=0
        ),
        name="turned_rows",
    )(which, hidden, partner_half)


def partial_kernel(facts, turned_ref, *refs):
    heads, (mine_ref, theirs_ref) = refs[facts:-2], refs[-2:]
    shard_rows, depth = heads[0].shape
    rows = mine_ref.shape[1]
    for i in range(len(heads) // 2):
        total = jnp.dot(heads[2 * i][...], turned_ref[:depth, :], preferred_element_type=F32)
        total += jnp.dot(heads[2 * i + 1][...], turned_ref[depth:, :], preferred_element_type=F32)
        mine_ref[i * shard_rows : (i + 1) * shard_rows, :] = total[:, :rows]
        theirs_ref[i * shard_rows : (i + 1) * shard_rows, :] = total[:, rows:]
    if facts:
        theirs_ref[mine_ref.shape[0] :, :] = refs[0][...]


def partial_scores(turned_rows, heads, facts=()):
    width, rows = turned_rows.shape
    columns = sum(head.shape[0] for head in heads) // 2
    below = sum(fact.shape[0] for fact in facts)
    return pl.pallas_call(
        functools.partial(partial_kernel, len(facts)),
        out_shape=[
            jax.ShapeDtypeStruct((columns, rows // 2), F32),
            jax.ShapeDtypeStruct((columns + below, rows // 2), F32),
        ],
        in_specs=[VMEM] * (1 + len(facts) + len(heads)),
        out_specs=[VMEM, VMEM],
        compiler_params=PARAMS,
        cost_estimate=pl.CostEstimate(
            flops=2 * rows * columns * width,
            bytes_accessed=2 * width * (rows + columns),
            transcendentals=0,
        ),
        name="partial_scores",
    )(turned_rows, *facts, *heads)


def advantage_of(own, outer, partner):
    rows = own.shape[1]
    eye = lax.broadcasted_iota(jnp.int32, (rows, rows), 0) == lax.broadcasted_iota(
        jnp.int32, (rows, rows), 1
    )
    groups = jnp.sum(jnp.where(eye, own[1:2, :], 0.0), axis=1, keepdims=True)
    sums, counts = jnp.zeros((rows, 1), F32), jnp.zeros((rows, 1), F32)
    for facts in (own, outer, partner):
        member = facts[1:2, :] == groups
        sums += jnp.sum(jnp.where(member, facts[0:1, :], 0.0), axis=1, keepdims=True)
        counts += jnp.sum(jnp.where(member, 1.0, 0.0), axis=1, keepdims=True)
    return own[0:1, :] - jnp.sum(jnp.where(eye, sums / counts, 0.0), axis=0, keepdims=True)


def loss_kernel(parts, shards, shard_ref, tokens_ref, own_ref, outer_ref, *refs):
    mine, theirs = refs[:parts], refs[parts : 2 * parts]
    logits_ref, logprob_ref, entropy_ref, dlogits_ref = refs[2 * parts :]
    shard = shard_ref[0]
    rows, columns = dlogits_ref.shape
    shard_rows = columns // shards

    lengths = [ref.shape[0] for ref in mine]
    partner = theirs[0][lengths[0] :, :]
    advantage = advantage_of(own_ref[...], outer_ref[...], partner)
    scores = jnp.concatenate(
        [a[...] + b[:n, :] for a, b, n in zip(mine, theirs, lengths)], axis=0
    )
    tokens = tokens_ref[...]
    relative = ((tokens // shard_rows) ^ shard) * shard_rows + tokens % shard_rows
    chosen = lax.broadcasted_iota(jnp.int32, (columns, rows), 0) == relative
    row_max = jnp.max(scores, axis=0, keepdims=True)
    unnormed = jnp.exp(scores - row_max)
    denominator = jnp.sum(unnormed, axis=0, keepdims=True)
    probabilities = unnormed / denominator
    dlogits = advantage * (probabilities - jnp.where(chosen, 1.0, 0.0))
    for i in range(shards):
        block = slice(i * shard_rows, (i + 1) * shard_rows)
        dlogits_ref[:, block] = dlogits[block, :].T.astype(BF16)
        place = pl.multiple_of((shard ^ i) * shard_rows, 128)
        logits_ref[:, pl.ds(place, shard_rows)] = scores[block, :].T.astype(BF16)
    log_total = row_max + jnp.log(denominator)
    picked = jnp.sum(jnp.where(chosen, scores, 0.0), axis=0, keepdims=True)
    logprob_ref[...] = picked - log_total
    entropy_ref[...] = log_total - jnp.sum(probabilities * scores, axis=0, keepdims=True)


def loss(shard, tokens, own, outer, mine, theirs, shards):
    rows = tokens.shape[1]
    columns = sum(part.shape[0] for part in mine)
    flat = jax.ShapeDtypeStruct((1, rows), F32)
    wide = jax.ShapeDtypeStruct((rows, columns), BF16)
    return pl.pallas_call(
        functools.partial(loss_kernel, len(mine), shards),
        out_shape=[wide, flat, flat, wide],
        in_specs=[SMEM] + [VMEM] * (3 + 2 * len(mine)),
        out_specs=[VMEM] * 4,
        compiler_params=PARAMS,
        cost_estimate=pl.CostEstimate(
            flops=10 * rows * columns,
            bytes_accessed=12 * rows * columns,
            transcendentals=rows * columns,
        ),
        name="loss",
    )(shard, tokens, own, outer, *mine, *theirs)


def multiplied(dlogits, heads, out_ref, start):
    block = 256
    for j in range(heads[0].shape[1] // block):
        part = slice(j * block, (j + 1) * block)
        head = jnp.concatenate([ref[:, part] for ref in heads], axis=0)
        product = jnp.dot(dlogits, head, preferred_element_type=F32)
        out_ref[:, start + j * block : start + (j + 1) * block] = product.astype(BF16)


def gradient_cost(rows, columns, width):
    return pl.CostEstimate(
        flops=2 * rows * columns * width,
        bytes_accessed=2 * width * (rows + columns),
        transcendentals=0,
    )


def first_kernel(dlogits_ref, *refs):
    heads, out_ref = refs[:-1], refs[-1]
    columns = dlogits_ref.shape[1]
    out_ref[:, :columns] = dlogits_ref[...]
    multiplied(dlogits_ref[...], heads, out_ref, columns)


def first_message(dlogits, heads):
    rows, columns = dlogits.shape
    width = heads[0].shape[1]
    return pl.pallas_call(
        first_kernel,
        out_shape=jax.ShapeDtypeStruct((rows, columns + width), BF16),
        in_specs=[VMEM] * (1 + len(heads)),
        out_specs=VMEM,
        compiler_params=PARAMS,
        cost_estimate=gradient_cost(rows, columns, width),
        name="first_message",
    )(dlogits, *heads)


def second_kernel(dlogits_ref, _, *refs):
    multiplied(dlogits_ref[...], refs[:-1], refs[-1], 0)


def second_message(dlogits, first, heads):
    rows, columns = dlogits.shape
    width = heads[0].shape[1]
    return pl.pallas_call(
        second_kernel,
        out_shape=jax.ShapeDtypeStruct((rows, width), BF16),
        in_specs=[VMEM, ANY] + [VMEM] * len(heads),
        out_specs=VMEM,
        compiler_params=PARAMS,
        cost_estimate=gradient_cost(rows, columns, width),
        name="second_message",
    )(dlogits, first, *heads)


def staying_kernel(which_ref, first_ref, *refs):
    heads, (out_ref, held_ref, sem) = refs[:-3], refs[-3:]
    width = held_ref.shape[1]
    depth = width // 2
    columns = first_ref.shape[1] - depth
    mine = pl.multiple_of(which_ref[0] * width, 128)
    other = pl.multiple_of((1 - which_ref[0]) * width, 128)
    copies = [
        pltpu.make_async_copy(
            first_ref.at[:, pl.ds(columns, depth)], out_ref.at[:, pl.ds(other, depth)], sem.at[0]
        )
    ]
    copies[0].start()
    dlogits = first_ref[:, :columns]
    for i in range(2):
        multiplied(dlogits, heads[i::2], held_ref, i * depth)
        copies.append(
            pltpu.make_async_copy(
                held_ref.at[:, pl.ds(i * depth, depth)],
                out_ref.at[:, pl.ds(pl.multiple_of(mine + i * depth, 128), depth)],
                sem.at[i + 1],
            )
        )
        copies[-1].start()
    for copy in copies:
        copy.wait()


def staying_gradient(which, first, heads):
    rows = first.shape[0]
    depth = heads[0].shape[1]
    columns = first.shape[1] - depth
    return pl.pallas_call(
        staying_kernel,
        out_shape=jax.ShapeDtypeStruct((rows, 4 * depth), BF16),
        in_specs=[SMEM] + [VMEM] * (1 + len(heads)),
        out_specs=HBM,
        scratch_shapes=[pltpu.VMEM((rows, 2 * depth), BF16), pltpu.SemaphoreType.DMA((3,))],
        compiler_params=PARAMS,
        cost_estimate=gradient_cost(rows, columns, 2 * depth),
        name="staying_gradient",
    )(which, first, *heads)


def placed_kernel(which_ref, second_ref, _, out_ref, sem):
    rows, depth = second_ref.shape
    start = pl.multiple_of((1 - which_ref[0]) * (2 * depth) + depth, 128)
    copies = []
    for i in range(4):
        part = pl.ds(i * (rows // 4), rows // 4)
        target = out_ref.at[part, pl.ds(start, depth)]
        copies.append(pltpu.make_async_copy(second_ref.at[part, :], target, sem.at[i]))
    for copy in copies:
        copy.start()
    for copy in copies:
        copy.wait()


def placed_beside(which, second, gradient):
    return pl.pallas_call(
        placed_kernel,
        out_shape=jax.ShapeDtypeStruct(gradient.shape, gradient.dtype),
        in_specs=[SMEM, VMEM, HBM],
        out_specs=HBM,
        scratch_shapes=[pltpu.SemaphoreType.DMA((4,))],
        input_output_aliases={2: 0},
        compiler_params=PARAMS,
        name="place_second",
    )(which, second, gradient)


def body(hidden, head_weight, tokens, rewards, group_ids):
    shards = lax.axis_size("vocab")
    which = (lax.axis_index("section") % 2).reshape(1)
    shard = lax.axis_index("vocab").reshape(1)
    near = [o for o in range(shards) if bin(o).count("1") <= 1]
    far = [o for o in range(shards) if bin(o).count("1") > 1]

    axes = ("vocab", "section")
    count = lax.axis_size(axes)
    own = jnp.stack([rewards, (group_ids + 1).astype(F32)] + [jnp.zeros_like(rewards)] * 6)
    beside = [(i, i + 1) for i in range(1, count - 1, 2)]
    outer = lax.ppermute(own, axes, beside + [(b, a) for a, b in beside])

    pieces = tuple(take(which, head_weight, 2))
    late_hidden, pieces, outer = lax.optimization_barrier((hidden, pieces, outer))
    (other_half,) = take(1 - which, late_hidden, 1)
    other_half, late_pieces = lax.optimization_barrier((other_half, pieces))
    heads = gathered(pieces, late_pieces, "vocab")
    partner_half = swapped(other_half, "section", 1)

    rows = turned(which, hidden, partner_half)
    mine, theirs = [], []
    for offsets, facts in ((near, (own,)), (far, ())):
        kept, sent = partial_scores(rows, [piece for o in offsets for piece in heads[o]], facts)
        mine.append(kept)
        theirs.append(swapped(sent, "section", 1))
    mine, theirs = in_order(mine, near + far, ()), in_order(theirs, near + far, (own.shape[0],))
    logits, logprob, entropy, dlogits = loss(
        shard, tokens[None, :], own, outer, mine, theirs, shards
    )
    pieces = [piece for pair in heads for piece in pair]
    first = first_message(dlogits, pieces[0::2])
    first_in = swapped(first, "section", 1)
    second_in = swapped(second_message(dlogits, first, pieces[1::2]), "section", 1)
    staying = staying_gradient(which, first_in, pieces)
    previous_grad = placed_beside(which, second_in, staying)
    return (logits, logprob[0], entropy[0], previous_grad)


def in_order(blocks, order, below):
    if order == sorted(order):
        return blocks
    extra = sum(below)
    first = blocks[0]
    kept = first.shape[0] - extra
    whole = jnp.concatenate([first[:kept], *blocks[1:]], axis=0)
    width = whole.shape[0] // len(order)
    parts = {offset: whole[i * width : (i + 1) * width] for i, offset in enumerate(order)}
    return [jnp.concatenate([parts[offset] for offset in sorted(order)] + [first[kept:]], axis=0)]


def solution(mesh):
    placed = (
        P(("seq", "vocab", "section"), None),
        P(("seq", "vocab"), None),
        P(("seq", "vocab", "section")),
        P(("seq", "vocab", "section")),
        P(("seq", "vocab", "section")),
    )
    return jax.shard_map(
        body,
        mesh=mesh,
        in_specs=placed,
        out_specs=(
            P(("seq", "vocab", "section"), None),
            P(("seq", "vocab", "section")),
            P(("seq", "vocab", "section")),
            P(("seq", "vocab", "section"), None),
        ),
        check_vma=False,
    )
```

```python
import functools

import jax
import jax.numpy as jnp
from jax import lax
from jax.experimental import pallas as pl
from jax.experimental.pallas import tpu as pltpu
from jax.sharding import PartitionSpec as P

F32, BF16 = jnp.float32, jnp.bfloat16
HBM = pl.BlockSpec(memory_space=pltpu.HBM)
ANY = pl.BlockSpec(memory_space=pl.ANY)
SMEM = pl.BlockSpec(memory_space=pltpu.SMEM)
VMEM = pl.BlockSpec(memory_space=pltpu.VMEM)
PARAMS = pltpu.CompilerParams(vmem_limit_bytes=4 * 1024 * 1024)
BELOW = 8


def swapped(value, axis, mask):
    pairs = [(source, source ^ mask) for source in range(lax.axis_size(axis))]
    return lax.ppermute(value, axis, pairs)


def gathered(first_wave, second_wave, axis):
    count = lax.axis_size(axis)
    masks = [1 << bit for bit in range((count - 1).bit_length())]
    uppers, lowers = {0: first_wave[0]}, {0: first_wave[1]}
    for mask in masks:
        early = mask == masks[0]
        uppers[mask] = swapped((first_wave if early else second_wave)[0], axis, mask)
    for mask in reversed(masks):
        early = mask == masks[-1]
        lowers[mask] = swapped((first_wave if early else second_wave)[1], axis, mask)
    for offset in sorted(range(1, count), key=lambda o: (bin(o).count("1"), o)):
        if offset in uppers:
            continue
        bits = [mask for mask in masks if offset & mask]
        uppers[offset] = swapped(uppers[offset ^ bits[-1]], axis, bits[-1])
        lowers[offset] = swapped(lowers[offset ^ bits[0]], axis, bits[0])
    return [(uppers[offset], lowers[offset]) for offset in range(count)]


def take_kernel(which_ref, value_ref, *refs):
    outs, sem = refs[:-1], refs[-1]
    width = outs[0].shape[1]
    start = which_ref[0] * width * len(outs)
    copies = []
    for i, out in enumerate(outs):
        source = value_ref.at[:, pl.ds(pl.multiple_of(start + i * width, 128), width)]
        copies.append(pltpu.make_async_copy(source, out, sem.at[i]))
    for copy in copies:
        copy.start()
    for copy in copies:
        copy.wait()


def take(which, value, pieces):
    rows, width = value.shape[0], value.shape[1] // 2 // pieces
    return pl.pallas_call(
        take_kernel,
        out_shape=[jax.ShapeDtypeStruct((rows, width), value.dtype)] * pieces,
        in_specs=[SMEM, ANY],
        out_specs=[ANY] * pieces,
        scratch_shapes=[pltpu.SemaphoreType.DMA((pieces,))],
        compiler_params=PARAMS,
        cost_estimate=pl.CostEstimate(
            flops=0, bytes_accessed=value.size * value.dtype.itemsize, transcendentals=0
        ),
        name="take_half",
    )(which, value)


def turned_kernel(which_ref, hidden_ref, partner_ref, out_ref):
    rows, width = partner_ref.shape
    block = 256
    for i in range(width // block):
        start = which_ref[0] * width + i * block
        own = hidden_ref[:, pl.ds(pl.multiple_of(start, 128), block)]
        out_ref[i * block : (i + 1) * block, :rows] = own.T
        part = slice(i * block, (i + 1) * block)
        out_ref[part, rows:] = partner_ref[:, part].T


def turned(which, hidden, partner_half):
    rows, width = partner_half.shape
    return pl.pallas_call(
        turned_kernel,
        out_shape=jax.ShapeDtypeStruct((width, 2 * rows), BF16),
        in_specs=[SMEM] + [VMEM] * 2,
        out_specs=VMEM,
        compiler_params=PARAMS,
        cost_estimate=pl.CostEstimate(
            flops=0, bytes_accessed=8 * rows * width, transcendentals=0
        ),
        name="turned_rows",
    )(which, hidden, partner_half)


def partial_kernel(facts, turned_ref, *refs):
    heads, (mine_ref, theirs_ref) = refs[facts:-2], refs[-2:]
    shard_rows, depth = heads[0].shape
    rows = mine_ref.shape[1]
    for i in range(len(heads) // 2):
        total = jnp.dot(heads[2 * i][...], turned_ref[:depth, :], preferred_element_type=F32)
        total += jnp.dot(heads[2 * i + 1][...], turned_ref[depth:, :], preferred_element_type=F32)
        mine_ref[i * shard_rows : (i + 1) * shard_rows, :] = total[:, :rows]
        theirs_ref[i * shard_rows : (i + 1) * shard_rows, :] = total[:, rows:]
    if facts:
        below = theirs_ref.shape[0] - mine_ref.shape[0]
        theirs_ref[mine_ref.shape[0] :, :] = jnp.zeros((below, rows), F32)
        theirs_ref[pl.ds(mine_ref.shape[0], refs[0].shape[0]), :] = refs[0][...]


def partial_scores(turned_rows, heads, facts=()):
    width, rows = turned_rows.shape
    columns = sum(head.shape[0] for head in heads) // 2
    below = BELOW * len(facts)
    return pl.pallas_call(
        functools.partial(partial_kernel, len(facts)),
        out_shape=[
            jax.ShapeDtypeStruct((columns, rows // 2), F32),
            jax.ShapeDtypeStruct((columns + below, rows // 2), F32),
        ],
        in_specs=[VMEM] * (1 + len(facts) + len(heads)),
        out_specs=[VMEM, VMEM],
        compiler_params=PARAMS,
        cost_estimate=pl.CostEstimate(
            flops=2 * rows * columns * width,
            bytes_accessed=2 * width * (rows + columns),
            transcendentals=0,
        ),
        name="partial_scores",
    )(turned_rows, *facts, *heads)


def advantage_of(own, outer, partner):
    rows = own.shape[1]
    eye = lax.broadcasted_iota(jnp.int32, (rows, rows), 0) == lax.broadcasted_iota(
        jnp.int32, (rows, rows), 1
    )
    groups = jnp.sum(jnp.where(eye, own[1:2, :], 0.0), axis=1, keepdims=True)
    sums, counts = jnp.zeros((rows, 1), F32), jnp.zeros((rows, 1), F32)
    for facts in (own, outer, partner):
        member = facts[1:2, :] == groups
        sums += jnp.sum(jnp.where(member, facts[0:1, :], 0.0), axis=1, keepdims=True)
        counts += jnp.sum(jnp.where(member, 1.0, 0.0), axis=1, keepdims=True)
    return own[0:1, :] - jnp.sum(jnp.where(eye, sums / counts, 0.0), axis=0, keepdims=True)


def loss_kernel(parts, shards, shard_ref, tokens_ref, own_ref, outer_ref, *refs):
    mine, theirs = refs[:parts], refs[parts : 2 * parts]
    logits_ref, logprob_ref, entropy_ref, dlogits_ref = refs[2 * parts :]
    shard = shard_ref[0]
    rows, columns = dlogits_ref.shape
    shard_rows = columns // shards

    lengths = [ref.shape[0] for ref in mine]
    partner = theirs[0][lengths[0] :, :]
    advantage = advantage_of(own_ref[...], outer_ref[...], partner)
    scores = jnp.concatenate(
        [a[...] + b[:n, :] for a, b, n in zip(mine, theirs, lengths)], axis=0
    )
    tokens = tokens_ref[...]
    relative = ((tokens // shard_rows) ^ shard) * shard_rows + tokens % shard_rows
    chosen = lax.broadcasted_iota(jnp.int32, (columns, rows), 0) == relative
    row_max = jnp.max(scores, axis=0, keepdims=True)
    unnormed = jnp.exp(scores - row_max)
    denominator = jnp.sum(unnormed, axis=0, keepdims=True)
    probabilities = unnormed / denominator
    dlogits = advantage * (probabilities - jnp.where(chosen, 1.0, 0.0))
    for i in range(shards):
        block = slice(i * shard_rows, (i + 1) * shard_rows)
        dlogits_ref[:, block] = dlogits[block, :].T.astype(BF16)
        place = pl.multiple_of((shard ^ i) * shard_rows, 128)
        logits_ref[:, pl.ds(place, shard_rows)] = scores[block, :].T.astype(BF16)
    log_total = row_max + jnp.log(denominator)
    picked = jnp.sum(jnp.where(chosen, scores, 0.0), axis=0, keepdims=True)
    logprob_ref[...] = picked - log_total
    entropy_ref[...] = log_total - jnp.sum(probabilities * scores, axis=0, keepdims=True)


def loss(shard, tokens, own, outer, mine, theirs, shards):
    rows = tokens.shape[1]
    columns = sum(part.shape[0] for part in mine)
    flat = jax.ShapeDtypeStruct((1, rows), F32)
    wide = jax.ShapeDtypeStruct((rows, columns), BF16)
    return pl.pallas_call(
        functools.partial(loss_kernel, len(mine), shards),
        out_shape=[wide, flat, flat, wide],
        in_specs=[SMEM] + [VMEM] * (3 + 2 * len(mine)),
        out_specs=[VMEM] * 4,
        compiler_params=pltpu.CompilerParams(vmem_limit_bytes=2 * 1024**2 + 32 * rows * columns),
        cost_estimate=pl.CostEstimate(
            flops=10 * rows * columns,
            bytes_accessed=12 * rows * columns,
            transcendentals=rows * columns,
        ),
        name="loss",
    )(shard, tokens, own, outer, *mine, *theirs)


def multiplied(dlogits, heads, out_ref, start):
    block = 256
    for j in range(heads[0].shape[1] // block):
        part = slice(j * block, (j + 1) * block)
        head = jnp.concatenate([ref[:, part] for ref in heads], axis=0)
        product = jnp.dot(dlogits, head, preferred_element_type=F32)
        out_ref[:, start + j * block : start + (j + 1) * block] = product.astype(BF16)


def gradient_cost(rows, columns, width):
    return pl.CostEstimate(
        flops=2 * rows * columns * width,
        bytes_accessed=2 * width * (rows + columns),
        transcendentals=0,
    )


def first_kernel(dlogits_ref, *refs):
    heads, out_ref = refs[:-1], refs[-1]
    columns = dlogits_ref.shape[1]
    out_ref[:, :columns] = dlogits_ref[...]
    multiplied(dlogits_ref[...], heads, out_ref, columns)


def first_message(dlogits, heads):
    rows, columns = dlogits.shape
    width = heads[0].shape[1]
    return pl.pallas_call(
        first_kernel,
        out_shape=jax.ShapeDtypeStruct((rows, columns + width), BF16),
        in_specs=[VMEM] * (1 + len(heads)),
        out_specs=VMEM,
        compiler_params=PARAMS,
        cost_estimate=gradient_cost(rows, columns, width),
        name="first_message",
    )(dlogits, *heads)


def second_kernel(dlogits_ref, _, *refs):
    multiplied(dlogits_ref[...], refs[:-1], refs[-1], 0)


def second_message(dlogits, first, heads):
    rows, columns = dlogits.shape
    width = heads[0].shape[1]
    return pl.pallas_call(
        second_kernel,
        out_shape=jax.ShapeDtypeStruct((rows, width), BF16),
        in_specs=[VMEM, ANY] + [VMEM] * len(heads),
        out_specs=VMEM,
        compiler_params=PARAMS,
        cost_estimate=gradient_cost(rows, columns, width),
        name="second_message",
    )(dlogits, first, *heads)


def staying_kernel(which_ref, first_ref, *refs):
    heads, (out_ref, held_ref, sem) = refs[:-3], refs[-3:]
    width = held_ref.shape[1]
    depth = width // 2
    columns = first_ref.shape[1] - depth
    mine = pl.multiple_of(which_ref[0] * width, 128)
    other = pl.multiple_of((1 - which_ref[0]) * width, 128)
    copies = [
        pltpu.make_async_copy(
            first_ref.at[:, pl.ds(columns, depth)], out_ref.at[:, pl.ds(other, depth)], sem.at[0]
        )
    ]
    copies[0].start()
    dlogits = first_ref[:, :columns]
    for i in range(2):
        multiplied(dlogits, heads[i::2], held_ref, i * depth)
        copies.append(
            pltpu.make_async_copy(
                held_ref.at[:, pl.ds(i * depth, depth)],
                out_ref.at[:, pl.ds(pl.multiple_of(mine + i * depth, 128), depth)],
                sem.at[i + 1],
            )
        )
        copies[-1].start()
    for copy in copies:
        copy.wait()


def staying_gradient(which, first, heads):
    rows = first.shape[0]
    depth = heads[0].shape[1]
    columns = first.shape[1] - depth
    return pl.pallas_call(
        staying_kernel,
        out_shape=jax.ShapeDtypeStruct((rows, 4 * depth), BF16),
        in_specs=[SMEM] + [VMEM] * (1 + len(heads)),
        out_specs=HBM,
        scratch_shapes=[pltpu.VMEM((rows, 2 * depth), BF16), pltpu.SemaphoreType.DMA((3,))],
        compiler_params=PARAMS,
        cost_estimate=gradient_cost(rows, columns, 2 * depth),
        name="staying_gradient",
    )(which, first, *heads)


def placed_kernel(which_ref, second_ref, _, out_ref, sem):
    rows, depth = second_ref.shape
    start = pl.multiple_of((1 - which_ref[0]) * (2 * depth) + depth, 128)
    copies = []
    for i in range(4):
        part = pl.ds(i * (rows // 4), rows // 4)
        target = out_ref.at[part, pl.ds(start, depth)]
        copies.append(pltpu.make_async_copy(second_ref.at[part, :], target, sem.at[i]))
    for copy in copies:
        copy.start()
    for copy in copies:
        copy.wait()


def placed_beside(which, second, gradient):
    return pl.pallas_call(
        placed_kernel,
        out_shape=jax.ShapeDtypeStruct(gradient.shape, gradient.dtype),
        in_specs=[SMEM, VMEM, HBM],
        out_specs=HBM,
        scratch_shapes=[pltpu.SemaphoreType.DMA((4,))],
        input_output_aliases={2: 0},
        compiler_params=PARAMS,
        name="place_second",
    )(which, second, gradient)


def body(hidden, head_weight, tokens, rewards, group_ids):
    shards = lax.axis_size("vocab")
    which = (lax.axis_index("section") % 2).reshape(1)
    shard = lax.axis_index("vocab").reshape(1)
    near = [o for o in range(shards) if bin(o).count("1") <= 1]
    far = [o for o in range(shards) if bin(o).count("1") > 1]

    axes = ("vocab", "section")
    count = lax.axis_size(axes)
    own = jnp.stack([rewards, (group_ids + 1).astype(F32)])
    beside = [(i, i + 1) for i in range(1, count - 1, 2)]
    outer = lax.ppermute(own, axes, beside + [(b, a) for a, b in beside])

    pieces = tuple(take(which, head_weight, 2))
    late_hidden, _ = lax.optimization_barrier((hidden, pieces))
    (other_half,) = take(1 - which, late_hidden, 1)
    other_half, late_pieces = lax.optimization_barrier((other_half, pieces))
    heads = gathered(pieces, late_pieces, "vocab")
    partner_half = swapped(other_half, "section", 1)

    rows = turned(which, hidden, partner_half)
    mine, theirs = [], []
    for offsets, facts in ((near, (own,)), (far, ())):
        if not facts:
            rows, outer = lax.optimization_barrier((rows, outer))
        kept, sent = partial_scores(rows, [piece for o in offsets for piece in heads[o]], facts)
        mine.append(kept)
        theirs.append(swapped(sent, "section", 1))
    mine, theirs = in_order(mine, near + far, 0), in_order(theirs, near + far, BELOW)
    logits, logprob, entropy, dlogits = loss(
        shard, tokens[None, :], own, outer, mine, theirs, shards
    )
    pieces = [piece for pair in heads for piece in pair]
    first = first_message(dlogits, pieces[0::2])
    first_in = swapped(first, "section", 1)
    second_in = swapped(second_message(dlogits, first, pieces[1::2]), "section", 1)
    staying = staying_gradient(which, first_in, pieces)
    previous_grad = placed_beside(which, second_in, staying)
    return (logits, logprob[0], entropy[0], previous_grad)


def in_order(blocks, order, below):
    if order == sorted(order):
        return blocks
    first = blocks[0]
    kept = first.shape[0] - below
    whole = jnp.concatenate([first[:kept], *blocks[1:]], axis=0)
    width = whole.shape[0] // len(order)
    parts = {offset: whole[i * width : (i + 1) * width] for i, offset in enumerate(order)}
    return [jnp.concatenate([parts[offset] for offset in sorted(order)] + [first[kept:]], axis=0)]


def solution(mesh):
    placed = (
        P(("seq", "vocab", "section"), None),
        P(("seq", "vocab"), None),
        P(("seq", "vocab", "section")),
        P(("seq", "vocab", "section")),
        P(("seq", "vocab", "section")),
    )
    return jax.shard_map(
        body,
        mesh=mesh,
        in_specs=placed,
        out_specs=(
            P(("seq", "vocab", "section"), None),
            P(("seq", "vocab", "section")),
            P(("seq", "vocab", "section")),
            P(("seq", "vocab", "section"), None),
        ),
        check_vma=False,
    )
```

```python
import functools

import jax
import jax.numpy as jnp
from jax import lax
from jax.experimental import pallas as pl
from jax.experimental.pallas import tpu as pltpu
from jax.sharding import PartitionSpec as P

F32, BF16 = jnp.float32, jnp.bfloat16
HBM = pl.BlockSpec(memory_space=pltpu.HBM)
ANY = pl.BlockSpec(memory_space=pl.ANY)
SMEM = pl.BlockSpec(memory_space=pltpu.SMEM)
VMEM = pl.BlockSpec(memory_space=pltpu.VMEM)
PARAMS = pltpu.CompilerParams(vmem_limit_bytes=4 * 1024 * 1024)
BELOW = 8


def swapped(value, axis, mask):
    pairs = [(source, source ^ mask) for source in range(lax.axis_size(axis))]
    return lax.ppermute(value, axis, pairs)


def gathered(first_wave, second_wave, axis):
    count = lax.axis_size(axis)
    masks = [1 << bit for bit in range((count - 1).bit_length())]
    uppers, lowers = {0: first_wave[0]}, {0: first_wave[1]}
    for mask in masks:
        early = mask == masks[0]
        uppers[mask] = swapped((first_wave if early else second_wave)[0], axis, mask)
    for mask in reversed(masks):
        early = mask == masks[-1]
        lowers[mask] = swapped((first_wave if early else second_wave)[1], axis, mask)
    for offset in sorted(range(1, count), key=lambda o: (bin(o).count("1"), o)):
        if offset in uppers:
            continue
        bits = [mask for mask in masks if offset & mask]
        uppers[offset] = swapped(uppers[offset ^ bits[-1]], axis, bits[-1])
        lowers[offset] = swapped(lowers[offset ^ bits[0]], axis, bits[0])
    return [(uppers[offset], lowers[offset]) for offset in range(count)]


def take_kernel(which_ref, value_ref, *refs):
    outs, sem = refs[:-1], refs[-1]
    width = outs[0].shape[1]
    start = which_ref[0] * width * len(outs)
    copies = []
    for i, out in enumerate(outs):
        source = value_ref.at[:, pl.ds(pl.multiple_of(start + i * width, 128), width)]
        copies.append(pltpu.make_async_copy(source, out, sem.at[i]))
    for copy in copies:
        copy.start()
    for copy in copies:
        copy.wait()


def take(which, value, pieces):
    rows, width = value.shape[0], value.shape[1] // 2 // pieces
    return pl.pallas_call(
        take_kernel,
        out_shape=[jax.ShapeDtypeStruct((rows, width), value.dtype)] * pieces,
        in_specs=[SMEM, ANY],
        out_specs=[ANY] * pieces,
        scratch_shapes=[pltpu.SemaphoreType.DMA((pieces,))],
        compiler_params=PARAMS,
        cost_estimate=pl.CostEstimate(
            flops=0, bytes_accessed=value.size * value.dtype.itemsize, transcendentals=0
        ),
        name="take_half",
    )(which, value)


def turned_kernel(which_ref, hidden_ref, partner_ref, out_ref):
    rows, width = partner_ref.shape
    block = 256
    for i in range(width // block):
        start = which_ref[0] * width + i * block
        own = hidden_ref[:, pl.ds(pl.multiple_of(start, 128), block)]
        out_ref[i * block : (i + 1) * block, :rows] = own.T
        part = slice(i * block, (i + 1) * block)
        out_ref[part, rows:] = partner_ref[:, part].T


def turned(which, hidden, partner_half):
    rows, width = partner_half.shape
    return pl.pallas_call(
        turned_kernel,
        out_shape=jax.ShapeDtypeStruct((width, 2 * rows), BF16),
        in_specs=[SMEM] + [VMEM] * 2,
        out_specs=VMEM,
        compiler_params=PARAMS,
        cost_estimate=pl.CostEstimate(
            flops=0, bytes_accessed=8 * rows * width, transcendentals=0
        ),
        name="turned_rows",
    )(which, hidden, partner_half)


def partial_kernel(facts, count, turned_ref, *refs):
    heads, (mine_ref, theirs_ref) = refs[facts : facts + count], refs[facts + count :][:2]
    for held, ref in zip(refs[facts + count + 2 :], heads):
        held[...] = ref[...]
    shard_rows, depth = heads[0].shape
    rows = mine_ref.shape[1]
    for i in range(len(heads) // 2):
        total = jnp.dot(heads[2 * i][...], turned_ref[:depth, :], preferred_element_type=F32)
        total += jnp.dot(heads[2 * i + 1][...], turned_ref[depth:, :], preferred_element_type=F32)
        mine_ref[i * shard_rows : (i + 1) * shard_rows, :] = total[:, :rows]
        theirs_ref[i * shard_rows : (i + 1) * shard_rows, :] = total[:, rows:]
    if facts:
        below = theirs_ref.shape[0] - mine_ref.shape[0]
        theirs_ref[mine_ref.shape[0] :, :] = jnp.zeros((below, rows), F32)
        theirs_ref[pl.ds(mine_ref.shape[0], refs[0].shape[0]), :] = refs[0][...]


def partial_scores(turned_rows, heads, facts=()):
    width, rows = turned_rows.shape
    columns = sum(head.shape[0] for head in heads) // 2
    below = BELOW * len(facts)
    return pl.pallas_call(
        functools.partial(partial_kernel, len(facts), len(heads)),
        out_shape=[
            jax.ShapeDtypeStruct((columns, rows // 2), F32),
            jax.ShapeDtypeStruct((columns + below, rows // 2), F32),
            *[jax.ShapeDtypeStruct(head.shape, head.dtype) for head in heads if not facts],
        ],
        in_specs=[VMEM] * (1 + len(facts) + len(heads)),
        out_specs=[VMEM] * (2 if facts else 2 + len(heads)),
        compiler_params=PARAMS,
        cost_estimate=pl.CostEstimate(
            flops=2 * rows * columns * width,
            bytes_accessed=2 * width * (rows + columns),
            transcendentals=0,
        ),
        name="partial_scores",
    )(turned_rows, *facts, *heads)


def advantage_of(own, outer, partner):
    rows = own.shape[1]
    eye = lax.broadcasted_iota(jnp.int32, (rows, rows), 0) == lax.broadcasted_iota(
        jnp.int32, (rows, rows), 1
    )
    groups = jnp.sum(jnp.where(eye, own[1:2, :], 0.0), axis=1, keepdims=True)
    sums, counts = jnp.zeros((rows, 1), F32), jnp.zeros((rows, 1), F32)
    for facts in (own, outer, partner):
        member = facts[1:2, :] == groups
        sums += jnp.sum(jnp.where(member, facts[0:1, :], 0.0), axis=1, keepdims=True)
        counts += jnp.sum(jnp.where(member, 1.0, 0.0), axis=1, keepdims=True)
    return own[0:1, :] - jnp.sum(jnp.where(eye, sums / counts, 0.0), axis=0, keepdims=True)


def loss_kernel(parts, shards, shard_ref, tokens_ref, own_ref, outer_ref, *refs):
    mine, theirs = refs[:parts], refs[parts : 2 * parts]
    logits_ref, logprob_ref, entropy_ref, dlogits_ref = refs[2 * parts :]
    shard = shard_ref[0]
    rows, columns = dlogits_ref.shape
    shard_rows = columns // shards

    lengths = [ref.shape[0] for ref in mine]
    partner = theirs[0][lengths[0] :, :]
    advantage = advantage_of(own_ref[...], outer_ref[...], partner)
    scores = jnp.concatenate(
        [a[...] + b[:n, :] for a, b, n in zip(mine, theirs, lengths)], axis=0
    )
    tokens = tokens_ref[...]
    relative = ((tokens // shard_rows) ^ shard) * shard_rows + tokens % shard_rows
    chosen = lax.broadcasted_iota(jnp.int32, (columns, rows), 0) == relative
    row_max = jnp.max(scores, axis=0, keepdims=True)
    unnormed = jnp.exp(scores - row_max)
    denominator = jnp.sum(unnormed, axis=0, keepdims=True)
    probabilities = unnormed / denominator
    dlogits = advantage * (probabilities - jnp.where(chosen, 1.0, 0.0))
    for i in range(shards):
        block = slice(i * shard_rows, (i + 1) * shard_rows)
        dlogits_ref[:, block] = dlogits[block, :].T.astype(BF16)
        place = pl.multiple_of((shard ^ i) * shard_rows, 128)
        logits_ref[:, pl.ds(place, shard_rows)] = scores[block, :].T.astype(BF16)
    log_total = row_max + jnp.log(denominator)
    picked = jnp.sum(jnp.where(chosen, scores, 0.0), axis=0, keepdims=True)
    logprob_ref[...] = picked - log_total
    entropy_ref[...] = log_total - jnp.sum(probabilities * scores, axis=0, keepdims=True)


def loss(shard, tokens, own, outer, mine, theirs, shards):
    rows = tokens.shape[1]
    columns = sum(part.shape[0] for part in mine)
    flat = jax.ShapeDtypeStruct((1, rows), F32)
    wide = jax.ShapeDtypeStruct((rows, columns), BF16)
    return pl.pallas_call(
        functools.partial(loss_kernel, len(mine), shards),
        out_shape=[wide, flat, flat, wide],
        in_specs=[SMEM] + [VMEM] * (3 + 2 * len(mine)),
        out_specs=[VMEM] * 4,
        compiler_params=pltpu.CompilerParams(vmem_limit_bytes=2 * 1024**2 + 32 * rows * columns),
        cost_estimate=pl.CostEstimate(
            flops=10 * rows * columns,
            bytes_accessed=12 * rows * columns,
            transcendentals=rows * columns,
        ),
        name="loss",
    )(shard, tokens, own, outer, *mine, *theirs)


def multiplied(dlogits, heads, out_ref, start):
    block = 256
    for j in range(heads[0].shape[1] // block):
        part = slice(j * block, (j + 1) * block)
        head = jnp.concatenate([ref[:, part] for ref in heads], axis=0)
        product = jnp.dot(dlogits, head, preferred_element_type=F32)
        out_ref[:, start + j * block : start + (j + 1) * block] = product.astype(BF16)


def gradient_cost(rows, columns, width):
    return pl.CostEstimate(
        flops=2 * rows * columns * width,
        bytes_accessed=2 * width * (rows + columns),
        transcendentals=0,
    )


def first_kernel(dlogits_ref, *refs):
    heads, out_ref = refs[:-1], refs[-1]
    columns = dlogits_ref.shape[1]
    out_ref[:, :columns] = dlogits_ref[...]
    multiplied(dlogits_ref[...], heads, out_ref, columns)


def first_message(dlogits, heads):
    rows, columns = dlogits.shape
    width = heads[0].shape[1]
    return pl.pallas_call(
        first_kernel,
        out_shape=jax.ShapeDtypeStruct((rows, columns + width), BF16),
        in_specs=[VMEM] * (1 + len(heads)),
        out_specs=VMEM,
        compiler_params=PARAMS,
        cost_estimate=gradient_cost(rows, columns, width),
        name="first_message",
    )(dlogits, *heads)


def second_kernel(dlogits_ref, _, *refs):
    multiplied(dlogits_ref[...], refs[:-1], refs[-1], 0)


def second_message(dlogits, first, heads):
    rows, columns = dlogits.shape
    width = heads[0].shape[1]
    return pl.pallas_call(
        second_kernel,
        out_shape=jax.ShapeDtypeStruct((rows, width), BF16),
        in_specs=[VMEM, ANY] + [VMEM] * len(heads),
        out_specs=VMEM,
        compiler_params=PARAMS,
        cost_estimate=gradient_cost(rows, columns, width),
        name="second_message",
    )(dlogits, first, *heads)


def staying_kernel(which_ref, first_ref, *refs):
    heads, (out_ref, held_ref, sem) = refs[:-3], refs[-3:]
    width = held_ref.shape[1]
    depth = width // 2
    columns = first_ref.shape[1] - depth
    mine = pl.multiple_of(which_ref[0] * width, 128)
    other = pl.multiple_of((1 - which_ref[0]) * width, 128)
    copies = [
        pltpu.make_async_copy(
            first_ref.at[:, pl.ds(columns, depth)], out_ref.at[:, pl.ds(other, depth)], sem.at[0]
        )
    ]
    copies[0].start()
    dlogits = first_ref[:, :columns]
    for i in range(2):
        multiplied(dlogits, heads[i::2], held_ref, i * depth)
        copies.append(
            pltpu.make_async_copy(
                held_ref.at[:, pl.ds(i * depth, depth)],
                out_ref.at[:, pl.ds(pl.multiple_of(mine + i * depth, 128), depth)],
                sem.at[i + 1],
            )
        )
        copies[-1].start()
    for copy in copies:
        copy.wait()


def staying_gradient(which, first, heads):
    rows = first.shape[0]
    depth = heads[0].shape[1]
    columns = first.shape[1] - depth
    return pl.pallas_call(
        staying_kernel,
        out_shape=jax.ShapeDtypeStruct((rows, 4 * depth), BF16),
        in_specs=[SMEM] + [VMEM] * (1 + len(heads)),
        out_specs=HBM,
        scratch_shapes=[pltpu.VMEM((rows, 2 * depth), BF16), pltpu.SemaphoreType.DMA((3,))],
        compiler_params=PARAMS,
        cost_estimate=gradient_cost(rows, columns, 2 * depth),
        name="staying_gradient",
    )(which, first, *heads)


def placed_kernel(which_ref, second_ref, _, out_ref, sem):
    rows, depth = second_ref.shape
    start = pl.multiple_of((1 - which_ref[0]) * (2 * depth) + depth, 128)
    copies = []
    for i in range(4):
        part = pl.ds(i * (rows // 4), rows // 4)
        target = out_ref.at[part, pl.ds(start, depth)]
        copies.append(pltpu.make_async_copy(second_ref.at[part, :], target, sem.at[i]))
    for copy in copies:
        copy.start()
    for copy in copies:
        copy.wait()


def placed_beside(which, second, gradient):
    return pl.pallas_call(
        placed_kernel,
        out_shape=jax.ShapeDtypeStruct(gradient.shape, gradient.dtype),
        in_specs=[SMEM, VMEM, HBM],
        out_specs=HBM,
        scratch_shapes=[pltpu.SemaphoreType.DMA((4,))],
        input_output_aliases={2: 0},
        compiler_params=PARAMS,
        name="place_second",
    )(which, second, gradient)


def body(hidden, head_weight, tokens, rewards, group_ids):
    shards = lax.axis_size("vocab")
    which = (lax.axis_index("section") % 2).reshape(1)
    shard = lax.axis_index("vocab").reshape(1)
    near = [o for o in range(shards) if bin(o).count("1") <= 1]
    far = [o for o in range(shards) if bin(o).count("1") > 1]

    axes = ("vocab", "section")
    count = lax.axis_size(axes)
    own = jnp.stack([rewards, (group_ids + 1).astype(F32)])
    beside = [(i, i + 1) for i in range(1, count - 1, 2)]
    pieces = tuple(take(which, head_weight, 2))
    late_hidden, _ = lax.optimization_barrier((hidden, pieces))
    (other_half,) = take(1 - which, late_hidden, 1)
    other_half, late_pieces = lax.optimization_barrier((other_half, pieces))
    heads = gathered(pieces, late_pieces, "vocab")
    partner_half = swapped(other_half, "section", 1)

    late_own, _ = lax.optimization_barrier((own, (heads[near[1]][1], heads[near[-1]][0])))
    outer = lax.ppermute(late_own, axes, beside + [(b, a) for a, b in beside])
    partner_half, outer = lax.optimization_barrier((partner_half, outer))
    rows = turned(which, hidden, partner_half)
    mine, theirs = [], []
    for offsets, facts in ((near, (own,)), (far, ())):
        pieces = [piece for o in offsets for piece in heads[o]]
        kept, sent, *again = partial_scores(rows, pieces, facts)
        mine.append(kept)
        theirs.append(swapped(sent, "section", 1))
    mine, theirs = in_order(mine, near + far, 0), in_order(theirs, near + far, BELOW)
    logits, logprob, entropy, dlogits = loss(
        shard, tokens[None, :], own, outer, mine, theirs, shards
    )
    for i, offset in enumerate(far):
        heads[offset] = again[2 * i : 2 * i + 2]
    pieces = [piece for pair in heads for piece in pair]
    first = first_message(dlogits, pieces[0::2])
    first_in = swapped(first, "section", 1)
    second_in = swapped(second_message(dlogits, first, pieces[1::2]), "section", 1)
    staying = staying_gradient(which, first_in, pieces)
    previous_grad = placed_beside(which, second_in, staying)
    return (logits, logprob[0], entropy[0], previous_grad)


def in_order(blocks, order, below):
    if order == sorted(order):
        return blocks
    first = blocks[0]
    kept = first.shape[0] - below
    whole = jnp.concatenate([first[:kept], *blocks[1:]], axis=0)
    width = whole.shape[0] // len(order)
    parts = {offset: whole[i * width : (i + 1) * width] for i, offset in enumerate(order)}
    return [jnp.concatenate([parts[offset] for offset in sorted(order)] + [first[kept:]], axis=0)]


def solution(mesh):
    placed = (
        P(("seq", "vocab", "section"), None),
        P(("seq", "vocab"), None),
        P(("seq", "vocab", "section")),
        P(("seq", "vocab", "section")),
        P(("seq", "vocab", "section")),
    )
    return jax.shard_map(
        body,
        mesh=mesh,
        in_specs=placed,
        out_specs=(
            P(("seq", "vocab", "section"), None),
            P(("seq", "vocab", "section")),
            P(("seq", "vocab", "section")),
            P(("seq", "vocab", "section"), None),
        ),
        check_vma=False,
    )
```

```python
import functools

import jax
import jax.numpy as jnp
from jax import lax
from jax.experimental import pallas as pl
from jax.experimental.pallas import tpu as pltpu
from jax.sharding import PartitionSpec as P

F32, BF16 = jnp.float32, jnp.bfloat16
HBM = pl.BlockSpec(memory_space=pltpu.HBM)
ANY = pl.BlockSpec(memory_space=pl.ANY)
SMEM = pl.BlockSpec(memory_space=pltpu.SMEM)
VMEM = pl.BlockSpec(memory_space=pltpu.VMEM)
PARAMS = pltpu.CompilerParams(vmem_limit_bytes=4 * 1024 * 1024)
BELOW = 8


def swapped(value, axis, mask):
    pairs = [(source, source ^ mask) for source in range(lax.axis_size(axis))]
    return lax.ppermute(value, axis, pairs)


def gathered(first_wave, second_wave, axis):
    count = lax.axis_size(axis)
    masks = [1 << bit for bit in range((count - 1).bit_length())]
    uppers, lowers = {0: first_wave[0]}, {0: first_wave[1]}
    for mask in masks:
        early = mask == masks[0]
        uppers[mask] = swapped((first_wave if early else second_wave)[0], axis, mask)
    for mask in reversed(masks):
        early = mask == masks[-1]
        lowers[mask] = swapped((first_wave if early else second_wave)[1], axis, mask)
    for offset in sorted(range(1, count), key=lambda o: (bin(o).count("1"), o)):
        if offset in uppers:
            continue
        bits = [mask for mask in masks if offset & mask]
        uppers[offset] = swapped(uppers[offset ^ bits[-1]], axis, bits[-1])
        lowers[offset] = swapped(lowers[offset ^ bits[0]], axis, bits[0])
    return [(uppers[offset], lowers[offset]) for offset in range(count)]


def take_kernel(which_ref, value_ref, *refs):
    outs, sem = refs[:-1], refs[-1]
    width = outs[0].shape[1]
    start = which_ref[0] * width * len(outs)
    copies = []
    for i, out in enumerate(outs):
        source = value_ref.at[:, pl.ds(pl.multiple_of(start + i * width, 128), width)]
        copies.append(pltpu.make_async_copy(source, out, sem.at[i]))
    for copy in copies:
        copy.start()
    for copy in copies:
        copy.wait()


def take(which, value, pieces):
    rows, width = value.shape[0], value.shape[1] // 2 // pieces
    return pl.pallas_call(
        take_kernel,
        out_shape=[jax.ShapeDtypeStruct((rows, width), value.dtype)] * pieces,
        in_specs=[SMEM, ANY],
        out_specs=[ANY] * pieces,
        scratch_shapes=[pltpu.SemaphoreType.DMA((pieces,))],
        compiler_params=PARAMS,
        cost_estimate=pl.CostEstimate(
            flops=0, bytes_accessed=value.size * value.dtype.itemsize, transcendentals=0
        ),
        name="take_half",
    )(which, value)


def turned_kernel(which_ref, hidden_ref, partner_ref, out_ref):
    rows, width = partner_ref.shape
    block = 256
    for i in range(width // block):
        start = which_ref[0] * width + i * block
        own = hidden_ref[:, pl.ds(pl.multiple_of(start, 128), block)]
        out_ref[i * block : (i + 1) * block, :rows] = own.T
        part = slice(i * block, (i + 1) * block)
        out_ref[part, rows:] = partner_ref[:, part].T


def turned(which, hidden, partner_half):
    rows, width = partner_half.shape
    return pl.pallas_call(
        turned_kernel,
        out_shape=jax.ShapeDtypeStruct((width, 2 * rows), BF16),
        in_specs=[SMEM] + [VMEM] * 2,
        out_specs=VMEM,
        compiler_params=PARAMS,
        cost_estimate=pl.CostEstimate(
            flops=0, bytes_accessed=8 * rows * width, transcendentals=0
        ),
        name="turned_rows",
    )(which, hidden, partner_half)


def partial_kernel(facts, count, turned_ref, *refs):
    heads, (mine_ref, theirs_ref) = refs[facts : facts + count], refs[facts + count :][:2]
    for held, ref in zip(refs[facts + count + 2 :], heads):
        held[...] = ref[...]
    shard_rows, depth = heads[0].shape
    rows = mine_ref.shape[1]
    for i in range(len(heads) // 2):
        total = jnp.dot(heads[2 * i][...], turned_ref[:depth, :], preferred_element_type=F32)
        total += jnp.dot(heads[2 * i + 1][...], turned_ref[depth:, :], preferred_element_type=F32)
        mine_ref[i * shard_rows : (i + 1) * shard_rows, :] = total[:, :rows]
        theirs_ref[i * shard_rows : (i + 1) * shard_rows, :] = total[:, rows:]
    if facts:
        below = theirs_ref.shape[0] - mine_ref.shape[0]
        theirs_ref[mine_ref.shape[0] :, :] = jnp.zeros((below, rows), F32)
        theirs_ref[pl.ds(mine_ref.shape[0], refs[0].shape[0]), :] = refs[0][...]


def partial_scores(turned_rows, heads, facts=()):
    width, rows = turned_rows.shape
    columns = sum(head.shape[0] for head in heads) // 2
    below = BELOW * len(facts)
    return pl.pallas_call(
        functools.partial(partial_kernel, len(facts), len(heads)),
        out_shape=[
            jax.ShapeDtypeStruct((columns, rows // 2), F32),
            jax.ShapeDtypeStruct((columns + below, rows // 2), F32),
            *[jax.ShapeDtypeStruct(head.shape, head.dtype) for head in heads if not facts],
        ],
        in_specs=[VMEM] * (1 + len(facts) + len(heads)),
        out_specs=[VMEM] * (2 if facts else 2 + len(heads)),
        compiler_params=PARAMS,
        cost_estimate=pl.CostEstimate(
            flops=2 * rows * columns * width,
            bytes_accessed=2 * width * (rows + columns),
            transcendentals=0,
        ),
        name="partial_scores",
    )(turned_rows, *facts, *heads)


def advantage_kernel(partner_ref, own_ref, outer_ref, out_ref):
    rows = own_ref.shape[1]
    partner = partner_ref[partner_ref.shape[0] - BELOW :, :]
    eye = lax.broadcasted_iota(jnp.int32, (rows, rows), 0) == lax.broadcasted_iota(
        jnp.int32, (rows, rows), 1
    )

    def upright(row):
        return jnp.sum(jnp.where(eye, row, 0.0), axis=1, keepdims=True)

    groups = upright(partner[1:2, :])
    sums, counts = jnp.zeros((rows, 1), F32), jnp.zeros((rows, 1), F32)
    for facts in (partner, own_ref[...], outer_ref[...]):
        member = facts[1:2, :] == groups
        sums += jnp.sum(jnp.where(member, facts[0:1, :], 0.0), axis=1, keepdims=True)
        counts += jnp.sum(jnp.where(member, 1.0, 0.0), axis=1, keepdims=True)
    out_ref[...] = jnp.broadcast_to(upright(partner[0:1, :]) - sums / counts, (rows, rows))


def advantages(partner, own, outer):
    rows = own.shape[1]
    return pl.pallas_call(
        advantage_kernel,
        out_shape=jax.ShapeDtypeStruct((rows, rows), F32),
        in_specs=[VMEM] * 3,
        out_specs=VMEM,
        compiler_params=PARAMS,
        name="advantage",
    )(partner, own, outer)


def loss_kernel(parts, shards, shard_ref, tokens_ref, *refs):
    mine, theirs = refs[:parts], refs[parts : 2 * parts]
    logits_ref, logprob_ref, entropy_ref, dlogits_ref = refs[2 * parts :]
    shard = shard_ref[0]
    rows, columns = dlogits_ref.shape
    shard_rows = columns // shards

    lengths = [ref.shape[0] for ref in mine]
    scores = jnp.concatenate(
        [a[...] + b[:n, :] for a, b, n in zip(mine, theirs, lengths)], axis=0
    )
    tokens = tokens_ref[...]
    relative = ((tokens // shard_rows) ^ shard) * shard_rows + tokens % shard_rows
    chosen = lax.broadcasted_iota(jnp.int32, (columns, rows), 0) == relative
    row_max = jnp.max(scores, axis=0, keepdims=True)
    unnormed = jnp.exp(scores - row_max)
    denominator = jnp.sum(unnormed, axis=0, keepdims=True)
    probabilities = unnormed / denominator
    dlogits = probabilities - jnp.where(chosen, 1.0, 0.0)
    for i in range(shards):
        block = slice(i * shard_rows, (i + 1) * shard_rows)
        dlogits_ref[:, block] = dlogits[block, :].T.astype(BF16)
        place = pl.multiple_of((shard ^ i) * shard_rows, 128)
        logits_ref[:, pl.ds(place, shard_rows)] = scores[block, :].T.astype(BF16)
    log_total = row_max + jnp.log(denominator)
    picked = jnp.sum(jnp.where(chosen, scores, 0.0), axis=0, keepdims=True)
    logprob_ref[...] = picked - log_total
    entropy_ref[...] = log_total - jnp.sum(probabilities * scores, axis=0, keepdims=True)


def loss(shard, tokens, mine, theirs, shards):
    rows = tokens.shape[1]
    columns = sum(part.shape[0] for part in mine)
    flat = jax.ShapeDtypeStruct((1, rows), F32)
    wide = jax.ShapeDtypeStruct((rows, columns), BF16)
    return pl.pallas_call(
        functools.partial(loss_kernel, len(mine), shards),
        out_shape=[wide, flat, flat, wide],
        in_specs=[SMEM] + [VMEM] * (1 + 2 * len(mine)),
        out_specs=[VMEM] * 4,
        compiler_params=pltpu.CompilerParams(vmem_limit_bytes=2 * 1024**2 + 32 * rows * columns),
        cost_estimate=pl.CostEstimate(
            flops=10 * rows * columns,
            bytes_accessed=12 * rows * columns,
            transcendentals=rows * columns,
        ),
        name="loss",
    )(shard, tokens, *mine, *theirs)


def scaling(advantage, width):
    return jnp.concatenate([advantage] * (width // advantage.shape[1]), axis=1)


def multiplied(dlogits, heads, out_ref, start, scale=None):
    block = 256
    scale = None if scale is None else scaling(scale, block)
    for j in range(heads[0].shape[1] // block):
        part = slice(j * block, (j + 1) * block)
        head = jnp.concatenate([ref[:, part] for ref in heads], axis=0)
        product = jnp.dot(dlogits, head, preferred_element_type=F32)
        product = product if scale is None else product * scale
        out_ref[:, start + j * block : start + (j + 1) * block] = product.astype(BF16)


def gradient_cost(rows, columns, width):
    return pl.CostEstimate(
        flops=2 * rows * columns * width,
        bytes_accessed=2 * width * (rows + columns),
        transcendentals=0,
    )


def first_kernel(dlogits_ref, *refs):
    heads, out_ref = refs[:-1], refs[-1]
    columns = dlogits_ref.shape[1]
    out_ref[:, :columns] = dlogits_ref[...]
    multiplied(dlogits_ref[...], heads, out_ref, columns)


def first_message(dlogits, heads):
    rows, columns = dlogits.shape
    width = heads[0].shape[1]
    return pl.pallas_call(
        first_kernel,
        out_shape=jax.ShapeDtypeStruct((rows, columns + width), BF16),
        in_specs=[VMEM] * (1 + len(heads)),
        out_specs=VMEM,
        compiler_params=PARAMS,
        cost_estimate=gradient_cost(rows, columns, width),
        name="first_message",
    )(dlogits, *heads)


def second_kernel(dlogits_ref, _, *refs):
    multiplied(dlogits_ref[...], refs[:-1], refs[-1], 0)


def second_message(dlogits, first, heads):
    rows, columns = dlogits.shape
    width = heads[0].shape[1]
    return pl.pallas_call(
        second_kernel,
        out_shape=jax.ShapeDtypeStruct((rows, width), BF16),
        in_specs=[VMEM, ANY] + [VMEM] * len(heads),
        out_specs=VMEM,
        compiler_params=PARAMS,
        cost_estimate=gradient_cost(rows, columns, width),
        name="second_message",
    )(dlogits, first, *heads)


def scaled(message_ref, advantage, columns, out_ref, start):
    block = 256
    scale = scaling(advantage, block)
    for j in range(0, columns.stop - columns.start, block):
        value = message_ref[:, columns.start + j : columns.start + j + block].astype(F32)
        out_ref[:, start + j : start + j + block] = (value * scale).astype(BF16)


def staying_kernel(which_ref, first_ref, advantage_ref, *refs):
    heads, (out_ref, held_ref, sem) = refs[:-3], refs[-3:]
    depth = held_ref.shape[1] // 3
    width = 2 * depth
    columns = first_ref.shape[1] - depth
    mine = pl.multiple_of(which_ref[0] * width, 128)
    other = pl.multiple_of((1 - which_ref[0]) * width, 128)
    advantage = advantage_ref[...]
    copies = []

    def put(i, place):
        source = held_ref.at[:, pl.ds(i * depth, depth)]
        target = out_ref.at[:, pl.ds(pl.multiple_of(place, 128), depth)]
        copies.append(pltpu.make_async_copy(source, target, sem.at[i]))
        copies[-1].start()

    scaled(first_ref, advantage, slice(columns, columns + depth), held_ref, 0)
    put(0, other)
    dlogits = first_ref[:, :columns]
    for i in range(2):
        multiplied(dlogits, heads[i::2], held_ref, (i + 1) * depth, advantage)
        put(i + 1, mine + i * depth)
    for copy in copies:
        copy.wait()


def staying_gradient(which, first, advantage, heads):
    rows = first.shape[0]
    depth = heads[0].shape[1]
    columns = first.shape[1] - depth
    return pl.pallas_call(
        staying_kernel,
        out_shape=jax.ShapeDtypeStruct((rows, 4 * depth), BF16),
        in_specs=[SMEM] + [VMEM] * (2 + len(heads)),
        out_specs=HBM,
        scratch_shapes=[pltpu.VMEM((rows, 3 * depth), BF16), pltpu.SemaphoreType.DMA((3,))],
        compiler_params=PARAMS,
        cost_estimate=gradient_cost(rows, columns, 2 * depth),
        name="staying_gradient",
    )(which, first, advantage, *heads)


def placed_kernel(which_ref, second_ref, advantage_ref, _, out_ref, held_ref, sem):
    depth = second_ref.shape[1]
    parts = 5 if depth % 1280 == 0 else 1
    width = depth // parts
    start = (1 - which_ref[0]) * (2 * depth) + depth
    copies = []
    for i in range(parts):
        part = slice(i * width, (i + 1) * width)
        scaled(second_ref, advantage_ref[...], part, held_ref, i * width)
        target = out_ref.at[:, pl.ds(pl.multiple_of(start + i * width, 128), width)]
        copies.append(
            pltpu.make_async_copy(held_ref.at[:, pl.ds(i * width, width)], target, sem.at[i])
        )
        copies[-1].start()
    for copy in copies:
        copy.wait()


def placed_beside(which, second, advantage, gradient):
    return pl.pallas_call(
        placed_kernel,
        out_shape=jax.ShapeDtypeStruct(gradient.shape, gradient.dtype),
        in_specs=[SMEM, VMEM, VMEM, HBM],
        out_specs=HBM,
        scratch_shapes=[pltpu.VMEM(second.shape, BF16), pltpu.SemaphoreType.DMA((5,))],
        input_output_aliases={3: 0},
        compiler_params=PARAMS,
        name="place_second",
    )(which, second, advantage, gradient)


def body(hidden, head_weight, tokens, rewards, group_ids):
    shards = lax.axis_size("vocab")
    which = (lax.axis_index("section") % 2).reshape(1)
    shard = lax.axis_index("vocab").reshape(1)
    near = [o for o in range(shards) if bin(o).count("1") <= 1]
    far = [o for o in range(shards) if bin(o).count("1") > 1]

    own = jnp.stack([rewards, (group_ids + 1).astype(F32)])
    pieces = tuple(take(which, head_weight, 2))
    late_hidden, _ = lax.optimization_barrier((hidden, pieces))
    (other_half,) = take(1 - which, late_hidden, 1)
    other_half, late_pieces = lax.optimization_barrier((other_half, pieces))
    heads = gathered(pieces, late_pieces, "vocab")
    partner_half = swapped(other_half, "section", 1)

    rows = turned(which, hidden, partner_half)
    mine, theirs = [], []
    for offsets, facts in ((near, (own,)), (far, ())):
        pieces = [piece for o in offsets for piece in heads[o]]
        kept, sent, *again = partial_scores(rows, pieces, facts)
        mine.append(kept)
        theirs.append(swapped(sent, "section", 1))
    partner_facts = theirs[0]
    mine, theirs = in_order(mine, near + far, 0), in_order(theirs, near + far, BELOW)
    logits, logprob, entropy, dlogits = loss(
        shard, tokens[None, :], mine, theirs, shards
    )
    for i, offset in enumerate(far):
        heads[offset] = again[2 * i : 2 * i + 2]
    pieces = [piece for pair in heads for piece in pair]
    first = first_message(dlogits, pieces[0::2])
    first_in = swapped(first, "section", 1)
    second = second_message(dlogits, first, pieces[1::2])
    second_in = swapped(second, "section", 1)

    late_own, _ = lax.optimization_barrier((own, second))
    axes = ("vocab", "section")
    count = lax.axis_size(axes)
    beyond = [(i + 2, i) for i in range(0, count - 2, 2)] + [(i, i + 2) for i in range(1, count - 2, 2)]
    outer = lax.ppermute(late_own, axes, beyond)
    advantage = advantages(partner_facts, own, outer)
    staying = staying_gradient(which, first_in, advantage, pieces)
    previous_grad = placed_beside(which, second_in, advantage, staying)
    return (logits, logprob[0], entropy[0], previous_grad)


def in_order(blocks, order, below):
    if order == sorted(order):
        return blocks
    first = blocks[0]
    kept = first.shape[0] - below
    whole = jnp.concatenate([first[:kept], *blocks[1:]], axis=0)
    width = whole.shape[0] // len(order)
    parts = {offset: whole[i * width : (i + 1) * width] for i, offset in enumerate(order)}
    return [jnp.concatenate([parts[offset] for offset in sorted(order)] + [first[kept:]], axis=0)]


def solution(mesh):
    placed = (
        P(("seq", "vocab", "section"), None),
        P(("seq", "vocab"), None),
        P(("seq", "vocab", "section")),
        P(("seq", "vocab", "section")),
        P(("seq", "vocab", "section")),
    )
    return jax.shard_map(
        body,
        mesh=mesh,
        in_specs=placed,
        out_specs=(
            P(("seq", "vocab", "section"), None),
            P(("seq", "vocab", "section")),
            P(("seq", "vocab", "section")),
            P(("seq", "vocab", "section"), None),
        ),
        check_vma=False,
    )
```

```python
import functools

import jax
import jax.numpy as jnp
from jax import lax
from jax.experimental import pallas as pl
from jax.experimental.pallas import tpu as pltpu
from jax.sharding import PartitionSpec as P

F32, BF16 = jnp.float32, jnp.bfloat16
HBM = pl.BlockSpec(memory_space=pltpu.HBM)
ANY = pl.BlockSpec(memory_space=pl.ANY)
SMEM = pl.BlockSpec(memory_space=pltpu.SMEM)
VMEM = pl.BlockSpec(memory_space=pltpu.VMEM)
PARAMS = pltpu.CompilerParams(vmem_limit_bytes=4 * 1024 * 1024)
BELOW = 8


def swapped(value, axis, mask):
    pairs = [(source, source ^ mask) for source in range(lax.axis_size(axis))]
    return lax.ppermute(value, axis, pairs)


def gathered(first_wave, second_wave, axis):
    count = lax.axis_size(axis)
    masks = [1 << bit for bit in range((count - 1).bit_length())]
    uppers, lowers = {0: first_wave[0]}, {0: first_wave[1]}
    for mask in masks:
        early = mask == masks[0]
        uppers[mask] = swapped((first_wave if early else second_wave)[0], axis, mask)
    for mask in reversed(masks):
        early = mask == masks[-1]
        lowers[mask] = swapped((first_wave if early else second_wave)[1], axis, mask)
    for offset in sorted(range(1, count), key=lambda o: (bin(o).count("1"), o)):
        if offset in uppers:
            continue
        bits = [mask for mask in masks if offset & mask]
        uppers[offset] = swapped(uppers[offset ^ bits[-1]], axis, bits[-1])
        lowers[offset] = swapped(lowers[offset ^ bits[0]], axis, bits[0])
    return [(uppers[offset], lowers[offset]) for offset in range(count)]


def take_kernel(which_ref, value_ref, *refs):
    outs, sem = refs[:-1], refs[-1]
    width = outs[0].shape[1]
    start = which_ref[0] * width * len(outs)
    copies = []
    for i, out in enumerate(outs):
        source = value_ref.at[:, pl.ds(pl.multiple_of(start + i * width, 128), width)]
        copies.append(pltpu.make_async_copy(source, out, sem.at[i]))
    for copy in copies:
        copy.start()
    for copy in copies:
        copy.wait()


def take(which, value, pieces):
    rows, width = value.shape[0], value.shape[1] // 2 // pieces
    return pl.pallas_call(
        take_kernel,
        out_shape=[jax.ShapeDtypeStruct((rows, width), value.dtype)] * pieces,
        in_specs=[SMEM, ANY],
        out_specs=[ANY] * pieces,
        scratch_shapes=[pltpu.SemaphoreType.DMA((pieces,))],
        compiler_params=PARAMS,
        cost_estimate=pl.CostEstimate(
            flops=0, bytes_accessed=value.size * value.dtype.itemsize, transcendentals=0
        ),
        name="take_half",
    )(which, value)


def turned_kernel(which_ref, hidden_ref, out_ref):
    width = out_ref.shape[0]
    block = 256
    for i in range(width // block):
        start = which_ref[0] * width + i * block
        own = hidden_ref[:, pl.ds(pl.multiple_of(start, 128), block)]
        out_ref[i * block : (i + 1) * block, :] = own.T


def turned(which, hidden):
    rows, width = hidden.shape[0], hidden.shape[1] // 2
    return pl.pallas_call(
        turned_kernel,
        out_shape=jax.ShapeDtypeStruct((width, rows), BF16),
        in_specs=[SMEM, VMEM],
        out_specs=VMEM,
        compiler_params=PARAMS,
        cost_estimate=pl.CostEstimate(
            flops=0, bytes_accessed=4 * rows * width, transcendentals=0
        ),
        name="turned_rows",
    )(which, hidden)


def beside_kernel(own_ref, first_ref, second_ref, out_ref):
    rows = own_ref.shape[1]
    out_ref[:, :rows] = own_ref[...]
    block = 256
    for i in range(own_ref.shape[0] // block):
        part = slice(i * block, (i + 1) * block)
        out_ref[part, rows:] = (first_ref[:, part] + second_ref[:, part]).T


def partner_beside(own, first_half, second_half):
    width, rows = own.shape
    return pl.pallas_call(
        beside_kernel,
        out_shape=jax.ShapeDtypeStruct((width, 2 * rows), BF16),
        in_specs=[VMEM] * 3,
        out_specs=VMEM,
        compiler_params=PARAMS,
        cost_estimate=pl.CostEstimate(
            flops=0, bytes_accessed=8 * rows * width, transcendentals=0
        ),
        name="partner_rows",
    )(own, first_half, second_half)


def partial_kernel(facts, count, turned_ref, *refs):
    heads, (mine_ref, theirs_ref) = refs[facts : facts + count], refs[facts + count :][:2]
    for held, ref in zip(refs[facts + count + 2 :], heads):
        held[...] = ref[...]
    shard_rows, depth = heads[0].shape
    rows = mine_ref.shape[1]
    for i in range(len(heads) // 2):
        total = jnp.dot(heads[2 * i][...], turned_ref[:depth, :], preferred_element_type=F32)
        total += jnp.dot(heads[2 * i + 1][...], turned_ref[depth:, :], preferred_element_type=F32)
        mine_ref[i * shard_rows : (i + 1) * shard_rows, :] = total[:, :rows]
        theirs_ref[i * shard_rows : (i + 1) * shard_rows, :] = total[:, rows:]
    if facts:
        below = theirs_ref.shape[0] - mine_ref.shape[0]
        theirs_ref[mine_ref.shape[0] :, :] = jnp.zeros((below, rows), F32)
        theirs_ref[pl.ds(mine_ref.shape[0], refs[0].shape[0]), :] = refs[0][...]


def partial_scores(turned_rows, heads, facts=()):
    width, rows = turned_rows.shape
    columns = sum(head.shape[0] for head in heads) // 2
    below = BELOW * len(facts)
    return pl.pallas_call(
        functools.partial(partial_kernel, len(facts), len(heads)),
        out_shape=[
            jax.ShapeDtypeStruct((columns, rows // 2), F32),
            jax.ShapeDtypeStruct((columns + below, rows // 2), F32),
            *[jax.ShapeDtypeStruct(head.shape, head.dtype) for head in heads if not facts],
        ],
        in_specs=[VMEM] * (1 + len(facts) + len(heads)),
        out_specs=[VMEM] * (2 if facts else 2 + len(heads)),
        compiler_params=PARAMS,
        cost_estimate=pl.CostEstimate(
            flops=2 * rows * columns * width,
            bytes_accessed=2 * width * (rows + columns),
            transcendentals=0,
        ),
        name="partial_scores",
    )(turned_rows, *facts, *heads)


def advantage_kernel(partner_ref, own_ref, outer_ref, out_ref):
    rows = own_ref.shape[1]
    partner = partner_ref[partner_ref.shape[0] - BELOW :, :]
    eye = lax.broadcasted_iota(jnp.int32, (rows, rows), 0) == lax.broadcasted_iota(
        jnp.int32, (rows, rows), 1
    )

    def upright(row):
        return jnp.sum(jnp.where(eye, row, 0.0), axis=1, keepdims=True)

    groups = upright(partner[1:2, :])
    sums, counts = jnp.zeros((rows, 1), F32), jnp.zeros((rows, 1), F32)
    for facts in (partner, own_ref[...], outer_ref[...]):
        member = facts[1:2, :] == groups
        sums += jnp.sum(jnp.where(member, facts[0:1, :], 0.0), axis=1, keepdims=True)
        counts += jnp.sum(jnp.where(member, 1.0, 0.0), axis=1, keepdims=True)
    out_ref[...] = jnp.broadcast_to(upright(partner[0:1, :]) - sums / counts, (rows, rows))


def advantages(partner, own, outer):
    rows = own.shape[1]
    return pl.pallas_call(
        advantage_kernel,
        out_shape=jax.ShapeDtypeStruct((rows, rows), F32),
        in_specs=[VMEM] * 3,
        out_specs=VMEM,
        compiler_params=PARAMS,
        name="advantage",
    )(partner, own, outer)


def loss_kernel(parts, shards, shard_ref, tokens_ref, *refs):
    mine, theirs = refs[:parts], refs[parts : 2 * parts]
    logits_ref, logprob_ref, entropy_ref, dlogits_ref = refs[2 * parts :]
    shard = shard_ref[0]
    rows, columns = dlogits_ref.shape
    shard_rows = columns // shards

    lengths = [ref.shape[0] for ref in mine]
    scores = jnp.concatenate(
        [a[...] + b[:n, :] for a, b, n in zip(mine, theirs, lengths)], axis=0
    )
    tokens = tokens_ref[...]
    relative = ((tokens // shard_rows) ^ shard) * shard_rows + tokens % shard_rows
    chosen = lax.broadcasted_iota(jnp.int32, (columns, rows), 0) == relative
    row_max = jnp.max(scores, axis=0, keepdims=True)
    unnormed = jnp.exp(scores - row_max)
    denominator = jnp.sum(unnormed, axis=0, keepdims=True)
    probabilities = unnormed / denominator
    dlogits = probabilities - jnp.where(chosen, 1.0, 0.0)
    for i in range(shards):
        block = slice(i * shard_rows, (i + 1) * shard_rows)
        dlogits_ref[:, block] = dlogits[block, :].T.astype(BF16)
        place = pl.multiple_of((shard ^ i) * shard_rows, 128)
        logits_ref[:, pl.ds(place, shard_rows)] = scores[block, :].T.astype(BF16)
    log_total = row_max + jnp.log(denominator)
    picked = jnp.sum(jnp.where(chosen, scores, 0.0), axis=0, keepdims=True)
    logprob_ref[...] = picked - log_total
    entropy_ref[...] = log_total - jnp.sum(probabilities * scores, axis=0, keepdims=True)


def loss(shard, tokens, mine, theirs, shards):
    rows = tokens.shape[1]
    columns = sum(part.shape[0] for part in mine)
    flat = jax.ShapeDtypeStruct((1, rows), F32)
    wide = jax.ShapeDtypeStruct((rows, columns), BF16)
    return pl.pallas_call(
        functools.partial(loss_kernel, len(mine), shards),
        out_shape=[wide, flat, flat, wide],
        in_specs=[SMEM] + [VMEM] * (1 + 2 * len(mine)),
        out_specs=[VMEM] * 4,
        compiler_params=pltpu.CompilerParams(vmem_limit_bytes=2 * 1024**2 + 32 * rows * columns),
        cost_estimate=pl.CostEstimate(
            flops=10 * rows * columns,
            bytes_accessed=12 * rows * columns,
            transcendentals=rows * columns,
        ),
        name="loss",
    )(shard, tokens, *mine, *theirs)


def scaling(advantage, width):
    return jnp.concatenate([advantage] * (width // advantage.shape[1]), axis=1)


def multiplied(dlogits, heads, out_ref, start, scale=None):
    block = 256
    scale = None if scale is None else scaling(scale, block)
    for j in range(heads[0].shape[1] // block):
        part = slice(j * block, (j + 1) * block)
        head = jnp.concatenate([ref[:, part] for ref in heads], axis=0)
        product = jnp.dot(dlogits, head, preferred_element_type=F32)
        product = product if scale is None else product * scale
        out_ref[:, start + j * block : start + (j + 1) * block] = product.astype(BF16)


def gradient_cost(rows, columns, width):
    return pl.CostEstimate(
        flops=2 * rows * columns * width,
        bytes_accessed=2 * width * (rows + columns),
        transcendentals=0,
    )


def first_kernel(dlogits_ref, *refs):
    heads, out_ref = refs[:-1], refs[-1]
    columns = dlogits_ref.shape[1]
    out_ref[:, :columns] = dlogits_ref[...]
    multiplied(dlogits_ref[...], heads, out_ref, columns)


def first_message(dlogits, heads):
    rows, columns = dlogits.shape
    width = heads[0].shape[1]
    return pl.pallas_call(
        first_kernel,
        out_shape=jax.ShapeDtypeStruct((rows, columns + width), BF16),
        in_specs=[VMEM] * (1 + len(heads)),
        out_specs=VMEM,
        compiler_params=PARAMS,
        cost_estimate=gradient_cost(rows, columns, width),
        name="first_message",
    )(dlogits, *heads)


def second_kernel(dlogits_ref, _, *refs):
    multiplied(dlogits_ref[...], refs[:-1], refs[-1], 0)


def second_message(dlogits, first, heads):
    rows, columns = dlogits.shape
    width = heads[0].shape[1]
    return pl.pallas_call(
        second_kernel,
        out_shape=jax.ShapeDtypeStruct((rows, width), BF16),
        in_specs=[VMEM, ANY] + [VMEM] * len(heads),
        out_specs=VMEM,
        compiler_params=PARAMS,
        cost_estimate=gradient_cost(rows, columns, width),
        name="second_message",
    )(dlogits, first, *heads)


def scaled(message_ref, advantage, columns, out_ref, start):
    block = 256
    scale = scaling(advantage, block)
    for j in range(0, columns.stop - columns.start, block):
        value = message_ref[:, columns.start + j : columns.start + j + block].astype(F32)
        out_ref[:, start + j : start + j + block] = (value * scale).astype(BF16)


def staying_kernel(which_ref, first_ref, advantage_ref, *refs):
    heads, (out_ref, held_ref, sem) = refs[:-3], refs[-3:]
    depth = held_ref.shape[1] // 3
    width = 2 * depth
    columns = first_ref.shape[1] - depth
    mine = pl.multiple_of(which_ref[0] * width, 128)
    other = pl.multiple_of((1 - which_ref[0]) * width, 128)
    advantage = advantage_ref[...]
    copies = []

    def put(i, place):
        source = held_ref.at[:, pl.ds(i * depth, depth)]
        target = out_ref.at[:, pl.ds(pl.multiple_of(place, 128), depth)]
        copies.append(pltpu.make_async_copy(source, target, sem.at[i]))
        copies[-1].start()

    scaled(first_ref, advantage, slice(columns, columns + depth), held_ref, 0)
    put(0, other)
    dlogits = first_ref[:, :columns]
    for i in range(2):
        multiplied(dlogits, heads[i::2], held_ref, (i + 1) * depth, advantage)
        put(i + 1, mine + i * depth)
    for copy in copies:
        copy.wait()


def staying_gradient(which, first, advantage, heads):
    rows = first.shape[0]
    depth = heads[0].shape[1]
    columns = first.shape[1] - depth
    return pl.pallas_call(
        staying_kernel,
        out_shape=jax.ShapeDtypeStruct((rows, 4 * depth), BF16),
        in_specs=[SMEM] + [VMEM] * (2 + len(heads)),
        out_specs=HBM,
        scratch_shapes=[pltpu.VMEM((rows, 3 * depth), BF16), pltpu.SemaphoreType.DMA((3,))],
        compiler_params=PARAMS,
        cost_estimate=gradient_cost(rows, columns, 2 * depth),
        name="staying_gradient",
    )(which, first, advantage, *heads)


def placed_kernel(which_ref, second_ref, advantage_ref, _, out_ref, held_ref, sem):
    depth = second_ref.shape[1]
    parts = 5 if depth % 1280 == 0 else 1
    width = depth // parts
    start = (1 - which_ref[0]) * (2 * depth) + depth
    copies = []
    for i in range(parts):
        part = slice(i * width, (i + 1) * width)
        scaled(second_ref, advantage_ref[...], part, held_ref, i * width)
        target = out_ref.at[:, pl.ds(pl.multiple_of(start + i * width, 128), width)]
        copies.append(
            pltpu.make_async_copy(held_ref.at[:, pl.ds(i * width, width)], target, sem.at[i])
        )
        copies[-1].start()
    for copy in copies:
        copy.wait()


def placed_beside(which, second, advantage, gradient):
    return pl.pallas_call(
        placed_kernel,
        out_shape=jax.ShapeDtypeStruct(gradient.shape, gradient.dtype),
        in_specs=[SMEM, VMEM, VMEM, HBM],
        out_specs=HBM,
        scratch_shapes=[pltpu.VMEM(second.shape, BF16), pltpu.SemaphoreType.DMA((5,))],
        input_output_aliases={3: 0},
        compiler_params=PARAMS,
        name="place_second",
    )(which, second, advantage, gradient)


def of_parts(value, members):
    count = lax.axis_size("section")
    pairs = [(p * count + i, p * count + (i ^ 1)) for p in members for i in range(count)]
    return lax.ppermute(value, ("seq", "section"), pairs)


def body(hidden, head_weight, tokens, rewards, group_ids):
    shards = lax.axis_size("vocab")
    which = (lax.axis_index("section") % 2).reshape(1)
    shard = lax.axis_index("vocab").reshape(1)
    near = [o for o in range(shards) if bin(o).count("1") <= 1]
    far = [o for o in range(shards) if bin(o).count("1") > 1]

    own = jnp.stack([rewards, (group_ids + 1).astype(F32)])
    parts = lax.axis_size("seq")
    leading, following = range(1, parts), range(1)

    (other_half,) = take(1 - which, hidden, 1)
    first_half = of_parts(other_half, following)
    pieces = tuple(take(which, head_weight, 2))
    pieces, first_half = lax.optimization_barrier((pieces, first_half))
    late_hidden, _ = lax.optimization_barrier((hidden, pieces))
    own_rows = turned(which, late_hidden)
    own_rows, late_pieces = lax.optimization_barrier((own_rows, pieces))
    heads = gathered(pieces, late_pieces, "vocab")
    arrived = [piece for o in near[1:] for piece in heads[o]]
    other_half, _ = lax.optimization_barrier((other_half, arrived))
    second_half = of_parts(other_half, leading)

    rows = partner_beside(own_rows, first_half, second_half)
    mine, theirs = [], []
    for offsets, facts in ((near, (own,)), (far, ())):
        pieces = [piece for o in offsets for piece in heads[o]]
        kept, sent, *again = partial_scores(rows, pieces, facts)
        mine.append(kept)
        theirs.append(swapped(sent, "section", 1))
    partner_facts = theirs[0]
    mine, theirs = in_order(mine, near + far, 0), in_order(theirs, near + far, BELOW)
    logits, logprob, entropy, dlogits = loss(
        shard, tokens[None, :], mine, theirs, shards
    )
    for i, offset in enumerate(far):
        heads[offset] = again[2 * i : 2 * i + 2]
    pieces = [piece for pair in heads for piece in pair]
    first = first_message(dlogits, pieces[0::2])
    first_in = swapped(first, "section", 1)
    second = second_message(dlogits, first, pieces[1::2])
    second_in = swapped(second, "section", 1)

    late_own, _ = lax.optimization_barrier((own, second))
    axes = ("vocab", "section")
    count = lax.axis_size(axes)
    beyond = [(i + 2, i) for i in range(0, count - 2, 2)] + [(i, i + 2) for i in range(1, count - 2, 2)]
    outer = lax.ppermute(late_own, axes, beyond)
    advantage = advantages(partner_facts, own, outer)
    staying = staying_gradient(which, first_in, advantage, pieces)
    previous_grad = placed_beside(which, second_in, advantage, staying)
    return (logits, logprob[0], entropy[0], previous_grad)


def in_order(blocks, order, below):
    if order == sorted(order):
        return blocks
    first = blocks[0]
    kept = first.shape[0] - below
    whole = jnp.concatenate([first[:kept], *blocks[1:]], axis=0)
    width = whole.shape[0] // len(order)
    parts = {offset: whole[i * width : (i + 1) * width] for i, offset in enumerate(order)}
    return [jnp.concatenate([parts[offset] for offset in sorted(order)] + [first[kept:]], axis=0)]


def solution(mesh):
    placed = (
        P(("seq", "vocab", "section"), None),
        P(("seq", "vocab"), None),
        P(("seq", "vocab", "section")),
        P(("seq", "vocab", "section")),
        P(("seq", "vocab", "section")),
    )
    return jax.shard_map(
        body,
        mesh=mesh,
        in_specs=placed,
        out_specs=(
            P(("seq", "vocab", "section"), None),
            P(("seq", "vocab", "section")),
            P(("seq", "vocab", "section")),
            P(("seq", "vocab", "section"), None),
        ),
        check_vma=False,
    )
```

```python
import functools

import jax
import jax.numpy as jnp
from jax import lax
from jax.experimental import pallas as pl
from jax.experimental.pallas import tpu as pltpu
from jax.sharding import PartitionSpec as P

F32, BF16 = jnp.float32, jnp.bfloat16
HBM = pl.BlockSpec(memory_space=pltpu.HBM)
ANY = pl.BlockSpec(memory_space=pl.ANY)
SMEM = pl.BlockSpec(memory_space=pltpu.SMEM)
VMEM = pl.BlockSpec(memory_space=pltpu.VMEM)
PARAMS = pltpu.CompilerParams(vmem_limit_bytes=4 * 1024 * 1024)
BELOW = 8


def swapped(value, axis, mask):
    pairs = [(source, source ^ mask) for source in range(lax.axis_size(axis))]
    return lax.ppermute(value, axis, pairs)


def gathered(first_wave, second_wave, axis):
    count = lax.axis_size(axis)
    masks = [1 << bit for bit in range((count - 1).bit_length())]
    uppers, lowers = {0: first_wave[0]}, {0: first_wave[1]}
    for mask in masks:
        early = mask == masks[0]
        uppers[mask] = swapped((first_wave if early else second_wave)[0], axis, mask)
    for mask in reversed(masks):
        early = mask == masks[-1]
        lowers[mask] = swapped((first_wave if early else second_wave)[1], axis, mask)
    for offset in sorted(range(1, count), key=lambda o: (bin(o).count("1"), o)):
        if offset in uppers:
            continue
        bits = [mask for mask in masks if offset & mask]
        uppers[offset] = swapped(uppers[offset ^ bits[-1]], axis, bits[-1])
        lowers[offset] = swapped(lowers[offset ^ bits[0]], axis, bits[0])
    return [(uppers[offset], lowers[offset]) for offset in range(count)]


def take_kernel(which_ref, value_ref, *refs):
    outs, sem = refs[:-1], refs[-1]
    width = outs[0].shape[1]
    start = which_ref[0] * width * len(outs)
    copies = []
    for i, out in enumerate(outs):
        source = value_ref.at[:, pl.ds(pl.multiple_of(start + i * width, 128), width)]
        copies.append(pltpu.make_async_copy(source, out, sem.at[i]))
    for copy in copies:
        copy.start()
    for copy in copies:
        copy.wait()


def take(which, value, pieces):
    rows, width = value.shape[0], value.shape[1] // 2 // pieces
    return pl.pallas_call(
        take_kernel,
        out_shape=[jax.ShapeDtypeStruct((rows, width), value.dtype)] * pieces,
        in_specs=[SMEM, ANY],
        out_specs=[ANY] * pieces,
        scratch_shapes=[pltpu.SemaphoreType.DMA((pieces,))],
        compiler_params=PARAMS,
        cost_estimate=pl.CostEstimate(
            flops=0, bytes_accessed=value.size * value.dtype.itemsize, transcendentals=0
        ),
        name="take_half",
    )(which, value)


def turned_kernel(which_ref, hidden_ref, partner_ref, out_ref):
    rows, width = partner_ref.shape
    block = 256
    for i in range(width // block):
        start = which_ref[0] * width + i * block
        own = hidden_ref[:, pl.ds(pl.multiple_of(start, 128), block)]
        out_ref[i * block : (i + 1) * block, :rows] = own.T
        part = slice(i * block, (i + 1) * block)
        out_ref[part, rows:] = partner_ref[:, part].T


def turned(which, hidden, partner_half):
    rows, width = partner_half.shape
    return pl.pallas_call(
        turned_kernel,
        out_shape=jax.ShapeDtypeStruct((width, 2 * rows), BF16),
        in_specs=[SMEM] + [VMEM] * 2,
        out_specs=VMEM,
        compiler_params=PARAMS,
        cost_estimate=pl.CostEstimate(
            flops=0, bytes_accessed=8 * rows * width, transcendentals=0
        ),
        name="turned_rows",
    )(which, hidden, partner_half)


def partial_kernel(facts, count, turned_ref, *refs):
    heads, (mine_ref, theirs_ref) = refs[facts : facts + count], refs[facts + count :][:2]
    for held, ref in zip(refs[facts + count + 2 :], heads):
        held[...] = ref[...]
    shard_rows, depth = heads[0].shape
    rows = mine_ref.shape[1]
    for i in range(len(heads) // 2):
        total = jnp.dot(heads[2 * i][...], turned_ref[:depth, :], preferred_element_type=F32)
        total += jnp.dot(heads[2 * i + 1][...], turned_ref[depth:, :], preferred_element_type=F32)
        mine_ref[i * shard_rows : (i + 1) * shard_rows, :] = total[:, :rows]
        theirs_ref[i * shard_rows : (i + 1) * shard_rows, :] = total[:, rows:]
    if facts:
        below = theirs_ref.shape[0] - mine_ref.shape[0]
        theirs_ref[mine_ref.shape[0] :, :] = jnp.zeros((below, rows), F32)
        theirs_ref[pl.ds(mine_ref.shape[0], refs[0].shape[0]), :] = refs[0][...]


def partial_scores(turned_rows, heads, facts=()):
    width, rows = turned_rows.shape
    columns = sum(head.shape[0] for head in heads) // 2
    below = BELOW * len(facts)
    return pl.pallas_call(
        functools.partial(partial_kernel, len(facts), len(heads)),
        out_shape=[
            jax.ShapeDtypeStruct((columns, rows // 2), F32),
            jax.ShapeDtypeStruct((columns + below, rows // 2), F32),
            *[jax.ShapeDtypeStruct(head.shape, head.dtype) for head in heads if not facts],
        ],
        in_specs=[VMEM] * (1 + len(facts) + len(heads)),
        out_specs=[VMEM] * (2 if facts else 2 + len(heads)),
        compiler_params=PARAMS,
        cost_estimate=pl.CostEstimate(
            flops=2 * rows * columns * width,
            bytes_accessed=2 * width * (rows + columns),
            transcendentals=0,
        ),
        name="partial_scores",
    )(turned_rows, *facts, *heads)


def advantage_of(own, outer, partner):
    rows = own.shape[1]
    eye = lax.broadcasted_iota(jnp.int32, (rows, rows), 0) == lax.broadcasted_iota(
        jnp.int32, (rows, rows), 1
    )
    groups = jnp.sum(jnp.where(eye, own[1:2, :], 0.0), axis=1, keepdims=True)
    sums, counts = jnp.zeros((rows, 1), F32), jnp.zeros((rows, 1), F32)
    for facts in (own, outer, partner):
        member = facts[1:2, :] == groups
        sums += jnp.sum(jnp.where(member, facts[0:1, :], 0.0), axis=1, keepdims=True)
        counts += jnp.sum(jnp.where(member, 1.0, 0.0), axis=1, keepdims=True)
    return own[0:1, :] - jnp.sum(jnp.where(eye, sums / counts, 0.0), axis=0, keepdims=True)


def loss_kernel(parts, shards, shard_ref, tokens_ref, own_ref, outer_ref, *refs):
    mine, theirs = refs[:parts], refs[parts : 2 * parts]
    logits_ref, logprob_ref, entropy_ref, dlogits_ref = refs[2 * parts :]
    shard = shard_ref[0]
    rows, columns = dlogits_ref.shape
    shard_rows = columns // shards

    lengths = [ref.shape[0] for ref in mine]
    partner = theirs[0][lengths[0] :, :]
    advantage = advantage_of(own_ref[...], outer_ref[...], partner)
    scores = jnp.concatenate(
        [a[...] + b[:n, :] for a, b, n in zip(mine, theirs, lengths)], axis=0
    )
    tokens = tokens_ref[...]
    relative = ((tokens // shard_rows) ^ shard) * shard_rows + tokens % shard_rows
    chosen = lax.broadcasted_iota(jnp.int32, (columns, rows), 0) == relative
    row_max = jnp.max(scores, axis=0, keepdims=True)
    unnormed = jnp.exp(scores - row_max)
    denominator = jnp.sum(unnormed, axis=0, keepdims=True)
    probabilities = unnormed / denominator
    dlogits = advantage * (probabilities - jnp.where(chosen, 1.0, 0.0))
    for i in range(shards):
        block = slice(i * shard_rows, (i + 1) * shard_rows)
        dlogits_ref[:, block] = dlogits[block, :].T.astype(BF16)
        place = pl.multiple_of((shard ^ i) * shard_rows, 128)
        logits_ref[:, pl.ds(place, shard_rows)] = scores[block, :].T.astype(BF16)
    log_total = row_max + jnp.log(denominator)
    picked = jnp.sum(jnp.where(chosen, scores, 0.0), axis=0, keepdims=True)
    logprob_ref[...] = picked - log_total
    entropy_ref[...] = log_total - jnp.sum(probabilities * scores, axis=0, keepdims=True)


def loss(shard, tokens, own, outer, mine, theirs, shards):
    rows = tokens.shape[1]
    columns = sum(part.shape[0] for part in mine)
    flat = jax.ShapeDtypeStruct((1, rows), F32)
    wide = jax.ShapeDtypeStruct((rows, columns), BF16)
    return pl.pallas_call(
        functools.partial(loss_kernel, len(mine), shards),
        out_shape=[wide, flat, flat, wide],
        in_specs=[SMEM] + [VMEM] * (3 + 2 * len(mine)),
        out_specs=[VMEM] * 4,
        compiler_params=pltpu.CompilerParams(vmem_limit_bytes=2 * 1024**2 + 32 * rows * columns),
        cost_estimate=pl.CostEstimate(
            flops=10 * rows * columns,
            bytes_accessed=12 * rows * columns,
            transcendentals=rows * columns,
        ),
        name="loss",
    )(shard, tokens, own, outer, *mine, *theirs)


def multiplied(dlogits, heads, out_ref, start):
    block = 256
    for j in range(heads[0].shape[1] // block):
        part = slice(j * block, (j + 1) * block)
        head = jnp.concatenate([ref[:, part] for ref in heads], axis=0)
        product = jnp.dot(dlogits, head, preferred_element_type=F32)
        out_ref[:, start + j * block : start + (j + 1) * block] = product.astype(BF16)


def gradient_cost(rows, columns, width):
    return pl.CostEstimate(
        flops=2 * rows * columns * width,
        bytes_accessed=2 * width * (rows + columns),
        transcendentals=0,
    )


def first_kernel(dlogits_ref, *refs):
    heads, out_ref = refs[:-1], refs[-1]
    columns = dlogits_ref.shape[1]
    out_ref[:, :columns] = dlogits_ref[...]
    multiplied(dlogits_ref[...], heads, out_ref, columns)


def first_message(dlogits, heads):
    rows, columns = dlogits.shape
    width = heads[0].shape[1]
    return pl.pallas_call(
        first_kernel,
        out_shape=jax.ShapeDtypeStruct((rows, columns + width), BF16),
        in_specs=[VMEM] * (1 + len(heads)),
        out_specs=VMEM,
        compiler_params=PARAMS,
        cost_estimate=gradient_cost(rows, columns, width),
        name="first_message",
    )(dlogits, *heads)


def second_kernel(dlogits_ref, _, *refs):
    multiplied(dlogits_ref[...], refs[:-1], refs[-1], 0)


def second_message(dlogits, first, heads):
    rows, columns = dlogits.shape
    width = heads[0].shape[1]
    return pl.pallas_call(
        second_kernel,
        out_shape=jax.ShapeDtypeStruct((rows, width), BF16),
        in_specs=[VMEM, ANY] + [VMEM] * len(heads),
        out_specs=VMEM,
        compiler_params=PARAMS,
        cost_estimate=gradient_cost(rows, columns, width),
        name="second_message",
    )(dlogits, first, *heads)


def staying_kernel(which_ref, first_ref, *refs):
    heads, (out_ref, held_ref, sem) = refs[:-3], refs[-3:]
    width = held_ref.shape[1]
    depth = width // 2
    columns = first_ref.shape[1] - depth
    mine = pl.multiple_of(which_ref[0] * width, 128)
    other = pl.multiple_of((1 - which_ref[0]) * width, 128)
    copies = [
        pltpu.make_async_copy(
            first_ref.at[:, pl.ds(columns, depth)], out_ref.at[:, pl.ds(other, depth)], sem.at[0]
        )
    ]
    copies[0].start()
    dlogits = first_ref[:, :columns]
    for i in range(2):
        multiplied(dlogits, heads[i::2], held_ref, i * depth)
        copies.append(
            pltpu.make_async_copy(
                held_ref.at[:, pl.ds(i * depth, depth)],
                out_ref.at[:, pl.ds(pl.multiple_of(mine + i * depth, 128), depth)],
                sem.at[i + 1],
            )
        )
        copies[-1].start()
    for copy in copies:
        copy.wait()


def staying_gradient(which, first, heads):
    rows = first.shape[0]
    depth = heads[0].shape[1]
    columns = first.shape[1] - depth
    return pl.pallas_call(
        staying_kernel,
        out_shape=jax.ShapeDtypeStruct((rows, 4 * depth), BF16),
        in_specs=[SMEM] + [VMEM] * (1 + len(heads)),
        out_specs=HBM,
        scratch_shapes=[pltpu.VMEM((rows, 2 * depth), BF16), pltpu.SemaphoreType.DMA((3,))],
        compiler_params=PARAMS,
        cost_estimate=gradient_cost(rows, columns, 2 * depth),
        name="staying_gradient",
    )(which, first, *heads)


def placed_kernel(which_ref, second_ref, _, out_ref, sem):
    rows, depth = second_ref.shape
    start = pl.multiple_of((1 - which_ref[0]) * (2 * depth) + depth, 128)
    copies = []
    for i in range(4):
        part = pl.ds(i * (rows // 4), rows // 4)
        target = out_ref.at[part, pl.ds(start, depth)]
        copies.append(pltpu.make_async_copy(second_ref.at[part, :], target, sem.at[i]))
    for copy in copies:
        copy.start()
    for copy in copies:
        copy.wait()


def placed_beside(which, second, gradient):
    return pl.pallas_call(
        placed_kernel,
        out_shape=jax.ShapeDtypeStruct(gradient.shape, gradient.dtype),
        in_specs=[SMEM, VMEM, HBM],
        out_specs=HBM,
        scratch_shapes=[pltpu.SemaphoreType.DMA((4,))],
        input_output_aliases={2: 0},
        compiler_params=PARAMS,
        name="place_second",
    )(which, second, gradient)


def body(hidden, head_weight, tokens, rewards, group_ids):
    shards = lax.axis_size("vocab")
    which = (lax.axis_index("section") % 2).reshape(1)
    shard = lax.axis_index("vocab").reshape(1)
    near = [o for o in range(shards) if bin(o).count("1") <= 1]
    far = [o for o in range(shards) if bin(o).count("1") > 1]

    axes = ("vocab", "section")
    count = lax.axis_size(axes)
    own = jnp.stack([rewards, (group_ids + 1).astype(F32)])
    beside = [(i, i + 1) for i in range(1, count - 1, 2)]
    pieces = tuple(take(which, head_weight, 2))
    late_hidden, _ = lax.optimization_barrier((hidden, pieces))
    (other_half,) = take(1 - which, late_hidden, 1)
    other_half, late_pieces = lax.optimization_barrier((other_half, pieces))
    heads = gathered(pieces, late_pieces, "vocab")
    partner_half = swapped(other_half, "section", 1)

    rows = turned(which, hidden, partner_half)
    mine, theirs = [], []
    for offsets, facts in ((near, (own,)), (far, ())):
        pieces = [piece for o in offsets for piece in heads[o]]
        kept, sent, *again = partial_scores(rows, pieces, facts)
        mine.append(kept)
        theirs.append(swapped(sent, "section", 1))
    late_own, kept = lax.optimization_barrier((own, kept))
    mine[-1] = kept
    outer = lax.ppermute(late_own, axes, beside + [(b, a) for a, b in beside])
    mine, theirs = in_order(mine, near + far, 0), in_order(theirs, near + far, BELOW)
    logits, logprob, entropy, dlogits = loss(
        shard, tokens[None, :], own, outer, mine, theirs, shards
    )
    for i, offset in enumerate(far):
        heads[offset] = again[2 * i : 2 * i + 2]
    pieces = [piece for pair in heads for piece in pair]
    first = first_message(dlogits, pieces[0::2])
    first_in = swapped(first, "section", 1)
    second_in = swapped(second_message(dlogits, first, pieces[1::2]), "section", 1)
    staying = staying_gradient(which, first_in, pieces)
    previous_grad = placed_beside(which, second_in, staying)
    return (logits, logprob[0], entropy[0], previous_grad)


def in_order(blocks, order, below):
    if order == sorted(order):
        return blocks
    first = blocks[0]
    kept = first.shape[0] - below
    whole = jnp.concatenate([first[:kept], *blocks[1:]], axis=0)
    width = whole.shape[0] // len(order)
    parts = {offset: whole[i * width : (i + 1) * width] for i, offset in enumerate(order)}
    return [jnp.concatenate([parts[offset] for offset in sorted(order)] + [first[kept:]], axis=0)]


def solution(mesh):
    placed = (
        P(("seq", "vocab", "section"), None),
        P(("seq", "vocab"), None),
        P(("seq", "vocab", "section")),
        P(("seq", "vocab", "section")),
        P(("seq", "vocab", "section")),
    )
    return jax.shard_map(
        body,
        mesh=mesh,
        in_specs=placed,
        out_specs=(
            P(("seq", "vocab", "section"), None),
            P(("seq", "vocab", "section")),
            P(("seq", "vocab", "section")),
            P(("seq", "vocab", "section"), None),
        ),
        check_vma=False,
    )
```

```python
import functools

import jax
import jax.numpy as jnp
from jax import lax
from jax.experimental import pallas as pl
from jax.experimental.pallas import tpu as pltpu
from jax.sharding import PartitionSpec as P

F32, BF16 = jnp.float32, jnp.bfloat16
HBM = pl.BlockSpec(memory_space=pltpu.HBM)
ANY = pl.BlockSpec(memory_space=pl.ANY)
SMEM = pl.BlockSpec(memory_space=pltpu.SMEM)
VMEM = pl.BlockSpec(memory_space=pltpu.VMEM)
PARAMS = pltpu.CompilerParams(vmem_limit_bytes=4 * 1024 * 1024)
BELOW = 8


def swapped(value, axis, mask):
    pairs = [(source, source ^ mask) for source in range(lax.axis_size(axis))]
    return lax.ppermute(value, axis, pairs)


def gathered(first_wave, second_wave, axis):
    count = lax.axis_size(axis)
    masks = [1 << bit for bit in range((count - 1).bit_length())]
    uppers, lowers = {0: first_wave[0]}, {0: first_wave[1]}
    for mask in masks:
        early = mask == masks[0]
        uppers[mask] = swapped((first_wave if early else second_wave)[0], axis, mask)
    for mask in reversed(masks):
        early = mask == masks[-1]
        lowers[mask] = swapped((first_wave if early else second_wave)[1], axis, mask)
    for offset in sorted(range(1, count), key=lambda o: (bin(o).count("1"), o)):
        if offset in uppers:
            continue
        bits = [mask for mask in masks if offset & mask]
        uppers[offset] = swapped(uppers[offset ^ bits[-1]], axis, bits[-1])
        lowers[offset] = swapped(lowers[offset ^ bits[0]], axis, bits[0])
    return [(uppers[offset], lowers[offset]) for offset in range(count)]


def take_kernel(which_ref, value_ref, *refs):
    outs, sem = refs[:-1], refs[-1]
    width = outs[0].shape[1]
    start = which_ref[0] * width * len(outs)
    copies = []
    for i, out in enumerate(outs):
        source = value_ref.at[:, pl.ds(pl.multiple_of(start + i * width, 128), width)]
        copies.append(pltpu.make_async_copy(source, out, sem.at[i]))
    for copy in copies:
        copy.start()
    for copy in copies:
        copy.wait()


def take(which, value, pieces):
    rows, width = value.shape[0], value.shape[1] // 2 // pieces
    return pl.pallas_call(
        take_kernel,
        out_shape=[jax.ShapeDtypeStruct((rows, width), value.dtype)] * pieces,
        in_specs=[SMEM, ANY],
        out_specs=[ANY] * pieces,
        scratch_shapes=[pltpu.SemaphoreType.DMA((pieces,))],
        compiler_params=PARAMS,
        cost_estimate=pl.CostEstimate(
            flops=0, bytes_accessed=value.size * value.dtype.itemsize, transcendentals=0
        ),
        name="take_half",
    )(which, value)


def turned_kernel(which_ref, hidden_ref, partner_ref, out_ref):
    rows, width = partner_ref.shape
    block = 256
    for i in range(width // block):
        start = which_ref[0] * width + i * block
        own = hidden_ref[:, pl.ds(pl.multiple_of(start, 128), block)]
        out_ref[i * block : (i + 1) * block, :rows] = own.T
        part = slice(i * block, (i + 1) * block)
        out_ref[part, rows:] = partner_ref[:, part].T


def turned(which, hidden, partner_half):
    rows, width = partner_half.shape
    return pl.pallas_call(
        turned_kernel,
        out_shape=jax.ShapeDtypeStruct((width, 2 * rows), BF16),
        in_specs=[SMEM] + [VMEM] * 2,
        out_specs=VMEM,
        compiler_params=PARAMS,
        cost_estimate=pl.CostEstimate(
            flops=0, bytes_accessed=8 * rows * width, transcendentals=0
        ),
        name="turned_rows",
    )(which, hidden, partner_half)


def partial_kernel(facts, count, turned_ref, *refs):
    heads, (mine_ref, theirs_ref) = refs[facts : facts + count], refs[facts + count :][:2]
    for held, ref in zip(refs[facts + count + 2 :], heads):
        held[...] = ref[...]
    shard_rows, depth = heads[0].shape
    rows = mine_ref.shape[1]
    for i in range(len(heads) // 2):
        total = jnp.dot(heads[2 * i][...], turned_ref[:depth, :], preferred_element_type=F32)
        total += jnp.dot(heads[2 * i + 1][...], turned_ref[depth:, :], preferred_element_type=F32)
        mine_ref[i * shard_rows : (i + 1) * shard_rows, :] = total[:, :rows]
        theirs_ref[i * shard_rows : (i + 1) * shard_rows, :] = total[:, rows:]
    if facts:
        below = theirs_ref.shape[0] - mine_ref.shape[0]
        theirs_ref[mine_ref.shape[0] :, :] = jnp.zeros((below, rows), F32)
        theirs_ref[pl.ds(mine_ref.shape[0], refs[0].shape[0]), :] = refs[0][...]


def partial_scores(turned_rows, heads, facts=()):
    width, rows = turned_rows.shape
    columns = sum(head.shape[0] for head in heads) // 2
    below = BELOW * len(facts)
    return pl.pallas_call(
        functools.partial(partial_kernel, len(facts), len(heads)),
        out_shape=[
            jax.ShapeDtypeStruct((columns, rows // 2), F32),
            jax.ShapeDtypeStruct((columns + below, rows // 2), F32),
            *[jax.ShapeDtypeStruct(head.shape, head.dtype) for head in heads if not facts],
        ],
        in_specs=[VMEM] * (1 + len(facts) + len(heads)),
        out_specs=[VMEM] * (2 if facts else 2 + len(heads)),
        compiler_params=PARAMS,
        cost_estimate=pl.CostEstimate(
            flops=2 * rows * columns * width,
            bytes_accessed=2 * width * (rows + columns),
            transcendentals=0,
        ),
        name="partial_scores",
    )(turned_rows, *facts, *heads)


def advantage_kernel(partner_ref, own_ref, outer_ref, out_ref):
    rows = own_ref.shape[1]
    partner = partner_ref[partner_ref.shape[0] - BELOW :, :]
    eye = lax.broadcasted_iota(jnp.int32, (rows, rows), 0) == lax.broadcasted_iota(
        jnp.int32, (rows, rows), 1
    )

    def upright(row):
        return jnp.sum(jnp.where(eye, row, 0.0), axis=1, keepdims=True)

    groups = upright(partner[1:2, :])
    sums, counts = jnp.zeros((rows, 1), F32), jnp.zeros((rows, 1), F32)
    for facts in (partner, own_ref[...], outer_ref[...]):
        member = facts[1:2, :] == groups
        sums += jnp.sum(jnp.where(member, facts[0:1, :], 0.0), axis=1, keepdims=True)
        counts += jnp.sum(jnp.where(member, 1.0, 0.0), axis=1, keepdims=True)
    out_ref[...] = jnp.broadcast_to(upright(partner[0:1, :]) - sums / counts, (rows, rows))


def advantages(partner, own, outer):
    rows = own.shape[1]
    return pl.pallas_call(
        advantage_kernel,
        out_shape=jax.ShapeDtypeStruct((rows, rows), F32),
        in_specs=[VMEM] * 3,
        out_specs=VMEM,
        compiler_params=PARAMS,
        cost_estimate=pl.CostEstimate(flops=20 * 10**9, bytes_accessed=0, transcendentals=0),
        name="advantage",
    )(partner, own, outer)


def loss_kernel(parts, shards, shard_ref, tokens_ref, *refs):
    mine, theirs = refs[:parts], refs[parts : 2 * parts]
    logits_ref, logprob_ref, entropy_ref, dlogits_ref = refs[2 * parts :]
    shard = shard_ref[0]
    rows, columns = dlogits_ref.shape
    shard_rows = columns // shards

    lengths = [ref.shape[0] for ref in mine]
    scores = jnp.concatenate(
        [a[...] + b[:n, :] for a, b, n in zip(mine, theirs, lengths)], axis=0
    )
    tokens = tokens_ref[...]
    relative = ((tokens // shard_rows) ^ shard) * shard_rows + tokens % shard_rows
    chosen = lax.broadcasted_iota(jnp.int32, (columns, rows), 0) == relative
    row_max = jnp.max(scores, axis=0, keepdims=True)
    unnormed = jnp.exp(scores - row_max)
    denominator = jnp.sum(unnormed, axis=0, keepdims=True)
    probabilities = unnormed / denominator
    dlogits = probabilities - jnp.where(chosen, 1.0, 0.0)
    for i in range(shards):
        block = slice(i * shard_rows, (i + 1) * shard_rows)
        dlogits_ref[:, block] = dlogits[block, :].T.astype(BF16)
        place = pl.multiple_of((shard ^ i) * shard_rows, 128)
        logits_ref[:, pl.ds(place, shard_rows)] = scores[block, :].T.astype(BF16)
    log_total = row_max + jnp.log(denominator)
    picked = jnp.sum(jnp.where(chosen, scores, 0.0), axis=0, keepdims=True)
    logprob_ref[...] = picked - log_total
    entropy_ref[...] = log_total - jnp.sum(probabilities * scores, axis=0, keepdims=True)


def loss(shard, tokens, mine, theirs, shards):
    rows = tokens.shape[1]
    columns = sum(part.shape[0] for part in mine)
    flat = jax.ShapeDtypeStruct((1, rows), F32)
    wide = jax.ShapeDtypeStruct((rows, columns), BF16)
    return pl.pallas_call(
        functools.partial(loss_kernel, len(mine), shards),
        out_shape=[wide, flat, flat, wide],
        in_specs=[SMEM] + [VMEM] * (1 + 2 * len(mine)),
        out_specs=[VMEM] * 4,
        compiler_params=pltpu.CompilerParams(vmem_limit_bytes=2 * 1024**2 + 32 * rows * columns),
        cost_estimate=pl.CostEstimate(
            flops=10 * rows * columns,
            bytes_accessed=12 * rows * columns,
            transcendentals=rows * columns,
        ),
        name="loss",
    )(shard, tokens, *mine, *theirs)


def scaling(advantage, width):
    return jnp.concatenate([advantage] * (width // advantage.shape[1]), axis=1)


def multiplied(dlogits, heads, out_ref, start, scale=None):
    block = 256
    scale = None if scale is None else scaling(scale, block)
    for j in range(heads[0].shape[1] // block):
        part = slice(j * block, (j + 1) * block)
        head = jnp.concatenate([ref[:, part] for ref in heads], axis=0)
        product = jnp.dot(dlogits, head, preferred_element_type=F32)
        product = product if scale is None else product * scale
        out_ref[:, start + j * block : start + (j + 1) * block] = product.astype(BF16)


def gradient_cost(rows, columns, width):
    return pl.CostEstimate(
        flops=2 * rows * columns * width,
        bytes_accessed=2 * width * (rows + columns),
        transcendentals=0,
    )


def first_kernel(dlogits_ref, *refs):
    heads, out_ref = refs[:-1], refs[-1]
    columns = dlogits_ref.shape[1]
    out_ref[:, :columns] = dlogits_ref[...]
    multiplied(dlogits_ref[...], heads, out_ref, columns)


def first_message(dlogits, heads):
    rows, columns = dlogits.shape
    width = heads[0].shape[1]
    return pl.pallas_call(
        first_kernel,
        out_shape=jax.ShapeDtypeStruct((rows, columns + width), BF16),
        in_specs=[VMEM] * (1 + len(heads)),
        out_specs=VMEM,
        compiler_params=PARAMS,
        cost_estimate=gradient_cost(rows, columns, width),
        name="first_message",
    )(dlogits, *heads)


def second_kernel(dlogits_ref, _, *refs):
    multiplied(dlogits_ref[...], refs[:-1], refs[-1], 0)


def second_message(dlogits, first, heads):
    rows, columns = dlogits.shape
    width = heads[0].shape[1]
    return pl.pallas_call(
        second_kernel,
        out_shape=jax.ShapeDtypeStruct((rows, width), BF16),
        in_specs=[VMEM, ANY] + [VMEM] * len(heads),
        out_specs=VMEM,
        compiler_params=PARAMS,
        cost_estimate=gradient_cost(32 * rows, columns, width),
        name="second_message",
    )(dlogits, first, *heads)


def scaled(message_ref, advantage, columns, out_ref, start):
    block = 256
    scale = scaling(advantage, block)
    for j in range(0, columns.stop - columns.start, block):
        value = message_ref[:, columns.start + j : columns.start + j + block].astype(F32)
        out_ref[:, start + j : start + j + block] = (value * scale).astype(BF16)


def staying_kernel(which_ref, first_ref, advantage_ref, *refs):
    heads, (out_ref, held_ref, sem) = refs[:-3], refs[-3:]
    depth = held_ref.shape[1] // 3
    width = 2 * depth
    columns = first_ref.shape[1] - depth
    mine = pl.multiple_of(which_ref[0] * width, 128)
    other = pl.multiple_of((1 - which_ref[0]) * width, 128)
    advantage = advantage_ref[...]
    copies = []

    def put(i, place):
        source = held_ref.at[:, pl.ds(i * depth, depth)]
        target = out_ref.at[:, pl.ds(pl.multiple_of(place, 128), depth)]
        copies.append(pltpu.make_async_copy(source, target, sem.at[i]))
        copies[-1].start()

    scaled(first_ref, advantage, slice(columns, columns + depth), held_ref, 0)
    put(0, other)
    dlogits = first_ref[:, :columns]
    for i in range(2):
        multiplied(dlogits, heads[i::2], held_ref, (i + 1) * depth, advantage)
        put(i + 1, mine + i * depth)
    for copy in copies:
        copy.wait()


def staying_gradient(which, first, advantage, heads):
    rows = first.shape[0]
    depth = heads[0].shape[1]
    columns = first.shape[1] - depth
    return pl.pallas_call(
        staying_kernel,
        out_shape=jax.ShapeDtypeStruct((rows, 4 * depth), BF16),
        in_specs=[SMEM] + [VMEM] * (2 + len(heads)),
        out_specs=HBM,
        scratch_shapes=[pltpu.VMEM((rows, 3 * depth), BF16), pltpu.SemaphoreType.DMA((3,))],
        compiler_params=PARAMS,
        cost_estimate=gradient_cost(rows, columns, 2 * depth),
        name="staying_gradient",
    )(which, first, advantage, *heads)


def placed_kernel(which_ref, second_ref, advantage_ref, _, out_ref, held_ref, sem):
    depth = second_ref.shape[1]
    parts = 5 if depth % 1280 == 0 else 1
    width = depth // parts
    start = (1 - which_ref[0]) * (2 * depth) + depth
    copies = []
    for i in range(parts):
        part = slice(i * width, (i + 1) * width)
        scaled(second_ref, advantage_ref[...], part, held_ref, i * width)
        target = out_ref.at[:, pl.ds(pl.multiple_of(start + i * width, 128), width)]
        copies.append(
            pltpu.make_async_copy(held_ref.at[:, pl.ds(i * width, width)], target, sem.at[i])
        )
        copies[-1].start()
    for copy in copies:
        copy.wait()


def placed_beside(which, second, advantage, gradient):
    return pl.pallas_call(
        placed_kernel,
        out_shape=jax.ShapeDtypeStruct(gradient.shape, gradient.dtype),
        in_specs=[SMEM, VMEM, VMEM, HBM],
        out_specs=HBM,
        scratch_shapes=[pltpu.VMEM(second.shape, BF16), pltpu.SemaphoreType.DMA((5,))],
        input_output_aliases={3: 0},
        compiler_params=PARAMS,
        name="place_second",
    )(which, second, advantage, gradient)


def body(hidden, head_weight, tokens, rewards, group_ids):
    shards = lax.axis_size("vocab")
    which = (lax.axis_index("section") % 2).reshape(1)
    shard = lax.axis_index("vocab").reshape(1)
    near = [o for o in range(shards) if bin(o).count("1") <= 1]
    far = [o for o in range(shards) if bin(o).count("1") > 1]

    own = jnp.stack([rewards, (group_ids + 1).astype(F32)])
    pieces = tuple(take(which, head_weight, 2))
    late_hidden, _ = lax.optimization_barrier((hidden, pieces))
    (other_half,) = take(1 - which, late_hidden, 1)
    other_half, late_pieces = lax.optimization_barrier((other_half, pieces))
    heads = gathered(pieces, late_pieces, "vocab")
    partner_half = swapped(other_half, "section", 1)

    rows = turned(which, hidden, partner_half)
    mine, theirs = [], []
    for offsets, facts in ((near, (own,)), (far, ())):
        pieces = [piece for o in offsets for piece in heads[o]]
        kept, sent, *again = partial_scores(rows, pieces, facts)
        mine.append(kept)
        theirs.append(swapped(sent, "section", 1))
    partner_facts = theirs[0]
    mine, theirs = in_order(mine, near + far, 0), in_order(theirs, near + far, BELOW)
    logits, logprob, entropy, dlogits = loss(
        shard, tokens[None, :], mine, theirs, shards
    )
    for i, offset in enumerate(far):
        heads[offset] = again[2 * i : 2 * i + 2]
    pieces = [piece for pair in heads for piece in pair]
    first = first_message(dlogits, pieces[0::2])
    first_in = swapped(first, "section", 1)
    second = second_message(dlogits, first, pieces[1::2])
    second_in = swapped(second, "section", 1)

    late_own, _ = lax.optimization_barrier((own, first))
    axes = ("vocab", "section")
    count = lax.axis_size(axes)
    beyond = [(i + 2, i) for i in range(0, count - 2, 2)] + [(i, i + 2) for i in range(1, count - 2, 2)]
    outer = lax.ppermute(late_own, axes, beyond)
    advantage = advantages(partner_facts, own, outer)
    staying = staying_gradient(which, first_in, advantage, pieces)
    previous_grad = placed_beside(which, second_in, advantage, staying)
    return (logits, logprob[0], entropy[0], previous_grad)


def in_order(blocks, order, below):
    if order == sorted(order):
        return blocks
    first = blocks[0]
    kept = first.shape[0] - below
    whole = jnp.concatenate([first[:kept], *blocks[1:]], axis=0)
    width = whole.shape[0] // len(order)
    parts = {offset: whole[i * width : (i + 1) * width] for i, offset in enumerate(order)}
    return [jnp.concatenate([parts[offset] for offset in sorted(order)] + [first[kept:]], axis=0)]


def solution(mesh):
    placed = (
        P(("seq", "vocab", "section"), None),
        P(("seq", "vocab"), None),
        P(("seq", "vocab", "section")),
        P(("seq", "vocab", "section")),
        P(("seq", "vocab", "section")),
    )
    return jax.shard_map(
        body,
        mesh=mesh,
        in_specs=placed,
        out_specs=(
            P(("seq", "vocab", "section"), None),
            P(("seq", "vocab", "section")),
            P(("seq", "vocab", "section")),
            P(("seq", "vocab", "section"), None),
        ),
        check_vma=False,
    )
```

```python
import functools

import jax
import jax.numpy as jnp
from jax import lax
from jax.experimental import pallas as pl
from jax.experimental.pallas import tpu as pltpu
from jax.sharding import PartitionSpec as P

F32, BF16 = jnp.float32, jnp.bfloat16
HBM = pl.BlockSpec(memory_space=pltpu.HBM)
ANY = pl.BlockSpec(memory_space=pl.ANY)
SMEM = pl.BlockSpec(memory_space=pltpu.SMEM)
VMEM = pl.BlockSpec(memory_space=pltpu.VMEM)
PARAMS = pltpu.CompilerParams(vmem_limit_bytes=4 * 1024 * 1024)
BELOW = 8


def swapped(value, axis, mask):
    pairs = [(source, source ^ mask) for source in range(lax.axis_size(axis))]
    return lax.ppermute(value, axis, pairs)


def gathered(first_wave, second_wave, axis):
    count = lax.axis_size(axis)
    masks = [1 << bit for bit in range((count - 1).bit_length())]
    uppers, lowers = {0: first_wave[0]}, {0: first_wave[1]}
    for mask in masks:
        early = mask == masks[0]
        uppers[mask] = swapped((first_wave if early else second_wave)[0], axis, mask)
    for mask in reversed(masks):
        early = mask == masks[-1]
        lowers[mask] = swapped((first_wave if early else second_wave)[1], axis, mask)
    for offset in sorted(range(1, count), key=lambda o: (bin(o).count("1"), o)):
        if offset in uppers:
            continue
        bits = [mask for mask in masks if offset & mask]
        uppers[offset] = swapped(uppers[offset ^ bits[-1]], axis, bits[-1])
        lowers[offset] = swapped(lowers[offset ^ bits[0]], axis, bits[0])
    return [(uppers[offset], lowers[offset]) for offset in range(count)]


def take_kernel(which_ref, value_ref, *refs):
    outs, sem = refs[:-1], refs[-1]
    width = outs[0].shape[1]
    start = which_ref[0] * width * len(outs)
    copies = []
    for i, out in enumerate(outs):
        source = value_ref.at[:, pl.ds(pl.multiple_of(start + i * width, 128), width)]
        copies.append(pltpu.make_async_copy(source, out, sem.at[i]))
    for copy in copies:
        copy.start()
    for copy in copies:
        copy.wait()


def take(which, value, pieces):
    rows, width = value.shape[0], value.shape[1] // 2 // pieces
    return pl.pallas_call(
        take_kernel,
        out_shape=[jax.ShapeDtypeStruct((rows, width), value.dtype)] * pieces,
        in_specs=[SMEM, ANY],
        out_specs=[ANY] * pieces,
        scratch_shapes=[pltpu.SemaphoreType.DMA((pieces,))],
        compiler_params=PARAMS,
        cost_estimate=pl.CostEstimate(
            flops=0, bytes_accessed=value.size * value.dtype.itemsize, transcendentals=0
        ),
        name="take_half",
    )(which, value)


def turned_kernel(which_ref, hidden_ref, partner_ref, out_ref):
    rows, width = partner_ref.shape
    block = 256
    for i in range(width // block):
        start = which_ref[0] * width + i * block
        own = hidden_ref[:, pl.ds(pl.multiple_of(start, 128), block)]
        out_ref[i * block : (i + 1) * block, :rows] = own.T
        part = slice(i * block, (i + 1) * block)
        out_ref[part, rows:] = partner_ref[:, part].T


def turned(which, hidden, partner_half):
    rows, width = partner_half.shape
    return pl.pallas_call(
        turned_kernel,
        out_shape=jax.ShapeDtypeStruct((width, 2 * rows), BF16),
        in_specs=[SMEM] + [VMEM] * 2,
        out_specs=VMEM,
        compiler_params=PARAMS,
        cost_estimate=pl.CostEstimate(
            flops=0, bytes_accessed=8 * rows * width, transcendentals=0
        ),
        name="turned_rows",
    )(which, hidden, partner_half)


def partial_kernel(facts, count, turned_ref, *refs):
    heads, (mine_ref, theirs_ref) = refs[facts : facts + count], refs[facts + count :][:2]
    for held, ref in zip(refs[facts + count + 2 :], heads):
        held[...] = ref[...]
    shard_rows, depth = heads[0].shape
    rows = mine_ref.shape[1]
    for i in range(len(heads) // 2):
        total = jnp.dot(heads[2 * i][...], turned_ref[:depth, :], preferred_element_type=F32)
        total += jnp.dot(heads[2 * i + 1][...], turned_ref[depth:, :], preferred_element_type=F32)
        mine_ref[i * shard_rows : (i + 1) * shard_rows, :] = total[:, :rows]
        theirs_ref[i * shard_rows : (i + 1) * shard_rows, :] = total[:, rows:]
    if facts:
        below = theirs_ref.shape[0] - mine_ref.shape[0]
        theirs_ref[mine_ref.shape[0] :, :] = jnp.zeros((below, rows), F32)
        theirs_ref[pl.ds(mine_ref.shape[0], refs[0].shape[0]), :] = refs[0][...]


def partial_scores(turned_rows, heads, facts=()):
    width, rows = turned_rows.shape
    columns = sum(head.shape[0] for head in heads) // 2
    below = BELOW * len(facts)
    return pl.pallas_call(
        functools.partial(partial_kernel, len(facts), len(heads)),
        out_shape=[
            jax.ShapeDtypeStruct((columns, rows // 2), F32),
            jax.ShapeDtypeStruct((columns + below, rows // 2), F32),
            *[jax.ShapeDtypeStruct(head.shape, head.dtype) for head in heads if not facts],
        ],
        in_specs=[VMEM] * (1 + len(facts) + len(heads)),
        out_specs=[VMEM] * (2 if facts else 2 + len(heads)),
        compiler_params=PARAMS,
        cost_estimate=pl.CostEstimate(
            flops=2 * rows * columns * width,
            bytes_accessed=2 * width * (rows + columns),
            transcendentals=0,
        ),
        name="partial_scores",
    )(turned_rows, *facts, *heads)


def advantage_kernel(partner_ref, own_ref, outer_ref, out_ref):
    rows = own_ref.shape[1]
    partner = partner_ref[partner_ref.shape[0] - BELOW :, :]
    eye = lax.broadcasted_iota(jnp.int32, (rows, rows), 0) == lax.broadcasted_iota(
        jnp.int32, (rows, rows), 1
    )

    def upright(row):
        return jnp.sum(jnp.where(eye, row, 0.0), axis=1, keepdims=True)

    groups = upright(partner[1:2, :])
    sums, counts = jnp.zeros((rows, 1), F32), jnp.zeros((rows, 1), F32)
    for facts in (partner, own_ref[...], outer_ref[...]):
        member = facts[1:2, :] == groups
        sums += jnp.sum(jnp.where(member, facts[0:1, :], 0.0), axis=1, keepdims=True)
        counts += jnp.sum(jnp.where(member, 1.0, 0.0), axis=1, keepdims=True)
    out_ref[...] = jnp.broadcast_to(upright(partner[0:1, :]) - sums / counts, (rows, rows))


def advantages(partner, own, outer):
    rows = own.shape[1]
    return pl.pallas_call(
        advantage_kernel,
        out_shape=jax.ShapeDtypeStruct((rows, rows), F32),
        in_specs=[VMEM] * 3,
        out_specs=VMEM,
        compiler_params=PARAMS,
        cost_estimate=pl.CostEstimate(flops=20 * 10**9, bytes_accessed=0, transcendentals=0),
        name="advantage",
    )(partner, own, outer)


def softmax_of(shard, tokens, mine, theirs, shards):
    scores = jnp.concatenate(
        [a[...] + b[: a.shape[0], :] for a, b in zip(mine, theirs)], axis=0
    )
    columns, rows = scores.shape
    shard_rows = columns // shards
    relative = ((tokens // shard_rows) ^ shard) * shard_rows + tokens % shard_rows
    chosen = lax.broadcasted_iota(jnp.int32, (columns, rows), 0) == relative
    row_max = jnp.max(scores, axis=0, keepdims=True)
    unnormed = jnp.exp(scores - row_max)
    return scores, chosen, row_max, unnormed, jnp.sum(unnormed, axis=0, keepdims=True)


def outputs_kernel(parts, shards, shard_ref, tokens_ref, *refs):
    mine, theirs = refs[:parts], refs[parts : 2 * parts]
    logits_ref, logprob_ref, entropy_ref = refs[2 * parts :]
    scores, chosen, row_max, unnormed, denominator = softmax_of(
        shard_ref[0], tokens_ref[...], mine, theirs, shards
    )
    shard_rows = scores.shape[0] // shards
    for i in range(shards):
        block = slice(i * shard_rows, (i + 1) * shard_rows)
        place = pl.multiple_of((shard_ref[0] ^ i) * shard_rows, 128)
        logits_ref[:, pl.ds(place, shard_rows)] = scores[block, :].T.astype(BF16)
    log_total = row_max + jnp.log(denominator)
    picked = jnp.sum(jnp.where(chosen, scores, 0.0), axis=0, keepdims=True)
    logprob_ref[...] = picked - log_total
    probabilities = unnormed / denominator
    entropy_ref[...] = log_total - jnp.sum(probabilities * scores, axis=0, keepdims=True)


def softmax_params(rows, columns):
    return pltpu.CompilerParams(vmem_limit_bytes=2 * 1024**2 + 32 * rows * columns)


def outputs(shard, tokens, mine, theirs, shards):
    rows = tokens.shape[1]
    columns = sum(part.shape[0] for part in mine)
    flat = jax.ShapeDtypeStruct((1, rows), F32)
    return pl.pallas_call(
        functools.partial(outputs_kernel, len(mine), shards),
        out_shape=[jax.ShapeDtypeStruct((rows, columns), BF16), flat, flat],
        in_specs=[SMEM] + [VMEM] * (1 + 2 * len(mine)),
        out_specs=[VMEM] * 3,
        compiler_params=softmax_params(rows, columns),
        cost_estimate=pl.CostEstimate(
            flops=10 * rows * columns,
            bytes_accessed=12 * rows * columns,
            transcendentals=rows * columns,
        ),
        name="outputs",
    )(shard, tokens, *mine, *theirs)


def scaling(advantage, width):
    return jnp.concatenate([advantage] * (width // advantage.shape[1]), axis=1)


def multiplied(dlogits, heads, out_ref, start, scale=None):
    block = 256
    scale = None if scale is None else scaling(scale, block)
    for j in range(heads[0].shape[1] // block):
        part = slice(j * block, (j + 1) * block)
        head = jnp.concatenate([ref[:, part] for ref in heads], axis=0)
        product = jnp.dot(dlogits, head, preferred_element_type=F32)
        product = product if scale is None else product * scale
        out_ref[:, start + j * block : start + (j + 1) * block] = product.astype(BF16)


def gradient_cost(rows, columns, width):
    return pl.CostEstimate(
        flops=2 * rows * columns * width,
        bytes_accessed=2 * width * (rows + columns),
        transcendentals=0,
    )


def first_kernel(parts, shards, shard_ref, tokens_ref, *refs):
    mine, theirs = refs[:parts], refs[parts : 2 * parts]
    heads, out_ref = refs[2 * parts : -1], refs[-1]
    _, chosen, _, unnormed, denominator = softmax_of(
        shard_ref[0], tokens_ref[...], mine, theirs, shards
    )
    columns = unnormed.shape[0]
    shard_rows = columns // shards
    dlogits = unnormed / denominator - jnp.where(chosen, 1.0, 0.0)
    for i in range(shards):
        block = slice(i * shard_rows, (i + 1) * shard_rows)
        out_ref[:, block] = dlogits[block, :].T.astype(BF16)
    multiplied(out_ref[:, :columns], heads, out_ref, columns)


def first_message(shard, tokens, mine, theirs, heads, shards):
    rows = tokens.shape[1]
    columns = sum(part.shape[0] for part in mine)
    width = heads[0].shape[1]
    return pl.pallas_call(
        functools.partial(first_kernel, len(mine), shards),
        out_shape=jax.ShapeDtypeStruct((rows, columns + width), BF16),
        in_specs=[SMEM] + [VMEM] * (1 + 2 * len(mine) + len(heads)),
        out_specs=VMEM,
        compiler_params=softmax_params(rows, columns),
        cost_estimate=gradient_cost(rows, columns, width),
        name="first_message",
    )(shard, tokens, *mine, *theirs, *heads)


def second_kernel(first_ref, *refs):
    heads, out_ref = refs[:-1], refs[-1]
    columns = first_ref.shape[1] - heads[0].shape[1]
    multiplied(first_ref[:, :columns], heads, out_ref, 0)


def second_message(first, heads):
    rows, width = first.shape[0], heads[0].shape[1]
    columns = first.shape[1] - width
    return pl.pallas_call(
        second_kernel,
        out_shape=jax.ShapeDtypeStruct((rows, width), BF16),
        in_specs=[VMEM] * (1 + len(heads)),
        out_specs=VMEM,
        compiler_params=PARAMS,
        cost_estimate=gradient_cost(32 * rows, columns, width),
        name="second_message",
    )(first, *heads)


def scaled(message_ref, advantage, columns, out_ref, start):
    block = 256
    scale = scaling(advantage, block)
    for j in range(0, columns.stop - columns.start, block):
        value = message_ref[:, columns.start + j : columns.start + j + block].astype(F32)
        out_ref[:, start + j : start + j + block] = (value * scale).astype(BF16)


def staying_kernel(which_ref, first_ref, advantage_ref, *refs):
    heads, (out_ref, held_ref, sem) = refs[:-3], refs[-3:]
    depth = held_ref.shape[1] // 3
    width = 2 * depth
    columns = first_ref.shape[1] - depth
    mine = pl.multiple_of(which_ref[0] * width, 128)
    other = pl.multiple_of((1 - which_ref[0]) * width, 128)
    advantage = advantage_ref[...]
    copies = []

    def put(i, place):
        source = held_ref.at[:, pl.ds(i * depth, depth)]
        target = out_ref.at[:, pl.ds(pl.multiple_of(place, 128), depth)]
        copies.append(pltpu.make_async_copy(source, target, sem.at[i]))
        copies[-1].start()

    scaled(first_ref, advantage, slice(columns, columns + depth), held_ref, 0)
    put(0, other)
    dlogits = first_ref[:, :columns]
    for i in range(2):
        multiplied(dlogits, heads[i::2], held_ref, (i + 1) * depth, advantage)
        put(i + 1, mine + i * depth)
    for copy in copies:
        copy.wait()


def staying_gradient(which, first, advantage, heads):
    rows = first.shape[0]
    depth = heads[0].shape[1]
    columns = first.shape[1] - depth
    return pl.pallas_call(
        staying_kernel,
        out_shape=jax.ShapeDtypeStruct((rows, 4 * depth), BF16),
        in_specs=[SMEM] + [VMEM] * (2 + len(heads)),
        out_specs=HBM,
        scratch_shapes=[pltpu.VMEM((rows, 3 * depth), BF16), pltpu.SemaphoreType.DMA((3,))],
        compiler_params=PARAMS,
        cost_estimate=gradient_cost(rows, columns, 2 * depth),
        name="staying_gradient",
    )(which, first, advantage, *heads)


def placed_kernel(which_ref, second_ref, advantage_ref, _, out_ref, held_ref, sem):
    depth = second_ref.shape[1]
    parts = 5 if depth % 1280 == 0 else 1
    width = depth // parts
    start = (1 - which_ref[0]) * (2 * depth) + depth
    copies = []
    for i in range(parts):
        part = slice(i * width, (i + 1) * width)
        scaled(second_ref, advantage_ref[...], part, held_ref, i * width)
        target = out_ref.at[:, pl.ds(pl.multiple_of(start + i * width, 128), width)]
        copies.append(
            pltpu.make_async_copy(held_ref.at[:, pl.ds(i * width, width)], target, sem.at[i])
        )
        copies[-1].start()
    for copy in copies:
        copy.wait()


def placed_beside(which, second, advantage, gradient):
    return pl.pallas_call(
        placed_kernel,
        out_shape=jax.ShapeDtypeStruct(gradient.shape, gradient.dtype),
        in_specs=[SMEM, VMEM, VMEM, HBM],
        out_specs=HBM,
        scratch_shapes=[pltpu.VMEM(second.shape, BF16), pltpu.SemaphoreType.DMA((5,))],
        input_output_aliases={3: 0},
        compiler_params=PARAMS,
        name="place_second",
    )(which, second, advantage, gradient)


def body(hidden, head_weight, tokens, rewards, group_ids):
    shards = lax.axis_size("vocab")
    which = (lax.axis_index("section") % 2).reshape(1)
    shard = lax.axis_index("vocab").reshape(1)
    near = [o for o in range(shards) if bin(o).count("1") <= 1]
    far = [o for o in range(shards) if bin(o).count("1") > 1]

    own = jnp.stack([rewards, (group_ids + 1).astype(F32)])
    pieces = tuple(take(which, head_weight, 2))
    late_hidden, _ = lax.optimization_barrier((hidden, pieces))
    (other_half,) = take(1 - which, late_hidden, 1)
    other_half, late_pieces = lax.optimization_barrier((other_half, pieces))
    heads = gathered(pieces, late_pieces, "vocab")
    partner_half = swapped(other_half, "section", 1)

    rows = turned(which, hidden, partner_half)
    mine, theirs = [], []
    for offsets, facts in ((near, (own,)), (far, ())):
        pieces = [piece for o in offsets for piece in heads[o]]
        kept, sent, *again = partial_scores(rows, pieces, facts)
        mine.append(kept)
        theirs.append(swapped(sent, "section", 1))
    partner_facts = theirs[0]
    mine, theirs = in_order(mine, near + far, 0), in_order(theirs, near + far, BELOW)
    for i, offset in enumerate(far):
        heads[offset] = again[2 * i : 2 * i + 2]
    pieces = [piece for pair in heads for piece in pair]
    flat_tokens = tokens[None, :]
    first = first_message(shard, flat_tokens, mine, theirs, pieces[0::2], shards)
    first_in = swapped(first, "section", 1)
    second = second_message(first, pieces[1::2])
    second_in = swapped(second, "section", 1)

    late_own, late_tokens, _ = lax.optimization_barrier((own, flat_tokens, first))
    logits, logprob, entropy = outputs(shard, late_tokens, mine, theirs, shards)
    partner_facts, logits, logprob, entropy = lax.optimization_barrier(
        (partner_facts, logits, logprob, entropy)
    )
    axes = ("vocab", "section")
    count = lax.axis_size(axes)
    beyond = [(i + 2, i) for i in range(0, count - 2, 2)] + [(i, i + 2) for i in range(1, count - 2, 2)]
    outer = lax.ppermute(late_own, axes, beyond)
    advantage = advantages(partner_facts, own, outer)
    staying = staying_gradient(which, first_in, advantage, pieces)
    previous_grad = placed_beside(which, second_in, advantage, staying)
    return (logits, logprob[0], entropy[0], previous_grad)


def in_order(blocks, order, below):
    if order == sorted(order):
        return blocks
    first = blocks[0]
    kept = first.shape[0] - below
    whole = jnp.concatenate([first[:kept], *blocks[1:]], axis=0)
    width = whole.shape[0] // len(order)
    parts = {offset: whole[i * width : (i + 1) * width] for i, offset in enumerate(order)}
    return [jnp.concatenate([parts[offset] for offset in sorted(order)] + [first[kept:]], axis=0)]


def solution(mesh):
    placed = (
        P(("seq", "vocab", "section"), None),
        P(("seq", "vocab"), None),
        P(("seq", "vocab", "section")),
        P(("seq", "vocab", "section")),
        P(("seq", "vocab", "section")),
    )
    return jax.shard_map(
        body,
        mesh=mesh,
        in_specs=placed,
        out_specs=(
            P(("seq", "vocab", "section"), None),
            P(("seq", "vocab", "section")),
            P(("seq", "vocab", "section")),
            P(("seq", "vocab", "section"), None),
        ),
        check_vma=False,
    )
```

```python
import functools

import jax
import jax.numpy as jnp
from jax import lax
from jax.experimental import pallas as pl
from jax.experimental.pallas import tpu as pltpu
from jax.sharding import PartitionSpec as P

F32, BF16 = jnp.float32, jnp.bfloat16
HBM = pl.BlockSpec(memory_space=pltpu.HBM)
ANY = pl.BlockSpec(memory_space=pl.ANY)
SMEM = pl.BlockSpec(memory_space=pltpu.SMEM)
VMEM = pl.BlockSpec(memory_space=pltpu.VMEM)
PARAMS = pltpu.CompilerParams(vmem_limit_bytes=4 * 1024 * 1024)
BELOW = 8


def swapped(value, axis, mask):
    pairs = [(source, source ^ mask) for source in range(lax.axis_size(axis))]
    return lax.ppermute(value, axis, pairs)


def gathered(first_wave, second_wave, axis):
    count = lax.axis_size(axis)
    masks = [1 << bit for bit in range((count - 1).bit_length())]
    uppers, lowers = {0: first_wave[0]}, {0: first_wave[1]}
    for mask in masks:
        early = mask == masks[0]
        uppers[mask] = swapped((first_wave if early else second_wave)[0], axis, mask)
    for mask in reversed(masks):
        early = mask == masks[-1]
        lowers[mask] = swapped((first_wave if early else second_wave)[1], axis, mask)
    for offset in sorted(range(1, count), key=lambda o: (bin(o).count("1"), o)):
        if offset in uppers:
            continue
        bits = [mask for mask in masks if offset & mask]
        uppers[offset] = swapped(uppers[offset ^ bits[-1]], axis, bits[-1])
        lowers[offset] = swapped(lowers[offset ^ bits[0]], axis, bits[0])
    return [(uppers[offset], lowers[offset]) for offset in range(count)]


def take_kernel(which_ref, value_ref, *refs):
    outs, sem = refs[:-1], refs[-1]
    width = outs[0].shape[1]
    start = which_ref[0] * width * len(outs)
    copies = []
    for i, out in enumerate(outs):
        source = value_ref.at[:, pl.ds(pl.multiple_of(start + i * width, 128), width)]
        copies.append(pltpu.make_async_copy(source, out, sem.at[i]))
    for copy in copies:
        copy.start()
    for copy in copies:
        copy.wait()


def take(which, value, pieces):
    rows, width = value.shape[0], value.shape[1] // 2 // pieces
    return pl.pallas_call(
        take_kernel,
        out_shape=[jax.ShapeDtypeStruct((rows, width), value.dtype)] * pieces,
        in_specs=[SMEM, ANY],
        out_specs=[ANY] * pieces,
        scratch_shapes=[pltpu.SemaphoreType.DMA((pieces,))],
        compiler_params=PARAMS,
        cost_estimate=pl.CostEstimate(
            flops=0, bytes_accessed=value.size * value.dtype.itemsize, transcendentals=0
        ),
        name="take_half",
    )(which, value)


def turned_kernel(which_ref, hidden_ref, partner_ref, out_ref):
    rows, width = partner_ref.shape
    block = 256
    for i in range(width // block):
        start = which_ref[0] * width + i * block
        own = hidden_ref[:, pl.ds(pl.multiple_of(start, 128), block)]
        out_ref[i * block : (i + 1) * block, :rows] = own.T
        part = slice(i * block, (i + 1) * block)
        out_ref[part, rows:] = partner_ref[:, part].T


def turned(which, hidden, partner_half):
    rows, width = partner_half.shape
    return pl.pallas_call(
        turned_kernel,
        out_shape=jax.ShapeDtypeStruct((width, 2 * rows), BF16),
        in_specs=[SMEM] + [VMEM] * 2,
        out_specs=VMEM,
        compiler_params=PARAMS,
        cost_estimate=pl.CostEstimate(
            flops=0, bytes_accessed=8 * rows * width, transcendentals=0
        ),
        name="turned_rows",
    )(which, hidden, partner_half)


def partial_kernel(facts, count, turned_ref, *refs):
    heads, (mine_ref, theirs_ref) = refs[facts : facts + count], refs[facts + count :][:2]
    for held, ref in zip(refs[facts + count + 2 :], heads):
        held[...] = ref[...]
    shard_rows, depth = heads[0].shape
    rows = mine_ref.shape[1]
    for i in range(len(heads) // 2):
        total = jnp.dot(heads[2 * i][...], turned_ref[:depth, :], preferred_element_type=F32)
        total += jnp.dot(heads[2 * i + 1][...], turned_ref[depth:, :], preferred_element_type=F32)
        mine_ref[i * shard_rows : (i + 1) * shard_rows, :] = total[:, :rows]
        theirs_ref[i * shard_rows : (i + 1) * shard_rows, :] = total[:, rows:]
    if facts:
        below = theirs_ref.shape[0] - mine_ref.shape[0]
        theirs_ref[mine_ref.shape[0] :, :] = jnp.zeros((below, rows), F32)
        theirs_ref[pl.ds(mine_ref.shape[0], refs[0].shape[0]), :] = refs[0][...]


def partial_scores(turned_rows, heads, facts=()):
    width, rows = turned_rows.shape
    columns = sum(head.shape[0] for head in heads) // 2
    below = BELOW * len(facts)
    return pl.pallas_call(
        functools.partial(partial_kernel, len(facts), len(heads)),
        out_shape=[
            jax.ShapeDtypeStruct((columns, rows // 2), F32),
            jax.ShapeDtypeStruct((columns + below, rows // 2), F32),
            *[jax.ShapeDtypeStruct(head.shape, head.dtype) for head in heads if not facts],
        ],
        in_specs=[VMEM] * (1 + len(facts) + len(heads)),
        out_specs=[VMEM] * (2 if facts else 2 + len(heads)),
        compiler_params=PARAMS,
        cost_estimate=pl.CostEstimate(
            flops=2 * rows * columns * width,
            bytes_accessed=2 * width * (rows + columns),
            transcendentals=0,
        ),
        name="partial_scores",
    )(turned_rows, *facts, *heads)


def advantage_kernel(partner_ref, own_ref, outer_ref, out_ref):
    rows = own_ref.shape[1]
    partner = partner_ref[partner_ref.shape[0] - BELOW :, :]
    eye = lax.broadcasted_iota(jnp.int32, (rows, rows), 0) == lax.broadcasted_iota(
        jnp.int32, (rows, rows), 1
    )

    def upright(row):
        return jnp.sum(jnp.where(eye, row, 0.0), axis=1, keepdims=True)

    groups = upright(partner[1:2, :])
    sums, counts = jnp.zeros((rows, 1), F32), jnp.zeros((rows, 1), F32)
    for facts in (partner, own_ref[...], outer_ref[...]):
        member = facts[1:2, :] == groups
        sums += jnp.sum(jnp.where(member, facts[0:1, :], 0.0), axis=1, keepdims=True)
        counts += jnp.sum(jnp.where(member, 1.0, 0.0), axis=1, keepdims=True)
    out_ref[...] = jnp.broadcast_to(upright(partner[0:1, :]) - sums / counts, (rows, rows))


def advantages(partner, own, outer):
    rows = own.shape[1]
    return pl.pallas_call(
        advantage_kernel,
        out_shape=jax.ShapeDtypeStruct((rows, rows), F32),
        in_specs=[VMEM] * 3,
        out_specs=VMEM,
        compiler_params=PARAMS,
        cost_estimate=pl.CostEstimate(flops=20 * 10**9, bytes_accessed=0, transcendentals=0),
        name="advantage",
    )(partner, own, outer)


def softmax_of(shard, tokens, mine, theirs, shards):
    scores = jnp.concatenate(
        [a[...] + b[: a.shape[0], :] for a, b in zip(mine, theirs)], axis=0
    )
    columns, rows = scores.shape
    shard_rows = columns // shards
    relative = ((tokens // shard_rows) ^ shard) * shard_rows + tokens % shard_rows
    chosen = lax.broadcasted_iota(jnp.int32, (columns, rows), 0) == relative
    row_max = jnp.max(scores, axis=0, keepdims=True)
    unnormed = jnp.exp(scores - row_max)
    return scores, chosen, row_max, unnormed, jnp.sum(unnormed, axis=0, keepdims=True)


def outputs_kernel(parts, shards, shard_ref, tokens_ref, *refs):
    mine, theirs = refs[:parts], refs[parts : 2 * parts]
    logits_ref, logprob_ref, entropy_ref = refs[2 * parts :]
    scores, chosen, row_max, unnormed, denominator = softmax_of(
        shard_ref[0], tokens_ref[...], mine, theirs, shards
    )
    shard_rows = scores.shape[0] // shards
    for i in range(shards):
        block = slice(i * shard_rows, (i + 1) * shard_rows)
        place = pl.multiple_of((shard_ref[0] ^ i) * shard_rows, 128)
        logits_ref[:, pl.ds(place, shard_rows)] = scores[block, :].T.astype(BF16)
    log_total = row_max + jnp.log(denominator)
    picked = jnp.sum(jnp.where(chosen, scores, 0.0), axis=0, keepdims=True)
    logprob_ref[...] = picked - log_total
    probabilities = unnormed / denominator
    entropy_ref[...] = log_total - jnp.sum(probabilities * scores, axis=0, keepdims=True)


def softmax_params(rows, columns):
    return pltpu.CompilerParams(vmem_limit_bytes=1024**2 + 16 * rows * columns)


def outputs(shard, tokens, mine, theirs, shards):
    rows = tokens.shape[1]
    columns = sum(part.shape[0] for part in mine)
    flat = jax.ShapeDtypeStruct((1, rows), F32)
    return pl.pallas_call(
        functools.partial(outputs_kernel, len(mine), shards),
        out_shape=[jax.ShapeDtypeStruct((rows, columns), BF16), flat, flat],
        in_specs=[SMEM] + [VMEM] * (1 + 2 * len(mine)),
        out_specs=[VMEM] * 3,
        compiler_params=softmax_params(rows, columns),
        cost_estimate=pl.CostEstimate(
            flops=10 * rows * columns,
            bytes_accessed=12 * rows * columns,
            transcendentals=rows * columns,
        ),
        name="outputs",
    )(shard, tokens, *mine, *theirs)


def scaling(advantage, width):
    return jnp.concatenate([advantage] * (width // advantage.shape[1]), axis=1)


def multiplied(dlogits, heads, out_ref, start, scale=None):
    block = 256
    scale = None if scale is None else scaling(scale, block)
    for j in range(heads[0].shape[1] // block):
        part = slice(j * block, (j + 1) * block)
        head = jnp.concatenate([ref[:, part] for ref in heads], axis=0)
        product = jnp.dot(dlogits, head, preferred_element_type=F32)
        product = product if scale is None else product * scale
        out_ref[:, start + j * block : start + (j + 1) * block] = product.astype(BF16)


def gradient_cost(rows, columns, width):
    return pl.CostEstimate(
        flops=2 * rows * columns * width,
        bytes_accessed=2 * width * (rows + columns),
        transcendentals=0,
    )


def first_kernel(parts, shards, shard_ref, tokens_ref, *refs):
    mine, theirs = refs[:parts], refs[parts : 2 * parts]
    heads, out_ref = refs[2 * parts : 2 * parts + shards], refs[-1]
    _, chosen, _, unnormed, denominator = softmax_of(
        shard_ref[0], tokens_ref[...], mine, theirs, shards
    )
    columns = unnormed.shape[0]
    shard_rows = columns // shards
    dlogits = unnormed / denominator - jnp.where(chosen, 1.0, 0.0)
    for i in range(shards):
        block = slice(i * shard_rows, (i + 1) * shard_rows)
        out_ref[:, block] = dlogits[block, :].T.astype(BF16)
    multiplied(out_ref[:, :columns], heads, out_ref, columns)


def first_message(shard, tokens, mine, theirs, heads, shards):
    rows = tokens.shape[1]
    columns = sum(part.shape[0] for part in mine)
    width = heads[0].shape[1]
    return pl.pallas_call(
        functools.partial(first_kernel, len(mine), shards),
        out_shape=jax.ShapeDtypeStruct((rows, columns + width), BF16),
        in_specs=[SMEM] + [VMEM] * (1 + 2 * len(mine) + len(heads)),
        out_specs=VMEM,
        compiler_params=softmax_params(rows, columns),
        cost_estimate=gradient_cost(rows, columns, width),
        name="first_message",
    )(shard, tokens, *mine, *theirs, *heads)


def second_kernel(first_ref, *refs):
    heads, out_ref = refs[:-1], refs[-1]
    columns = first_ref.shape[1] - heads[0].shape[1]
    multiplied(first_ref[:, :columns], heads, out_ref, 0)


def second_message(first, heads):
    rows, width = first.shape[0], heads[0].shape[1]
    columns = first.shape[1] - width
    return pl.pallas_call(
        second_kernel,
        out_shape=jax.ShapeDtypeStruct((rows, width), BF16),
        in_specs=[VMEM] * (1 + len(heads)),
        out_specs=VMEM,
        compiler_params=PARAMS,
        cost_estimate=gradient_cost(32 * rows, columns, width),
        name="second_message",
    )(first, *heads)


def scaled(message_ref, advantage, columns, out_ref, start):
    block = 256
    scale = scaling(advantage, block)
    for j in range(0, columns.stop - columns.start, block):
        value = message_ref[:, columns.start + j : columns.start + j + block].astype(F32)
        out_ref[:, start + j : start + j + block] = (value * scale).astype(BF16)


def staying_kernel(which_ref, first_ref, advantage_ref, *refs):
    heads, (out_ref, held_ref, sem) = refs[:-3], refs[-3:]
    depth = held_ref.shape[1] // 3
    width = 2 * depth
    columns = first_ref.shape[1] - depth
    mine = pl.multiple_of(which_ref[0] * width, 128)
    other = pl.multiple_of((1 - which_ref[0]) * width, 128)
    advantage = advantage_ref[...]
    copies = []

    def put(i, place):
        source = held_ref.at[:, pl.ds(i * depth, depth)]
        target = out_ref.at[:, pl.ds(pl.multiple_of(place, 128), depth)]
        copies.append(pltpu.make_async_copy(source, target, sem.at[i]))
        copies[-1].start()

    scaled(first_ref, advantage, slice(columns, columns + depth), held_ref, 0)
    put(0, other)
    dlogits = first_ref[:, :columns]
    for i in range(2):
        multiplied(dlogits, heads[i::2], held_ref, (i + 1) * depth, advantage)
        put(i + 1, mine + i * depth)
    for copy in copies:
        copy.wait()


def staying_gradient(which, first, advantage, heads):
    rows = first.shape[0]
    depth = heads[0].shape[1]
    columns = first.shape[1] - depth
    return pl.pallas_call(
        staying_kernel,
        out_shape=jax.ShapeDtypeStruct((rows, 4 * depth), BF16),
        in_specs=[SMEM] + [VMEM] * (2 + len(heads)),
        out_specs=HBM,
        scratch_shapes=[pltpu.VMEM((rows, 3 * depth), BF16), pltpu.SemaphoreType.DMA((3,))],
        compiler_params=PARAMS,
        cost_estimate=gradient_cost(rows, columns, 2 * depth),
        name="staying_gradient",
    )(which, first, advantage, *heads)


def placed_kernel(which_ref, second_ref, advantage_ref, _, out_ref, held_ref, sem):
    depth = second_ref.shape[1]
    parts = 5 if depth % 1280 == 0 else 1
    width = depth // parts
    start = (1 - which_ref[0]) * (2 * depth) + depth
    copies = []
    for i in range(parts):
        part = slice(i * width, (i + 1) * width)
        scaled(second_ref, advantage_ref[...], part, held_ref, i * width)
        target = out_ref.at[:, pl.ds(pl.multiple_of(start + i * width, 128), width)]
        copies.append(
            pltpu.make_async_copy(held_ref.at[:, pl.ds(i * width, width)], target, sem.at[i])
        )
        copies[-1].start()
    for copy in copies:
        copy.wait()


def placed_beside(which, second, advantage, gradient):
    return pl.pallas_call(
        placed_kernel,
        out_shape=jax.ShapeDtypeStruct(gradient.shape, gradient.dtype),
        in_specs=[SMEM, VMEM, VMEM, HBM],
        out_specs=HBM,
        scratch_shapes=[pltpu.VMEM(second.shape, BF16), pltpu.SemaphoreType.DMA((5,))],
        input_output_aliases={3: 0},
        compiler_params=PARAMS,
        name="place_second",
    )(which, second, advantage, gradient)


def body(hidden, head_weight, tokens, rewards, group_ids):
    shards = lax.axis_size("vocab")
    which = (lax.axis_index("section") % 2).reshape(1)
    shard = lax.axis_index("vocab").reshape(1)
    near = [o for o in range(shards) if bin(o).count("1") <= 1]
    far = [o for o in range(shards) if bin(o).count("1") > 1]

    own = jnp.stack([rewards, (group_ids + 1).astype(F32)])
    pieces = tuple(take(which, head_weight, 2))
    late_hidden, _ = lax.optimization_barrier((hidden, pieces))
    (other_half,) = take(1 - which, late_hidden, 1)
    other_half, late_pieces = lax.optimization_barrier((other_half, pieces))
    heads = gathered(pieces, late_pieces, "vocab")
    partner_half = swapped(other_half, "section", 1)

    rows = turned(which, hidden, partner_half)
    mine, theirs = [], []
    for offsets, facts in ((near, (own,)), (far, ())):
        pieces = [piece for o in offsets for piece in heads[o]]
        kept, sent, *again = partial_scores(rows, pieces, facts)
        mine.append(kept)
        theirs.append(swapped(sent, "section", 1))
    partner_facts = theirs[0]
    mine, theirs = in_order(mine, near + far, 0), in_order(theirs, near + far, BELOW)
    for i, offset in enumerate(far):
        heads[offset] = again[2 * i : 2 * i + 2]
    pieces = [piece for pair in heads for piece in pair]
    flat_tokens = tokens[None, :]
    first = first_message(shard, flat_tokens, mine, theirs, pieces[0::2] + pieces[1::2], shards)
    first_in = swapped(first, "section", 1)
    second = second_message(first, pieces[1::2])
    second_in = swapped(second, "section", 1)

    late_own, late_tokens, _ = lax.optimization_barrier((own, flat_tokens, first))
    logits, logprob, entropy = outputs(shard, late_tokens, mine, theirs, shards)
    partner_facts, logits, logprob, entropy = lax.optimization_barrier(
        (partner_facts, logits, logprob, entropy)
    )
    axes = ("vocab", "section")
    count = lax.axis_size(axes)
    beyond = [(i + 2, i) for i in range(0, count - 2, 2)] + [(i, i + 2) for i in range(1, count - 2, 2)]
    outer = lax.ppermute(late_own, axes, beyond)
    advantage = advantages(partner_facts, own, outer)
    staying = staying_gradient(which, first_in, advantage, pieces)
    previous_grad = placed_beside(which, second_in, advantage, staying)
    return (logits, logprob[0], entropy[0], previous_grad)


def in_order(blocks, order, below):
    if order == sorted(order):
        return blocks
    first = blocks[0]
    kept = first.shape[0] - below
    whole = jnp.concatenate([first[:kept], *blocks[1:]], axis=0)
    width = whole.shape[0] // len(order)
    parts = {offset: whole[i * width : (i + 1) * width] for i, offset in enumerate(order)}
    return [jnp.concatenate([parts[offset] for offset in sorted(order)] + [first[kept:]], axis=0)]


def solution(mesh):
    placed = (
        P(("seq", "vocab", "section"), None),
        P(("seq", "vocab"), None),
        P(("seq", "vocab", "section")),
        P(("seq", "vocab", "section")),
        P(("seq", "vocab", "section")),
    )
    return jax.shard_map(
        body,
        mesh=mesh,
        in_specs=placed,
        out_specs=(
            P(("seq", "vocab", "section"), None),
            P(("seq", "vocab", "section")),
            P(("seq", "vocab", "section")),
            P(("seq", "vocab", "section"), None),
        ),
        check_vma=False,
    )
```

```python
import functools

import jax
import jax.numpy as jnp
from jax import lax
from jax.experimental import pallas as pl
from jax.experimental.pallas import tpu as pltpu
from jax.sharding import PartitionSpec as P

F32, BF16 = jnp.float32, jnp.bfloat16
HBM = pl.BlockSpec(memory_space=pltpu.HBM)
ANY = pl.BlockSpec(memory_space=pl.ANY)
SMEM = pl.BlockSpec(memory_space=pltpu.SMEM)
VMEM = pl.BlockSpec(memory_space=pltpu.VMEM)
PARAMS = pltpu.CompilerParams(vmem_limit_bytes=4 * 1024 * 1024)
BELOW = 8


def swapped(value, axis, mask):
    pairs = [(source, source ^ mask) for source in range(lax.axis_size(axis))]
    return lax.ppermute(value, axis, pairs)


def gathered(first_wave, second_wave, axis):
    count = lax.axis_size(axis)
    masks = [1 << bit for bit in range((count - 1).bit_length())]
    uppers, lowers = {0: first_wave[0]}, {0: first_wave[1]}
    for mask in masks:
        early = mask == masks[0]
        uppers[mask] = swapped((first_wave if early else second_wave)[0], axis, mask)
    for mask in reversed(masks):
        early = mask == masks[-1]
        lowers[mask] = swapped((first_wave if early else second_wave)[1], axis, mask)
    for offset in sorted(range(1, count), key=lambda o: (bin(o).count("1"), o)):
        if offset in uppers:
            continue
        bits = [mask for mask in masks if offset & mask]
        uppers[offset] = swapped(uppers[offset ^ bits[-1]], axis, bits[-1])
        lowers[offset] = swapped(lowers[offset ^ bits[0]], axis, bits[0])
    return [(uppers[offset], lowers[offset]) for offset in range(count)]


def take_kernel(count, which_ref, *refs):
    values, outs, sem = refs[:count], refs[count:-1], refs[-1]
    rows, width = values[0].shape[0], outs[0].shape[1]
    start = which_ref[0] * width * len(outs)
    copies = []
    for i, out in enumerate(outs):
        for j, value in enumerate(values):
            source = value.at[:, pl.ds(pl.multiple_of(start + i * width, 128), width)]
            target = out.at[pl.ds(j * rows, rows), :]
            copies.append(pltpu.make_async_copy(source, target, sem.at[i, j]))
    for copy in copies:
        copy.start()
    for copy in copies:
        copy.wait()


def take(which, values, pieces):
    rows, width = len(values) * values[0].shape[0], values[0].shape[1] // 2 // pieces
    return pl.pallas_call(
        functools.partial(take_kernel, len(values)),
        out_shape=[jax.ShapeDtypeStruct((rows, width), BF16)] * pieces,
        in_specs=[SMEM] + [ANY] * len(values),
        out_specs=[ANY] * pieces,
        scratch_shapes=[pltpu.SemaphoreType.DMA((pieces, len(values)))],
        compiler_params=PARAMS,
        cost_estimate=pl.CostEstimate(
            flops=0, bytes_accessed=4 * rows * width * pieces, transcendentals=0
        ),
        name="take_half",
    )(which, *values)


def turned_kernel(which_ref, hidden_ref, partner_ref, out_ref):
    rows, width = partner_ref.shape
    block = 256
    for i in range(width // block):
        start = which_ref[0] * width + i * block
        own = hidden_ref[:, pl.ds(pl.multiple_of(start, 128), block)]
        out_ref[i * block : (i + 1) * block, :rows] = own.T
        part = slice(i * block, (i + 1) * block)
        out_ref[part, rows:] = partner_ref[:, part].T


def turned(which, hidden, partner_half):
    rows, width = partner_half.shape
    return pl.pallas_call(
        turned_kernel,
        out_shape=jax.ShapeDtypeStruct((width, 2 * rows), BF16),
        in_specs=[SMEM] + [VMEM] * 2,
        out_specs=VMEM,
        compiler_params=PARAMS,
        cost_estimate=pl.CostEstimate(
            flops=0, bytes_accessed=8 * rows * width, transcendentals=0
        ),
        name="turned_rows",
    )(which, hidden, partner_half)


def partial_kernel(facts, count, turned_ref, *refs):
    heads, (mine_ref, theirs_ref) = refs[facts : facts + count], refs[facts + count :][:2]
    for held, ref in zip(refs[facts + count + 2 :], heads):
        held[...] = ref[...]
    shard_rows, depth = heads[0].shape
    rows = mine_ref.shape[1]
    for i in range(len(heads) // 2):
        total = jnp.dot(heads[2 * i][...], turned_ref[:depth, :], preferred_element_type=F32)
        total += jnp.dot(heads[2 * i + 1][...], turned_ref[depth:, :], preferred_element_type=F32)
        mine_ref[i * shard_rows : (i + 1) * shard_rows, :] = total[:, :rows]
        theirs_ref[i * shard_rows : (i + 1) * shard_rows, :] = total[:, rows:]
    if facts:
        below = theirs_ref.shape[0] - mine_ref.shape[0]
        theirs_ref[mine_ref.shape[0] :, :] = jnp.zeros((below, rows), F32)
        theirs_ref[pl.ds(mine_ref.shape[0], refs[0].shape[0]), :] = refs[0][...]


def partial_scores(turned_rows, heads, facts=()):
    width, rows = turned_rows.shape
    columns = sum(head.shape[0] for head in heads) // 2
    below = BELOW * len(facts)
    return pl.pallas_call(
        functools.partial(partial_kernel, len(facts), len(heads)),
        out_shape=[
            jax.ShapeDtypeStruct((columns, rows // 2), F32),
            jax.ShapeDtypeStruct((columns + below, rows // 2), F32),
            *[jax.ShapeDtypeStruct(head.shape, head.dtype) for head in heads if not facts],
        ],
        in_specs=[VMEM] * (1 + len(facts) + len(heads)),
        out_specs=[VMEM] * (2 if facts else 2 + len(heads)),
        compiler_params=PARAMS,
        cost_estimate=pl.CostEstimate(
            flops=2 * rows * columns * width,
            bytes_accessed=2 * width * (rows + columns),
            transcendentals=0,
        ),
        name="partial_scores",
    )(turned_rows, *facts, *heads)


def advantage_kernel(partner_ref, own_ref, outer_ref, out_ref):
    rows = own_ref.shape[1]
    partner = partner_ref[partner_ref.shape[0] - BELOW :, :]
    eye = lax.broadcasted_iota(jnp.int32, (rows, rows), 0) == lax.broadcasted_iota(
        jnp.int32, (rows, rows), 1
    )

    def upright(row):
        return jnp.sum(jnp.where(eye, row, 0.0), axis=1, keepdims=True)

    groups = upright(partner[1:2, :])
    sums, counts = jnp.zeros((rows, 1), F32), jnp.zeros((rows, 1), F32)
    for facts in (partner, own_ref[...], outer_ref[...]):
        member = facts[1:2, :] == groups
        sums += jnp.sum(jnp.where(member, facts[0:1, :], 0.0), axis=1, keepdims=True)
        counts += jnp.sum(jnp.where(member, 1.0, 0.0), axis=1, keepdims=True)
    out_ref[...] = jnp.broadcast_to(upright(partner[0:1, :]) - sums / counts, (rows, rows))


def advantages(partner, own, outer):
    rows = own.shape[1]
    return pl.pallas_call(
        advantage_kernel,
        out_shape=jax.ShapeDtypeStruct((rows, rows), F32),
        in_specs=[VMEM] * 3,
        out_specs=VMEM,
        compiler_params=PARAMS,
        cost_estimate=pl.CostEstimate(flops=20 * 10**9, bytes_accessed=0, transcendentals=0),
        name="advantage",
    )(partner, own, outer)


def softmax_of(shard, tokens, mine, theirs, shards):
    scores = jnp.concatenate(
        [a[...] + b[: a.shape[0], :] for a, b in zip(mine, theirs)], axis=0
    )
    columns, rows = scores.shape
    shard_rows = columns // shards
    relative = ((tokens // shard_rows) ^ shard) * shard_rows + tokens % shard_rows
    chosen = lax.broadcasted_iota(jnp.int32, (columns, rows), 0) == relative
    row_max = jnp.max(scores, axis=0, keepdims=True)
    unnormed = jnp.exp(scores - row_max)
    return scores, chosen, row_max, unnormed, jnp.sum(unnormed, axis=0, keepdims=True)


def outputs_kernel(parts, shards, shard_ref, tokens_ref, *refs):
    mine, theirs = refs[:parts], refs[parts : 2 * parts]
    logits_ref, logprob_ref, entropy_ref = refs[2 * parts :]
    scores, chosen, row_max, unnormed, denominator = softmax_of(
        shard_ref[0], tokens_ref[...], mine, theirs, shards
    )
    shard_rows = scores.shape[0] // shards
    for i in range(shards):
        block = slice(i * shard_rows, (i + 1) * shard_rows)
        place = pl.multiple_of((shard_ref[0] ^ i) * shard_rows, 128)
        logits_ref[:, pl.ds(place, shard_rows)] = scores[block, :].T.astype(BF16)
    log_total = row_max + jnp.log(denominator)
    picked = jnp.sum(jnp.where(chosen, scores, 0.0), axis=0, keepdims=True)
    logprob_ref[...] = picked - log_total
    probabilities = unnormed / denominator
    entropy_ref[...] = log_total - jnp.sum(probabilities * scores, axis=0, keepdims=True)


def softmax_params(rows, columns):
    return pltpu.CompilerParams(vmem_limit_bytes=1024**2 + 16 * rows * columns)


def outputs(shard, tokens, mine, theirs, shards):
    rows = tokens.shape[1]
    columns = sum(part.shape[0] for part in mine)
    flat = jax.ShapeDtypeStruct((1, rows), F32)
    return pl.pallas_call(
        functools.partial(outputs_kernel, len(mine), shards),
        out_shape=[jax.ShapeDtypeStruct((rows, columns), BF16), flat, flat],
        in_specs=[SMEM] + [VMEM] * (1 + 2 * len(mine)),
        out_specs=[VMEM] * 3,
        compiler_params=softmax_params(rows, columns),
        cost_estimate=pl.CostEstimate(
            flops=10 * rows * columns,
            bytes_accessed=12 * rows * columns,
            transcendentals=rows * columns,
        ),
        name="outputs",
    )(shard, tokens, *mine, *theirs)


def scaling(advantage, width):
    return jnp.concatenate([advantage] * (width // advantage.shape[1]), axis=1)


def multiplied(dlogits, heads, out_ref, start, scale=None):
    block = 256
    scale = None if scale is None else scaling(scale, block)
    for j in range(heads[0].shape[1] // block):
        part = slice(j * block, (j + 1) * block)
        head = jnp.concatenate([ref[:, part] for ref in heads], axis=0)
        product = jnp.dot(dlogits, head, preferred_element_type=F32)
        product = product if scale is None else product * scale
        out_ref[:, start + j * block : start + (j + 1) * block] = product.astype(BF16)


def gradient_cost(rows, columns, width):
    return pl.CostEstimate(
        flops=2 * rows * columns * width,
        bytes_accessed=2 * width * (rows + columns),
        transcendentals=0,
    )


def first_kernel(parts, shards, shard_ref, tokens_ref, *refs):
    mine, theirs = refs[:parts], refs[parts : 2 * parts]
    heads, out_ref = refs[2 * parts : 2 * parts + shards], refs[-1]
    _, chosen, _, unnormed, denominator = softmax_of(
        shard_ref[0], tokens_ref[...], mine, theirs, shards
    )
    columns = unnormed.shape[0]
    shard_rows = columns // shards
    dlogits = unnormed / denominator - jnp.where(chosen, 1.0, 0.0)
    for i in range(shards):
        block = slice(i * shard_rows, (i + 1) * shard_rows)
        out_ref[:, block] = dlogits[block, :].T.astype(BF16)
    multiplied(out_ref[:, :columns], heads, out_ref, columns)


def first_message(shard, tokens, mine, theirs, heads, shards):
    rows = tokens.shape[1]
    columns = sum(part.shape[0] for part in mine)
    width = heads[0].shape[1]
    return pl.pallas_call(
        functools.partial(first_kernel, len(mine), shards),
        out_shape=jax.ShapeDtypeStruct((rows, columns + width), BF16),
        in_specs=[SMEM] + [VMEM] * (1 + 2 * len(mine) + len(heads)),
        out_specs=VMEM,
        compiler_params=softmax_params(rows, columns),
        cost_estimate=gradient_cost(rows, columns, width),
        name="first_message",
    )(shard, tokens, *mine, *theirs, *heads)


def second_kernel(first_ref, *refs):
    heads, out_ref = refs[:-1], refs[-1]
    columns = first_ref.shape[1] - heads[0].shape[1]
    multiplied(first_ref[:, :columns], heads, out_ref, 0)


def second_message(first, heads):
    rows, width = first.shape[0], heads[0].shape[1]
    columns = first.shape[1] - width
    return pl.pallas_call(
        second_kernel,
        out_shape=jax.ShapeDtypeStruct((rows, width), BF16),
        in_specs=[VMEM] * (1 + len(heads)),
        out_specs=VMEM,
        compiler_params=PARAMS,
        cost_estimate=gradient_cost(32 * rows, columns, width),
        name="second_message",
    )(first, *heads)


def scaled(message_ref, advantage, columns, out_ref, start):
    block = 256
    scale = scaling(advantage, block)
    for j in range(0, columns.stop - columns.start, block):
        value = message_ref[:, columns.start + j : columns.start + j + block].astype(F32)
        out_ref[:, start + j : start + j + block] = (value * scale).astype(BF16)


def staying_kernel(which_ref, first_ref, advantage_ref, *refs):
    heads, (out_ref, held_ref, sem) = refs[:-3], refs[-3:]
    depth = held_ref.shape[1] // 3
    width = 2 * depth
    columns = first_ref.shape[1] - depth
    mine = pl.multiple_of(which_ref[0] * width, 128)
    other = pl.multiple_of((1 - which_ref[0]) * width, 128)
    advantage = advantage_ref[...]
    copies = []

    def put(i, place):
        source = held_ref.at[:, pl.ds(i * depth, depth)]
        target = out_ref.at[:, pl.ds(pl.multiple_of(place, 128), depth)]
        copies.append(pltpu.make_async_copy(source, target, sem.at[i]))
        copies[-1].start()

    scaled(first_ref, advantage, slice(columns, columns + depth), held_ref, 0)
    put(0, other)
    dlogits = first_ref[:, :columns]
    for i in range(2):
        multiplied(dlogits, heads[i::2], held_ref, (i + 1) * depth, advantage)
        put(i + 1, mine + i * depth)
    for copy in copies:
        copy.wait()


def staying_gradient(which, first, advantage, heads):
    rows = first.shape[0]
    depth = heads[0].shape[1]
    columns = first.shape[1] - depth
    return pl.pallas_call(
        staying_kernel,
        out_shape=jax.ShapeDtypeStruct((rows, 4 * depth), BF16),
        in_specs=[SMEM] + [VMEM] * (2 + len(heads)),
        out_specs=HBM,
        scratch_shapes=[pltpu.VMEM((rows, 3 * depth), BF16), pltpu.SemaphoreType.DMA((3,))],
        compiler_params=PARAMS,
        cost_estimate=gradient_cost(rows, columns, 2 * depth),
        name="staying_gradient",
    )(which, first, advantage, *heads)


def placed_kernel(which_ref, second_ref, advantage_ref, _, out_ref, held_ref, sem):
    depth = second_ref.shape[1]
    parts = 5 if depth % 1280 == 0 else 1
    width = depth // parts
    start = (1 - which_ref[0]) * (2 * depth) + depth
    copies = []
    for i in range(parts):
        part = slice(i * width, (i + 1) * width)
        scaled(second_ref, advantage_ref[...], part, held_ref, i * width)
        target = out_ref.at[:, pl.ds(pl.multiple_of(start + i * width, 128), width)]
        copies.append(
            pltpu.make_async_copy(held_ref.at[:, pl.ds(i * width, width)], target, sem.at[i])
        )
        copies[-1].start()
    for copy in copies:
        copy.wait()


def placed_beside(which, second, advantage, gradient):
    return pl.pallas_call(
        placed_kernel,
        out_shape=jax.ShapeDtypeStruct(gradient.shape, gradient.dtype),
        in_specs=[SMEM, VMEM, VMEM, HBM],
        out_specs=HBM,
        scratch_shapes=[pltpu.VMEM(second.shape, BF16), pltpu.SemaphoreType.DMA((5,))],
        input_output_aliases={3: 0},
        compiler_params=PARAMS,
        name="place_second",
    )(which, second, advantage, gradient)


def body(hidden, head_weight, tokens, rewards, group_ids):
    shards = lax.axis_size("vocab")
    which = (lax.axis_index("section") % 2).reshape(1)
    shard = lax.axis_index("vocab").reshape(1)
    near = [o for o in range(shards) if bin(o).count("1") <= 1]
    far = [o for o in range(shards) if bin(o).count("1") > 1]

    own = jnp.stack([rewards, (group_ids + 1).astype(F32)])
    middle = head_weight.shape[0] // 2
    pieces = tuple(take(which, (head_weight[:middle], head_weight[middle:]), 2))
    late_hidden, _ = lax.optimization_barrier((hidden, pieces))
    (other_half,) = take(1 - which, (late_hidden,), 1)
    other_half, late_pieces = lax.optimization_barrier((other_half, pieces))
    heads = gathered(pieces, late_pieces, "vocab")
    partner_half = swapped(other_half, "section", 1)

    rows = turned(which, hidden, partner_half)
    mine, theirs = [], []
    for offsets, facts in ((near, (own,)), (far, ())):
        pieces = [piece for o in offsets for piece in heads[o]]
        kept, sent, *again = partial_scores(rows, pieces, facts)
        mine.append(kept)
        theirs.append(swapped(sent, "section", 1))
    partner_facts = theirs[0]
    mine, theirs = in_order(mine, near + far, 0), in_order(theirs, near + far, BELOW)
    for i, offset in enumerate(far):
        heads[offset] = again[2 * i : 2 * i + 2]
    pieces = [piece for pair in heads for piece in pair]
    flat_tokens = tokens[None, :]
    first = first_message(shard, flat_tokens, mine, theirs, pieces[0::2] + pieces[1::2], shards)
    first_in = swapped(first, "section", 1)
    second = second_message(first, pieces[1::2])
    second_in = swapped(second, "section", 1)

    late_own, late_tokens, _ = lax.optimization_barrier((own, flat_tokens, first))
    logits, logprob, entropy = outputs(shard, late_tokens, mine, theirs, shards)
    partner_facts, logits, logprob, entropy = lax.optimization_barrier(
        (partner_facts, logits, logprob, entropy)
    )
    axes = ("vocab", "section")
    count = lax.axis_size(axes)
    beyond = [(i + 2, i) for i in range(0, count - 2, 2)] + [(i, i + 2) for i in range(1, count - 2, 2)]
    outer = lax.ppermute(late_own, axes, beyond)
    advantage = advantages(partner_facts, own, outer)
    staying = staying_gradient(which, first_in, advantage, pieces)
    previous_grad = placed_beside(which, second_in, advantage, staying)
    return (logits, logprob[0], entropy[0], previous_grad)


def in_order(blocks, order, below):
    if order == sorted(order):
        return blocks
    first = blocks[0]
    kept = first.shape[0] - below
    whole = jnp.concatenate([first[:kept], *blocks[1:]], axis=0)
    width = whole.shape[0] // len(order)
    parts = {offset: whole[i * width : (i + 1) * width] for i, offset in enumerate(order)}
    return [jnp.concatenate([parts[offset] for offset in sorted(order)] + [first[kept:]], axis=0)]


def solution(mesh):
    placed = (
        P(("seq", "vocab", "section"), None),
        P(("seq", "vocab"), None),
        P(("seq", "vocab", "section")),
        P(("seq", "vocab", "section")),
        P(("seq", "vocab", "section")),
    )
    return jax.shard_map(
        body,
        mesh=mesh,
        in_specs=placed,
        out_specs=(
            P(("seq", "vocab", "section"), None),
            P(("seq", "vocab", "section")),
            P(("seq", "vocab", "section")),
            P(("seq", "vocab", "section"), None),
        ),
        check_vma=False,
    )
```

```python
import functools

import jax
import jax.numpy as jnp
from jax import lax
from jax.experimental import pallas as pl
from jax.experimental.pallas import tpu as pltpu
from jax.sharding import PartitionSpec as P

F32, BF16 = jnp.float32, jnp.bfloat16
HBM = pl.BlockSpec(memory_space=pltpu.HBM)
ANY = pl.BlockSpec(memory_space=pl.ANY)
SMEM = pl.BlockSpec(memory_space=pltpu.SMEM)
VMEM = pl.BlockSpec(memory_space=pltpu.VMEM)
PARAMS = pltpu.CompilerParams(vmem_limit_bytes=4 * 1024 * 1024)
BELOW = 8


def swapped(value, axis, mask):
    pairs = [(source, source ^ mask) for source in range(lax.axis_size(axis))]
    return lax.ppermute(value, axis, pairs)


def gathered(first_wave, second_wave, axis):
    count = lax.axis_size(axis)
    masks = [1 << bit for bit in range((count - 1).bit_length())]
    uppers, lowers = {0: first_wave[0]}, {0: first_wave[1]}
    for mask in masks:
        early = mask == masks[0]
        uppers[mask] = swapped((first_wave if early else second_wave)[0], axis, mask)
    for mask in reversed(masks):
        early = mask == masks[-1]
        lowers[mask] = swapped((first_wave if early else second_wave)[1], axis, mask)
    for offset in sorted(range(1, count), key=lambda o: (bin(o).count("1"), o)):
        if offset in uppers:
            continue
        bits = [mask for mask in masks if offset & mask]
        uppers[offset] = swapped(uppers[offset ^ bits[-1]], axis, bits[-1])
        lowers[offset] = swapped(lowers[offset ^ bits[0]], axis, bits[0])
    return [(uppers[offset], lowers[offset]) for offset in range(count)]


def take_kernel(which_ref, value_ref, *refs):
    outs, sem = refs[:-1], refs[-1]
    width = outs[0].shape[1]
    start = which_ref[0] * width * len(outs)
    copies = []
    for i, out in enumerate(outs):
        source = value_ref.at[:, pl.ds(pl.multiple_of(start + i * width, 128), width)]
        copies.append(pltpu.make_async_copy(source, out, sem.at[i]))
    for copy in copies:
        copy.start()
    for copy in copies:
        copy.wait()


def take(which, value, pieces):
    rows, width = value.shape[0], value.shape[1] // 2 // pieces
    return pl.pallas_call(
        take_kernel,
        out_shape=[jax.ShapeDtypeStruct((rows, width), value.dtype)] * pieces,
        in_specs=[SMEM, ANY],
        out_specs=[ANY] * pieces,
        scratch_shapes=[pltpu.SemaphoreType.DMA((pieces,))],
        compiler_params=PARAMS,
        cost_estimate=pl.CostEstimate(
            flops=0, bytes_accessed=value.size * value.dtype.itemsize, transcendentals=0
        ),
        name="take_half",
    )(which, value)


def turned_kernel(which_ref, hidden_ref, partner_ref, out_ref):
    rows, width = partner_ref.shape
    block = 256
    for i in range(width // block):
        start = which_ref[0] * width + i * block
        own = hidden_ref[:, pl.ds(pl.multiple_of(start, 128), block)]
        out_ref[i * block : (i + 1) * block, :rows] = own.T
        part = slice(i * block, (i + 1) * block)
        out_ref[part, rows:] = partner_ref[:, part].T


def turned(which, hidden, partner_half):
    rows, width = partner_half.shape
    return pl.pallas_call(
        turned_kernel,
        out_shape=jax.ShapeDtypeStruct((width, 2 * rows), BF16),
        in_specs=[SMEM] + [VMEM] * 2,
        out_specs=VMEM,
        compiler_params=PARAMS,
        cost_estimate=pl.CostEstimate(
            flops=0, bytes_accessed=8 * rows * width, transcendentals=0
        ),
        name="turned_rows",
    )(which, hidden, partner_half)


def partial_kernel(facts, count, turned_ref, *refs):
    heads, (mine_ref, theirs_ref) = refs[facts : facts + count], refs[facts + count :][:2]
    for held, ref in zip(refs[facts + count + 2 :], heads):
        held[...] = ref[...]
    shard_rows, depth = heads[0].shape
    rows = mine_ref.shape[1]
    for i in range(len(heads) // 2):
        total = jnp.dot(heads[2 * i][...], turned_ref[:depth, :], preferred_element_type=F32)
        total += jnp.dot(heads[2 * i + 1][...], turned_ref[depth:, :], preferred_element_type=F32)
        mine_ref[i * shard_rows : (i + 1) * shard_rows, :] = total[:, :rows]
        theirs_ref[i * shard_rows : (i + 1) * shard_rows, :] = total[:, rows:]
    if facts:
        below = theirs_ref.shape[0] - mine_ref.shape[0]
        theirs_ref[mine_ref.shape[0] :, :] = jnp.zeros((below, rows), F32)
        theirs_ref[pl.ds(mine_ref.shape[0], refs[0].shape[0]), :] = refs[0][...]


def partial_scores(turned_rows, heads, facts=()):
    width, rows = turned_rows.shape
    columns = sum(head.shape[0] for head in heads) // 2
    below = BELOW * len(facts)
    return pl.pallas_call(
        functools.partial(partial_kernel, len(facts), len(heads)),
        out_shape=[
            jax.ShapeDtypeStruct((columns, rows // 2), F32),
            jax.ShapeDtypeStruct((columns + below, rows // 2), F32),
            *[jax.ShapeDtypeStruct(head.shape, head.dtype) for head in heads if not facts],
        ],
        in_specs=[VMEM] * (1 + len(facts) + len(heads)),
        out_specs=[VMEM] * (2 if facts else 2 + len(heads)),
        compiler_params=PARAMS,
        cost_estimate=pl.CostEstimate(
            flops=2 * rows * columns * width,
            bytes_accessed=2 * width * (rows + columns),
            transcendentals=0,
        ),
        name="partial_scores",
    )(turned_rows, *facts, *heads)


def advantage_kernel(partner_ref, own_ref, outer_ref, out_ref):
    rows = own_ref.shape[1]
    partner = partner_ref[partner_ref.shape[0] - BELOW :, :]
    eye = lax.broadcasted_iota(jnp.int32, (rows, rows), 0) == lax.broadcasted_iota(
        jnp.int32, (rows, rows), 1
    )

    def upright(row):
        return jnp.sum(jnp.where(eye, row, 0.0), axis=1, keepdims=True)

    groups = upright(partner[1:2, :])
    sums, counts = jnp.zeros((rows, 1), F32), jnp.zeros((rows, 1), F32)
    for facts in (partner, own_ref[...], outer_ref[...]):
        member = facts[1:2, :] == groups
        sums += jnp.sum(jnp.where(member, facts[0:1, :], 0.0), axis=1, keepdims=True)
        counts += jnp.sum(jnp.where(member, 1.0, 0.0), axis=1, keepdims=True)
    out_ref[...] = jnp.broadcast_to(upright(partner[0:1, :]) - sums / counts, (rows, rows))


def advantages(partner, own, outer):
    rows = own.shape[1]
    return pl.pallas_call(
        advantage_kernel,
        out_shape=jax.ShapeDtypeStruct((rows, rows), F32),
        in_specs=[VMEM] * 3,
        out_specs=VMEM,
        compiler_params=PARAMS,
        cost_estimate=pl.CostEstimate(flops=20 * 10**9, bytes_accessed=0, transcendentals=0),
        name="advantage",
    )(partner, own, outer)


def softmax_of(shard, tokens, mine, theirs, shards):
    scores = jnp.concatenate(
        [a[...] + b[: a.shape[0], :] for a, b in zip(mine, theirs)], axis=0
    )
    columns, rows = scores.shape
    shard_rows = columns // shards
    relative = ((tokens // shard_rows) ^ shard) * shard_rows + tokens % shard_rows
    chosen = lax.broadcasted_iota(jnp.int32, (columns, rows), 0) == relative
    row_max = jnp.max(scores, axis=0, keepdims=True)
    unnormed = jnp.exp(scores - row_max)
    return scores, chosen, row_max, unnormed, jnp.sum(unnormed, axis=0, keepdims=True)


def outputs_kernel(parts, shards, shard_ref, tokens_ref, *refs):
    mine, theirs = refs[:parts], refs[parts : 2 * parts]
    logits_ref, logprob_ref, entropy_ref = refs[2 * parts :]
    scores, chosen, row_max, unnormed, denominator = softmax_of(
        shard_ref[0], tokens_ref[...], mine, theirs, shards
    )
    shard_rows = scores.shape[0] // shards
    for i in range(shards):
        block = slice(i * shard_rows, (i + 1) * shard_rows)
        place = pl.multiple_of((shard_ref[0] ^ i) * shard_rows, 128)
        logits_ref[:, pl.ds(place, shard_rows)] = scores[block, :].T.astype(BF16)
    log_total = row_max + jnp.log(denominator)
    picked = jnp.sum(jnp.where(chosen, scores, 0.0), axis=0, keepdims=True)
    logprob_ref[...] = picked - log_total
    probabilities = unnormed / denominator
    entropy_ref[...] = log_total - jnp.sum(probabilities * scores, axis=0, keepdims=True)


def softmax_params(rows, columns):
    return pltpu.CompilerParams(vmem_limit_bytes=1024**2 + 16 * rows * columns)


def outputs(shard, tokens, mine, theirs, shards):
    rows = tokens.shape[1]
    columns = sum(part.shape[0] for part in mine)
    flat = jax.ShapeDtypeStruct((1, rows), F32)
    return pl.pallas_call(
        functools.partial(outputs_kernel, len(mine), shards),
        out_shape=[jax.ShapeDtypeStruct((rows, columns), BF16), flat, flat],
        in_specs=[SMEM] + [VMEM] * (1 + 2 * len(mine)),
        out_specs=[VMEM] * 3,
        compiler_params=softmax_params(rows, columns),
        cost_estimate=pl.CostEstimate(
            flops=10 * rows * columns,
            bytes_accessed=12 * rows * columns,
            transcendentals=rows * columns,
        ),
        name="outputs",
    )(shard, tokens, *mine, *theirs)


def scaling(advantage, width):
    return jnp.concatenate([advantage] * (width // advantage.shape[1]), axis=1)


def multiplied(dlogits, heads, out_ref, start, scale=None):
    block = 256
    scale = None if scale is None else scaling(scale, block)
    for j in range(heads[0].shape[1] // block):
        part = slice(j * block, (j + 1) * block)
        head = jnp.concatenate([ref[:, part] for ref in heads], axis=0)
        product = jnp.dot(dlogits, head, preferred_element_type=F32)
        product = product if scale is None else product * scale
        out_ref[:, start + j * block : start + (j + 1) * block] = product.astype(BF16)


def gradient_cost(rows, columns, width):
    return pl.CostEstimate(
        flops=2 * rows * columns * width,
        bytes_accessed=2 * width * (rows + columns),
        transcendentals=0,
    )


def first_kernel(parts, shards, shard_ref, tokens_ref, *refs):
    mine, theirs = refs[:parts], refs[parts : 2 * parts]
    heads, out_ref = refs[2 * parts : 2 * parts + shards], refs[-1]
    _, chosen, _, unnormed, denominator = softmax_of(
        shard_ref[0], tokens_ref[...], mine, theirs, shards
    )
    columns = unnormed.shape[0]
    shard_rows = columns // shards
    dlogits = unnormed / denominator - jnp.where(chosen, 1.0, 0.0)
    for i in range(shards):
        block = slice(i * shard_rows, (i + 1) * shard_rows)
        out_ref[:, block] = dlogits[block, :].T.astype(BF16)
    multiplied(out_ref[:, :columns], heads, out_ref, columns)


def first_message(shard, tokens, mine, theirs, heads, shards):
    rows = tokens.shape[1]
    columns = sum(part.shape[0] for part in mine)
    width = heads[0].shape[1]
    return pl.pallas_call(
        functools.partial(first_kernel, len(mine), shards),
        out_shape=jax.ShapeDtypeStruct((rows, columns + width), BF16),
        in_specs=[SMEM] + [VMEM] * (1 + 2 * len(mine) + len(heads)),
        out_specs=VMEM,
        compiler_params=softmax_params(rows, columns),
        cost_estimate=gradient_cost(rows, columns, width),
        name="first_message",
    )(shard, tokens, *mine, *theirs, *heads)


def second_kernel(first_ref, *refs):
    heads, out_ref = refs[:-1], refs[-1]
    columns = first_ref.shape[1] - heads[0].shape[1]
    multiplied(first_ref[:, :columns], heads, out_ref, 0)


def second_message(first, heads):
    rows, width = first.shape[0], heads[0].shape[1]
    columns = first.shape[1] - width
    return pl.pallas_call(
        second_kernel,
        out_shape=jax.ShapeDtypeStruct((rows, width), BF16),
        in_specs=[VMEM] * (1 + len(heads)),
        out_specs=VMEM,
        compiler_params=PARAMS,
        cost_estimate=gradient_cost(32 * rows, columns, width),
        name="second_message",
    )(first, *heads)


def scaled(message_ref, advantage, columns, out_ref, start):
    block = 256
    scale = scaling(advantage, block)
    for j in range(0, columns.stop - columns.start, block):
        value = message_ref[:, columns.start + j : columns.start + j + block].astype(F32)
        out_ref[:, start + j : start + j + block] = (value * scale).astype(BF16)


def staying_kernel(which_ref, first_ref, advantage_ref, *refs):
    heads, (out_ref, held_ref, sem) = refs[:-3], refs[-3:]
    depth = held_ref.shape[1] // 3
    width = 2 * depth
    columns = first_ref.shape[1] - depth
    mine = pl.multiple_of(which_ref[0] * width, 128)
    other = pl.multiple_of((1 - which_ref[0]) * width, 128)
    advantage = advantage_ref[...]
    copies = []

    def put(i, place):
        source = held_ref.at[:, pl.ds(i * depth, depth)]
        target = out_ref.at[:, pl.ds(pl.multiple_of(place, 128), depth)]
        copies.append(pltpu.make_async_copy(source, target, sem.at[i]))
        copies[-1].start()

    scaled(first_ref, advantage, slice(columns, columns + depth), held_ref, 0)
    put(0, other)
    dlogits = first_ref[:, :columns]
    for i in range(2):
        multiplied(dlogits, heads[i::2], held_ref, (i + 1) * depth, advantage)
        put(i + 1, mine + i * depth)
    for copy in copies:
        copy.wait()


def staying_gradient(which, first, advantage, heads):
    rows = first.shape[0]
    depth = heads[0].shape[1]
    columns = first.shape[1] - depth
    return pl.pallas_call(
        staying_kernel,
        out_shape=jax.ShapeDtypeStruct((rows, 4 * depth), BF16),
        in_specs=[SMEM] + [VMEM] * (2 + len(heads)),
        out_specs=HBM,
        scratch_shapes=[pltpu.VMEM((rows, 3 * depth), BF16), pltpu.SemaphoreType.DMA((3,))],
        compiler_params=PARAMS,
        cost_estimate=gradient_cost(rows, columns, 2 * depth),
        name="staying_gradient",
    )(which, first, advantage, *heads)


def placed_kernel(which_ref, second_ref, advantage_ref, _, out_ref, held_ref, sem):
    depth = second_ref.shape[1]
    parts = 5 if depth % 1280 == 0 else 1
    width = depth // parts
    start = (1 - which_ref[0]) * (2 * depth) + depth
    copies = []
    for i in range(parts):
        part = slice(i * width, (i + 1) * width)
        scaled(second_ref, advantage_ref[...], part, held_ref, i * width)
        target = out_ref.at[:, pl.ds(pl.multiple_of(start + i * width, 128), width)]
        copies.append(
            pltpu.make_async_copy(held_ref.at[:, pl.ds(i * width, width)], target, sem.at[i])
        )
        copies[-1].start()
    for copy in copies:
        copy.wait()


def placed_beside(which, second, advantage, gradient):
    return pl.pallas_call(
        placed_kernel,
        out_shape=jax.ShapeDtypeStruct(gradient.shape, gradient.dtype),
        in_specs=[SMEM, VMEM, VMEM, HBM],
        out_specs=HBM,
        scratch_shapes=[pltpu.VMEM(second.shape, BF16), pltpu.SemaphoreType.DMA((5,))],
        input_output_aliases={3: 0},
        compiler_params=PARAMS,
        name="place_second",
    )(which, second, advantage, gradient)


def body(hidden, head_weight, tokens, rewards, group_ids):
    shards = lax.axis_size("vocab")
    which = (lax.axis_index("section") % 2).reshape(1)
    shard = lax.axis_index("vocab").reshape(1)
    near = [o for o in range(shards) if bin(o).count("1") <= 1]
    far = [o for o in range(shards) if bin(o).count("1") > 1]

    own = jnp.stack([rewards, (group_ids + 1).astype(F32)])
    pieces = tuple(take(which, head_weight, 2))
    late_hidden, _ = lax.optimization_barrier((hidden, pieces))
    (other_half,) = take(1 - which, late_hidden, 1)
    other_half, late_pieces = lax.optimization_barrier((other_half, pieces))
    heads = gathered(pieces, late_pieces, "vocab")
    partner_half = swapped(other_half, "section", 1)

    rows = turned(which, hidden, partner_half)
    mine, theirs = [], []
    for offsets, facts in ((near, (own,)), (far, ())):
        pieces = [piece for o in offsets for piece in heads[o]]
        kept, sent, *again = partial_scores(rows, pieces, facts)
        mine.append(kept)
        theirs.append(swapped(sent, "section", 1))
    partner_facts = theirs[0]
    mine, theirs = in_order(mine, near + far, 0), in_order(theirs, near + far, BELOW)
    for i, offset in enumerate(far):
        heads[offset] = again[2 * i : 2 * i + 2]
    pieces = [piece for pair in heads for piece in pair]
    flat_tokens = tokens[None, :]
    first = first_message(shard, flat_tokens, mine, theirs, pieces[0::2] + pieces[1::2], shards)
    first_in = swapped(first, "section", 1)
    second = second_message(first, pieces[1::2])
    second_in = swapped(second, "section", 1)

    late_own, _ = lax.optimization_barrier((own, first))
    late_tokens, _ = lax.optimization_barrier((flat_tokens, second))
    logits, logprob, entropy = outputs(shard, late_tokens, mine, theirs, shards)
    partner_facts, logits, logprob, entropy = lax.optimization_barrier(
        (partner_facts, logits, logprob, entropy)
    )
    axes = ("vocab", "section")
    count = lax.axis_size(axes)
    beyond = [(i + 2, i) for i in range(0, count - 2, 2)] + [(i, i + 2) for i in range(1, count - 2, 2)]
    outer = lax.ppermute(late_own, axes, beyond)
    advantage = advantages(partner_facts, own, outer)
    staying = staying_gradient(which, first_in, advantage, pieces)
    previous_grad = placed_beside(which, second_in, advantage, staying)
    return (logits, logprob[0], entropy[0], previous_grad)


def in_order(blocks, order, below):
    if order == sorted(order):
        return blocks
    first = blocks[0]
    kept = first.shape[0] - below
    whole = jnp.concatenate([first[:kept], *blocks[1:]], axis=0)
    width = whole.shape[0] // len(order)
    parts = {offset: whole[i * width : (i + 1) * width] for i, offset in enumerate(order)}
    return [jnp.concatenate([parts[offset] for offset in sorted(order)] + [first[kept:]], axis=0)]


def solution(mesh):
    placed = (
        P(("seq", "vocab", "section"), None),
        P(("seq", "vocab"), None),
        P(("seq", "vocab", "section")),
        P(("seq", "vocab", "section")),
        P(("seq", "vocab", "section")),
    )
    return jax.shard_map(
        body,
        mesh=mesh,
        in_specs=placed,
        out_specs=(
            P(("seq", "vocab", "section"), None),
            P(("seq", "vocab", "section")),
            P(("seq", "vocab", "section")),
            P(("seq", "vocab", "section"), None),
        ),
        check_vma=False,
    )
```

```python
import functools

import jax
import jax.numpy as jnp
from jax import lax
from jax.experimental import pallas as pl
from jax.experimental.pallas import tpu as pltpu
from jax.sharding import PartitionSpec as P

F32, BF16 = jnp.float32, jnp.bfloat16
HBM = pl.BlockSpec(memory_space=pltpu.HBM)
ANY = pl.BlockSpec(memory_space=pl.ANY)
SMEM = pl.BlockSpec(memory_space=pltpu.SMEM)
VMEM = pl.BlockSpec(memory_space=pltpu.VMEM)
PARAMS = pltpu.CompilerParams(vmem_limit_bytes=4 * 1024 * 1024)
BELOW = 8


def swapped(value, axis, mask):
    pairs = [(source, source ^ mask) for source in range(lax.axis_size(axis))]
    return lax.ppermute(value, axis, pairs)


def gathered(first_wave, second_wave, axis):
    count = lax.axis_size(axis)
    masks = [1 << bit for bit in range((count - 1).bit_length())]
    uppers, lowers = {0: first_wave[0]}, {0: first_wave[1]}
    for mask in masks:
        early = mask == masks[0]
        uppers[mask] = swapped((first_wave if early else second_wave)[0], axis, mask)
    for mask in reversed(masks):
        early = mask == masks[-1]
        lowers[mask] = swapped((first_wave if early else second_wave)[1], axis, mask)
    for offset in sorted(range(1, count), key=lambda o: (bin(o).count("1"), o)):
        if offset in uppers:
            continue
        bits = [mask for mask in masks if offset & mask]
        uppers[offset] = swapped(uppers[offset ^ bits[-1]], axis, bits[-1])
        lowers[offset] = swapped(lowers[offset ^ bits[0]], axis, bits[0])
    return [(uppers[offset], lowers[offset]) for offset in range(count)]


def take_kernel(which_ref, value_ref, *refs):
    outs, sem = refs[:-1], refs[-1]
    width = outs[0].shape[1]
    start = which_ref[0] * width * len(outs)
    copies = []
    for i, out in enumerate(outs):
        source = value_ref.at[:, pl.ds(pl.multiple_of(start + i * width, 128), width)]
        copies.append(pltpu.make_async_copy(source, out, sem.at[i]))
    for copy in copies:
        copy.start()
    for copy in copies:
        copy.wait()


def take(which, value, pieces):
    rows, width = value.shape[0], value.shape[1] // 2 // pieces
    return pl.pallas_call(
        take_kernel,
        out_shape=[jax.ShapeDtypeStruct((rows, width), value.dtype)] * pieces,
        in_specs=[SMEM, ANY],
        out_specs=[ANY] * pieces,
        scratch_shapes=[pltpu.SemaphoreType.DMA((pieces,))],
        compiler_params=PARAMS,
        cost_estimate=pl.CostEstimate(
            flops=0, bytes_accessed=value.size * value.dtype.itemsize, transcendentals=0
        ),
        name="take_half",
    )(which, value)


def turned_kernel(which_ref, hidden_ref, partner_ref, out_ref):
    rows, width = partner_ref.shape
    block = 256
    for i in range(width // block):
        start = which_ref[0] * width + i * block
        own = hidden_ref[:, pl.ds(pl.multiple_of(start, 128), block)]
        out_ref[i * block : (i + 1) * block, :rows] = own.T
        part = slice(i * block, (i + 1) * block)
        out_ref[part, rows:] = partner_ref[:, part].T


def turned(which, hidden, partner_half):
    rows, width = partner_half.shape
    return pl.pallas_call(
        turned_kernel,
        out_shape=jax.ShapeDtypeStruct((width, 2 * rows), BF16),
        in_specs=[SMEM] + [VMEM] * 2,
        out_specs=VMEM,
        compiler_params=PARAMS,
        cost_estimate=pl.CostEstimate(
            flops=0, bytes_accessed=8 * rows * width, transcendentals=0
        ),
        name="turned_rows",
    )(which, hidden, partner_half)


def partial_kernel(facts, count, turned_ref, *refs):
    heads, (mine_ref, theirs_ref) = refs[facts : facts + count], refs[facts + count :][:2]
    for held, ref in zip(refs[facts + count + 2 :], heads):
        held[...] = ref[...]
    shard_rows, depth = heads[0].shape
    rows = mine_ref.shape[1]
    for i in range(len(heads) // 2):
        total = jnp.dot(heads[2 * i][...], turned_ref[:depth, :], preferred_element_type=F32)
        total += jnp.dot(heads[2 * i + 1][...], turned_ref[depth:, :], preferred_element_type=F32)
        mine_ref[i * shard_rows : (i + 1) * shard_rows, :] = total[:, :rows]
        theirs_ref[i * shard_rows : (i + 1) * shard_rows, :] = total[:, rows:]
    if facts:
        below = theirs_ref.shape[0] - mine_ref.shape[0]
        theirs_ref[mine_ref.shape[0] :, :] = jnp.zeros((below, rows), F32)
        theirs_ref[pl.ds(mine_ref.shape[0], refs[0].shape[0]), :] = refs[0][...]


def partial_scores(turned_rows, heads, facts=()):
    width, rows = turned_rows.shape
    columns = sum(head.shape[0] for head in heads) // 2
    below = BELOW * len(facts)
    return pl.pallas_call(
        functools.partial(partial_kernel, len(facts), len(heads)),
        out_shape=[
            jax.ShapeDtypeStruct((columns, rows // 2), F32),
            jax.ShapeDtypeStruct((columns + below, rows // 2), F32),
            *[jax.ShapeDtypeStruct(head.shape, head.dtype) for head in heads if not facts],
        ],
        in_specs=[VMEM] * (1 + len(facts) + len(heads)),
        out_specs=[VMEM] * (2 if facts else 2 + len(heads)),
        compiler_params=PARAMS,
        cost_estimate=pl.CostEstimate(
            flops=2 * rows * columns * width,
            bytes_accessed=2 * width * (rows + columns),
            transcendentals=0,
        ),
        name="partial_scores",
    )(turned_rows, *facts, *heads)


def advantage_kernel(partner_ref, own_ref, outer_ref, out_ref):
    rows = own_ref.shape[1]
    partner = partner_ref[partner_ref.shape[0] - BELOW :, :]
    eye = lax.broadcasted_iota(jnp.int32, (rows, rows), 0) == lax.broadcasted_iota(
        jnp.int32, (rows, rows), 1
    )

    def upright(row):
        return jnp.sum(jnp.where(eye, row, 0.0), axis=1, keepdims=True)

    groups = upright(partner[1:2, :])
    sums, counts = jnp.zeros((rows, 1), F32), jnp.zeros((rows, 1), F32)
    for facts in (partner, own_ref[...], outer_ref[...]):
        member = facts[1:2, :] == groups
        sums += jnp.sum(jnp.where(member, facts[0:1, :], 0.0), axis=1, keepdims=True)
        counts += jnp.sum(jnp.where(member, 1.0, 0.0), axis=1, keepdims=True)
    out_ref[...] = jnp.broadcast_to(upright(partner[0:1, :]) - sums / counts, (rows, rows))


def advantages(partner, own, outer):
    rows = own.shape[1]
    return pl.pallas_call(
        advantage_kernel,
        out_shape=jax.ShapeDtypeStruct((rows, rows), F32),
        in_specs=[VMEM] * 3,
        out_specs=VMEM,
        compiler_params=PARAMS,
        cost_estimate=pl.CostEstimate(flops=20 * 10**9, bytes_accessed=0, transcendentals=0),
        name="advantage",
    )(partner, own, outer)


def softmax_of(shard, tokens, mine, theirs, shards):
    scores = jnp.concatenate(
        [a[...] + b[: a.shape[0], :] for a, b in zip(mine, theirs)], axis=0
    )
    columns, rows = scores.shape
    shard_rows = columns // shards
    relative = ((tokens // shard_rows) ^ shard) * shard_rows + tokens % shard_rows
    chosen = lax.broadcasted_iota(jnp.int32, (columns, rows), 0) == relative
    row_max = jnp.max(scores, axis=0, keepdims=True)
    unnormed = jnp.exp(scores - row_max)
    return scores, chosen, row_max, unnormed, jnp.sum(unnormed, axis=0, keepdims=True)


def outputs_kernel(parts, shards, shard_ref, tokens_ref, *refs):
    mine, theirs = refs[:parts], refs[parts : 2 * parts]
    logits_ref, logprob_ref, entropy_ref = refs[2 * parts :]
    scores, chosen, row_max, unnormed, denominator = softmax_of(
        shard_ref[0], tokens_ref[...], mine, theirs, shards
    )
    shard_rows = scores.shape[0] // shards
    for i in range(shards):
        block = slice(i * shard_rows, (i + 1) * shard_rows)
        place = pl.multiple_of((shard_ref[0] ^ i) * shard_rows, 128)
        logits_ref[:, pl.ds(place, shard_rows)] = scores[block, :].T.astype(BF16)
    log_total = row_max + jnp.log(denominator)
    picked = jnp.sum(jnp.where(chosen, scores, 0.0), axis=0, keepdims=True)
    logprob_ref[...] = picked - log_total
    probabilities = unnormed / denominator
    entropy_ref[...] = log_total - jnp.sum(probabilities * scores, axis=0, keepdims=True)


def softmax_params(rows, columns):
    return pltpu.CompilerParams(vmem_limit_bytes=1024**2 + 16 * rows * columns)


def outputs(shard, tokens, mine, theirs, shards):
    rows = tokens.shape[1]
    columns = sum(part.shape[0] for part in mine)
    flat = jax.ShapeDtypeStruct((1, rows), F32)
    return pl.pallas_call(
        functools.partial(outputs_kernel, len(mine), shards),
        out_shape=[jax.ShapeDtypeStruct((rows, columns), BF16), flat, flat],
        in_specs=[SMEM] + [VMEM] * (1 + 2 * len(mine)),
        out_specs=[VMEM] * 3,
        compiler_params=softmax_params(rows, columns),
        cost_estimate=pl.CostEstimate(
            flops=10 * rows * columns,
            bytes_accessed=12 * rows * columns,
            transcendentals=rows * columns,
        ),
        name="outputs",
    )(shard, tokens, *mine, *theirs)


def scaling(advantage, width):
    return jnp.concatenate([advantage] * (width // advantage.shape[1]), axis=1)


def multiplied(dlogits, heads, out_ref, start, scale=None):
    block = 256
    scale = None if scale is None else scaling(scale, block)
    for j in range(heads[0].shape[1] // block):
        part = slice(j * block, (j + 1) * block)
        head = jnp.concatenate([ref[:, part] for ref in heads], axis=0)
        product = jnp.dot(dlogits, head, preferred_element_type=F32)
        product = product if scale is None else product * scale
        out_ref[:, start + j * block : start + (j + 1) * block] = product.astype(BF16)


def gradient_cost(rows, columns, width):
    return pl.CostEstimate(
        flops=2 * rows * columns * width,
        bytes_accessed=2 * width * (rows + columns),
        transcendentals=0,
    )


def first_kernel(parts, shards, shard_ref, tokens_ref, *refs):
    mine, theirs = refs[:parts], refs[parts : 2 * parts]
    heads, out_ref = refs[2 * parts : 2 * parts + shards], refs[-1]
    _, chosen, _, unnormed, denominator = softmax_of(
        shard_ref[0], tokens_ref[...], mine, theirs, shards
    )
    columns = unnormed.shape[0]
    shard_rows = columns // shards
    dlogits = unnormed / denominator - jnp.where(chosen, 1.0, 0.0)
    for i in range(shards):
        block = slice(i * shard_rows, (i + 1) * shard_rows)
        out_ref[:, block] = dlogits[block, :].T.astype(BF16)
    multiplied(out_ref[:, :columns], heads, out_ref, columns)


def first_message(shard, tokens, mine, theirs, heads, shards):
    rows = tokens.shape[1]
    columns = sum(part.shape[0] for part in mine)
    width = heads[0].shape[1]
    return pl.pallas_call(
        functools.partial(first_kernel, len(mine), shards),
        out_shape=jax.ShapeDtypeStruct((rows, columns + width), BF16),
        in_specs=[SMEM] + [VMEM] * (1 + 2 * len(mine) + len(heads)),
        out_specs=VMEM,
        compiler_params=softmax_params(rows, columns),
        cost_estimate=gradient_cost(rows, columns, width),
        name="first_message",
    )(shard, tokens, *mine, *theirs, *heads)


def second_kernel(first_ref, *refs):
    heads, out_ref = refs[:-1], refs[-1]
    columns = first_ref.shape[1] - heads[0].shape[1]
    multiplied(first_ref[:, :columns], heads, out_ref, 0)


def second_message(first, heads):
    rows, width = first.shape[0], heads[0].shape[1]
    columns = first.shape[1] - width
    return pl.pallas_call(
        second_kernel,
        out_shape=jax.ShapeDtypeStruct((rows, width), BF16),
        in_specs=[VMEM] * (1 + len(heads)),
        out_specs=VMEM,
        compiler_params=PARAMS,
        cost_estimate=gradient_cost(32 * rows, columns, width),
        name="second_message",
    )(first, *heads)


def scaled(message_ref, advantage, columns, out_ref, start):
    block = 256
    scale = scaling(advantage, block)
    for j in range(0, columns.stop - columns.start, block):
        value = message_ref[:, columns.start + j : columns.start + j + block].astype(F32)
        out_ref[:, start + j : start + j + block] = (value * scale).astype(BF16)


def staying_kernel(which_ref, first_ref, advantage_ref, *refs):
    heads, (out_ref, held_ref, sem) = refs[:-3], refs[-3:]
    depth = held_ref.shape[1] // 3
    width = 2 * depth
    columns = first_ref.shape[1] - depth
    mine = pl.multiple_of(which_ref[0] * width, 128)
    other = pl.multiple_of((1 - which_ref[0]) * width, 128)
    advantage = advantage_ref[...]
    copies = []

    def put(i, place):
        source = held_ref.at[:, pl.ds(i * depth, depth)]
        target = out_ref.at[:, pl.ds(pl.multiple_of(place, 128), depth)]
        copies.append(pltpu.make_async_copy(source, target, sem.at[i]))
        copies[-1].start()

    scaled(first_ref, advantage, slice(columns, columns + depth), held_ref, 0)
    put(0, other)
    dlogits = first_ref[:, :columns]
    for i in range(2):
        multiplied(dlogits, heads[i::2], held_ref, (i + 1) * depth, advantage)
        put(i + 1, mine + i * depth)
    for copy in copies:
        copy.wait()


def staying_gradient(which, first, advantage, heads):
    rows = first.shape[0]
    depth = heads[0].shape[1]
    columns = first.shape[1] - depth
    return pl.pallas_call(
        staying_kernel,
        out_shape=jax.ShapeDtypeStruct((rows, 4 * depth), BF16),
        in_specs=[SMEM] + [VMEM] * (2 + len(heads)),
        out_specs=HBM,
        scratch_shapes=[pltpu.VMEM((rows, 3 * depth), BF16), pltpu.SemaphoreType.DMA((3,))],
        compiler_params=PARAMS,
        cost_estimate=gradient_cost(rows, columns, 2 * depth),
        name="staying_gradient",
    )(which, first, advantage, *heads)


def placed_kernel(which_ref, second_ref, advantage_ref, _, out_ref, held_ref, sem):
    depth = second_ref.shape[1]
    parts = 1
    width = depth // parts
    start = (1 - which_ref[0]) * (2 * depth) + depth
    copies = []
    for i in range(parts):
        part = slice(i * width, (i + 1) * width)
        scaled(second_ref, advantage_ref[...], part, held_ref, i * width)
        target = out_ref.at[:, pl.ds(pl.multiple_of(start + i * width, 128), width)]
        copies.append(
            pltpu.make_async_copy(held_ref.at[:, pl.ds(i * width, width)], target, sem.at[i])
        )
        copies[-1].start()
    for copy in copies:
        copy.wait()


def placed_beside(which, second, advantage, gradient):
    return pl.pallas_call(
        placed_kernel,
        out_shape=jax.ShapeDtypeStruct(gradient.shape, gradient.dtype),
        in_specs=[SMEM, VMEM, VMEM, HBM],
        out_specs=HBM,
        scratch_shapes=[pltpu.VMEM(second.shape, BF16), pltpu.SemaphoreType.DMA((1,))],
        input_output_aliases={3: 0},
        compiler_params=PARAMS,
        name="place_second",
    )(which, second, advantage, gradient)


def body(hidden, head_weight, tokens, rewards, group_ids):
    shards = lax.axis_size("vocab")
    which = (lax.axis_index("section") % 2).reshape(1)
    shard = lax.axis_index("vocab").reshape(1)
    near = [o for o in range(shards) if bin(o).count("1") <= 1]
    far = [o for o in range(shards) if bin(o).count("1") > 1]

    own = jnp.stack([rewards, (group_ids + 1).astype(F32)])
    pieces = tuple(take(which, head_weight, 2))
    late_hidden, _ = lax.optimization_barrier((hidden, pieces))
    (other_half,) = take(1 - which, late_hidden, 1)
    other_half, late_pieces = lax.optimization_barrier((other_half, pieces))
    heads = gathered(pieces, late_pieces, "vocab")
    partner_half = swapped(other_half, "section", 1)

    rows = turned(which, hidden, partner_half)
    mine, theirs = [], []
    for offsets, facts in ((near, (own,)), (far, ())):
        pieces = [piece for o in offsets for piece in heads[o]]
        kept, sent, *again = partial_scores(rows, pieces, facts)
        mine.append(kept)
        theirs.append(swapped(sent, "section", 1))
    partner_facts = theirs[0]
    mine, theirs = in_order(mine, near + far, 0), in_order(theirs, near + far, BELOW)
    for i, offset in enumerate(far):
        heads[offset] = again[2 * i : 2 * i + 2]
    pieces = [piece for pair in heads for piece in pair]
    flat_tokens = tokens[None, :]
    first = first_message(shard, flat_tokens, mine, theirs, pieces[0::2] + pieces[1::2], shards)
    first_in = swapped(first, "section", 1)
    second = second_message(first, pieces[1::2])
    second_in = swapped(second, "section", 1)

    late_own, late_tokens, _ = lax.optimization_barrier((own, flat_tokens, first))
    logits, logprob, entropy = outputs(shard, late_tokens, mine, theirs, shards)
    partner_facts, logits, logprob, entropy = lax.optimization_barrier(
        (partner_facts, logits, logprob, entropy)
    )
    axes = ("vocab", "section")
    count = lax.axis_size(axes)
    beyond = [(i + 2, i) for i in range(0, count - 2, 2)] + [(i, i + 2) for i in range(1, count - 2, 2)]
    outer = lax.ppermute(late_own, axes, beyond)
    advantage = advantages(partner_facts, own, outer)
    staying = staying_gradient(which, first_in, advantage, pieces)
    previous_grad = placed_beside(which, second_in, advantage, staying)
    return (logits, logprob[0], entropy[0], previous_grad)


def in_order(blocks, order, below):
    if order == sorted(order):
        return blocks
    first = blocks[0]
    kept = first.shape[0] - below
    whole = jnp.concatenate([first[:kept], *blocks[1:]], axis=0)
    width = whole.shape[0] // len(order)
    parts = {offset: whole[i * width : (i + 1) * width] for i, offset in enumerate(order)}
    return [jnp.concatenate([parts[offset] for offset in sorted(order)] + [first[kept:]], axis=0)]


def solution(mesh):
    placed = (
        P(("seq", "vocab", "section"), None),
        P(("seq", "vocab"), None),
        P(("seq", "vocab", "section")),
        P(("seq", "vocab", "section")),
        P(("seq", "vocab", "section")),
    )
    return jax.shard_map(
        body,
        mesh=mesh,
        in_specs=placed,
        out_specs=(
            P(("seq", "vocab", "section"), None),
            P(("seq", "vocab", "section")),
            P(("seq", "vocab", "section")),
            P(("seq", "vocab", "section"), None),
        ),
        check_vma=False,
    )
```
